128 devices in a mesh: order: 32 (over z, y, x_hi), mp: 4 (over x_lo, core).
Axes of the slice: x: 4 (x_hi: 2, x_lo: 2; x = x_hi * 2 + x_lo), y: 4, z: 4, core: 2. Of those that a mesh axis runs over, the one named last changes fastest.
Arguments:
- feats: float32 [256, 131072], P(None, 'order'), may hold values from -60 to 60
- serial_rank: int32 [131072], P('order'), may hold values from 0 to 131071, as said below
- neighbours: int32 [27, 131072], P(None, 'order'), may hold values from -1 to 131071, as said below
- norm_gain: float32 [5, 256], replicated, may hold values from 0.5 to 1.5
- norm_bias: float32 [5, 256], replicated, may hold values from -1.5 to 1.5
- qkv_weight: bfloat16 [2, 3, 256, 256], P(None, None, None, 'mp'), may hold values from -25 to 25
- qkv_bias: bfloat16 [2, 3, 256], P(None, None, 'mp'), may hold values from -1.5 to 1.5
- proj_weight: bfloat16 [2, 256, 256], P(None, 'mp'), may hold values from -0.375 to 0.375
- proj_bias: bfloat16 [2, 256], replicated, may hold values from -1.5 to 1.5
- fc1_weight: bfloat16 [2, 256, 1024], P(None, None, 'mp'), may hold values from -0.375 to 0.375
- fc1_bias: bfloat16 [2, 1024], P(None, 'mp'), may hold values from -2.5 to 2.5
- fc2_weight: bfloat16 [2, 1024, 256], P(None, 'mp'), may hold values from -0.1875 to 0.1875
- fc2_bias: bfloat16 [2, 256], replicated, may hold values from -1.5 to 1.5
- conv_weight: bfloat16 [27, 256, 256], P(None, None, 'mp'), may hold values from -0.109375 to 0.109375
- conv_bias: bfloat16 [256], P('mp'), may hold values from -2.5 to 2.5
- cpe_weight: bfloat16 [256, 256], replicated, may hold values from -0.375 to 0.375
- cpe_bias: bfloat16 [256], replicated, may hold values from -2.5 to 2.5
Outputs:
- result: float32 [256, 131072], P('mp', 'order')
The draws below stay inside these ranges and needn't reach their ends.
Inputs may be any that keep to these rules, and one draw needn't show every extreme that they name: A permutation: the token at position t of the first order takes position serial_rank[t] of the second; order index j holds second-order positions j * 4096 to (j + 1) * 4096 - 1; of the 4096 tokens of one order index at most 256 take positions of any one order index, and exactly 256 do for some pairs. `neighbours`: each entry is -1 or a position within 128 of the column's own; row 13 is the column's own position; rows 0 and 26 are the own position minus and plus 128 wherever that lies inside the sequence.
All inputs are finite; a program needn't handle non-finite values.
Results may differ from the reference program's by a relative error of at most 0.018.
The reference program's roundings to bfloat16 on the way count: a program that leaves them out, or rounds other values in their place, can miss the bound.
Values may be sent and summed in bfloat16 or wider, within the bound.
A program may use at most 128 MiB of HBM per device.

```python
import functools
import math
import jax
import jax.numpy as jnp
from jax import lax

C = 256
HEADS = 16
PATCH = 1024
FFN = 1024
OFFS = 27
HALO = 128
TOK_DEV = 4096
HDIM = 16
TOKENS = 131072


def shuffle_one(subkey):
    return jax.random.permutation(subkey, TOK_DEV)


def draw_feats(key, part):
    key = jax.random.fold_in(key, 11)
    first_key, feature_key, token_key = jax.random.split(key, 3)
    values = jnp.clip(jax.random.normal(first_key, (C, TOKENS), jnp.float32), -4.0, 4.0)
    lowest, highest = (0.5, 5.0)
    feature_scale = jnp.exp(jax.random.uniform(feature_key, (C, 1), jnp.float32, math.log(0.3), math.log(3.0)))
    token_scale = jnp.exp(jax.random.uniform(token_key, (1, TOKENS), jnp.float32, math.log(lowest), math.log(highest)))
    return values * feature_scale * token_scale


def draw_serial_rank(key, part):
    key = jax.random.fold_in(key, 22)
    shift_key, order_key, place_key = jax.random.split(key, 3)
    groups = TOKENS // TOK_DEV
    even_count = TOK_DEV // groups
    quarter = groups // 4
    pattern = jnp.concatenate([jnp.ones((quarter,), jnp.int32), -jnp.ones((quarter,), jnp.int32), jnp.zeros((groups - 2 * quarter,), jnp.int32)])
    pattern = jax.random.permutation(shift_key, pattern)
    repeats = even_count * (1 + pattern)
    template = jnp.repeat(jnp.arange(groups, dtype=jnp.int32), repeats, total_repeat_length=TOK_DEV)
    sources = jnp.arange(groups, dtype=jnp.int32)
    shuffles = jax.vmap(shuffle_one)(jax.random.split(order_key, groups))
    owners = (sources[:, None] + template[shuffles]) % groups
    counts = even_count * (1 + pattern[(sources[None, :] - sources[:, None]) % groups])
    offsets = jnp.cumsum(counts, axis=0) - counts
    starts = jnp.cumsum(counts, axis=1) - counts

    def ranks_of(row_owners, row_starts):
        sorting = jnp.argsort(row_owners, stable=True)
        sorted_owners = row_owners[sorting]
        inside = jnp.arange(TOK_DEV, dtype=jnp.int32) - row_starts[sorted_owners]
        return jnp.zeros((TOK_DEV,), jnp.int32).at[sorting].set(inside)
    inside_ranks = jax.vmap(ranks_of)(owners, starts)
    arrival = offsets[sources[:, None], owners] + inside_ranks
    placements = jax.vmap(shuffle_one)(jax.random.split(place_key, groups))
    positions = placements[owners, arrival]
    return (owners * TOK_DEV + positions).reshape(TOKENS).astype(jnp.int32)


def draw_neighbours(key, part):
    key = jax.random.fold_in(key, 33)
    offset_key, keep_key, level_key = jax.random.split(key, 3)
    positions = jnp.arange(TOKENS, dtype=jnp.int32)[None, :]
    offsets = jax.random.randint(offset_key, (OFFS, TOKENS), -HALO, HALO + 1)
    kernel_row = jnp.arange(OFFS, dtype=jnp.int32)[:, None]
    centre = OFFS // 2
    offsets = jnp.where(kernel_row == centre, 0, offsets)
    offsets = jnp.where(kernel_row == 0, -HALO, offsets)
    offsets = jnp.where(kernel_row == OFFS - 1, HALO, offsets)
    levels = jnp.repeat(jax.random.randint(level_key, (TOKENS // TOK_DEV,), 1, 5), TOK_DEV)[None, :]
    present = jax.random.randint(keep_key, (OFFS, TOKENS), 0, 5) < levels
    present = present | (kernel_row == centre) | (kernel_row == 0) | (kernel_row == OFFS - 1)
    neighbour_pos = positions + offsets
    usable = present & (neighbour_pos >= 0) & (neighbour_pos < TOKENS)
    return jnp.where(usable, neighbour_pos, -1).astype(jnp.int32)


def draw_qkv_weight(key, part):
    key = jax.random.fold_in(key, 44)
    value_key = jax.random.fold_in(key, 0)
    values = jnp.clip(jax.random.normal(value_key, (2, 3, C, C), jnp.float32), -4.0, 4.0) / math.sqrt(C)
    return values.astype(jnp.bfloat16)


def steps_of(key, dims, cuts, least, largest):
    level = 1.0
    for dim, blocks in cuts:
        heights = jax.random.uniform(jax.random.fold_in(jax.random.fold_in(key, 6), dim), (blocks,), jnp.float32, least / len(cuts), largest / len(cuts))
        level = level * jnp.repeat(jnp.exp(heights), dims[dim] // blocks).reshape((-1,) + (1,) * (len(dims) - 1 - dim))
    return level


def noise(rng, dims, scale, limit, cuts=(), held_as=jnp.bfloat16):
    entries = jax.random.normal(rng, dims, jnp.float32) * scale
    if len(cuts) > 0:
        entries = steps_of(rng, dims, cuts, -0.22, 0.18) * entries
    return jnp.clip(entries, min=-limit, max=limit).astype(held_as)


def setup_inputs(seed: int = 0) -> dict:
    streams_of = jax.random.split(jax.random.key(seed), 18)
    feats = draw_feats(jax.random.fold_in(streams_of[17], 71), 0)
    serial_rank = draw_serial_rank(jax.random.fold_in(streams_of[17], 71), 0)
    neighbours = draw_neighbours(jax.random.fold_in(streams_of[17], 71), 0)
    norm_gain = jnp.clip(jax.random.uniform(streams_of[3], (5, C), jnp.float32, 0.5, 1.5), 0.5, 1.5)
    norm_bias = noise(streams_of[4], (5, C), 0.3, 1.5, (), jnp.float32)
    qkv_weight = draw_qkv_weight(jax.random.fold_in(streams_of[17], 71), 0)
    qkv_bias = noise(streams_of[6], (2, 3, C), 0.3, 1.5, ((2, 4),))
    proj_weight = noise(streams_of[7], (2, C, C), C ** -0.5, 0.375, ((1, 4),))
    proj_bias = noise(streams_of[8], (2, C), 0.3, 1.5)
    fc1_weight = noise(streams_of[9], (2, C, FFN), C ** -0.5, 0.375, ((2, 4),))
    fc1_bias = noise(streams_of[10], (2, FFN), 0.5, 2.5, ((1, 4),))
    fc2_weight = noise(streams_of[11], (2, FFN, C), FFN ** -0.5, 0.1875, ((1, 4),))
    fc2_bias = noise(streams_of[12], (2, C), 0.3, 1.5)
    conv_weight = noise(streams_of[13], (OFFS, C, C), (OFFS * C // 2) ** -0.5, 0.109375, ((2, 4),))
    conv_bias = noise(streams_of[14], (C,), 0.5, 2.5, ((0, 4),))
    cpe_weight = noise(streams_of[15], (C, C), C ** -0.5, 0.375)
    cpe_bias = noise(streams_of[16], (C,), 0.5, 2.5)
    return dict(feats=feats, serial_rank=serial_rank, neighbours=neighbours, norm_gain=norm_gain, norm_bias=norm_bias, qkv_weight=qkv_weight, qkv_bias=qkv_bias, proj_weight=proj_weight, proj_bias=proj_bias, fc1_weight=fc1_weight, fc1_bias=fc1_bias, fc2_weight=fc2_weight, fc2_bias=fc2_bias, conv_weight=conv_weight, conv_bias=conv_bias, cpe_weight=cpe_weight, cpe_bias=cpe_bias)


epsilon = 1e-05

def layer_norm(values, scale_row, shift_row):
    average = lax.optimization_barrier(jnp.mean(values, axis=0, keepdims=True))
    centred = values - average
    variance = lax.optimization_barrier(jnp.mean(centred * centred, axis=0, keepdims=True))
    return centred * lax.rsqrt(variance + epsilon) * scale_row[:, None] + shift_row[:, None]

def mixing_block(columns, block_id, norm_id, params):
    norm_gain, norm_bias, qkv_weight, qkv_bias, proj_weight, proj_bias, fc1_weight, fc1_bias, fc2_weight, fc2_bias = params
    normed = layer_norm(columns, norm_gain[norm_id], norm_bias[norm_id]).astype(jnp.bfloat16)
    projected = jnp.einsum('jcl,cp->jlp', qkv_weight[block_id].astype(jnp.float32), normed.astype(jnp.float32))
    triples = (projected + qkv_bias[block_id].astype(jnp.float32)[:, :, None]).astype(jnp.bfloat16)
    triples = lax.optimization_barrier(triples).astype(jnp.float32).reshape(3, HEADS, HDIM, PATCH)
    scores = jnp.einsum('hdq,hdk->hqk', triples[0], triples[1]) * (1.0 / math.sqrt(HDIM))
    chances = jax.nn.softmax(scores, axis=-1).astype(jnp.bfloat16)
    chances = lax.optimization_barrier(chances).astype(jnp.float32)
    head_out = jnp.einsum('hqk,hdk->hdq', chances, triples[2]).astype(jnp.bfloat16).reshape(C, PATCH)
    attended = columns + (jnp.dot(proj_weight[block_id].T, head_out, preferred_element_type=jnp.float32) + proj_bias[block_id].astype(jnp.float32)[:, None])
    normed_two = layer_norm(attended, norm_gain[norm_id + 1], norm_bias[norm_id + 1]).astype(jnp.bfloat16)
    hidden = jnp.dot(fc1_weight[block_id].T, normed_two, preferred_element_type=jnp.float32) + fc1_bias[block_id].astype(jnp.float32)[:, None]
    hidden = jax.nn.gelu(hidden, approximate=False).astype(jnp.bfloat16)
    return attended + (jnp.dot(fc2_weight[block_id].T, hidden, preferred_element_type=jnp.float32) + fc2_bias[block_id].astype(jnp.float32)[:, None])

def run_block(stream, block_id, norm_id, params):
    patch_count = stream.shape[1] // PATCH
    pieces = stream.reshape(C, patch_count, PATCH).transpose(1, 0, 2)
    stepper = functools.partial(mixing_block, block_id=block_id, norm_id=norm_id, params=params)
    finished = lax.map(stepper, pieces)
    return finished.transpose(1, 0, 2).reshape(C, patch_count * PATCH)

def reference(feats, serial_rank, neighbours, norm_gain, norm_bias, qkv_weight, qkv_bias, proj_weight, proj_bias, fc1_weight, fc1_bias, fc2_weight, fc2_bias, conv_weight, conv_bias, cpe_weight, cpe_bias):
    params = (norm_gain, norm_bias, qkv_weight, qkv_bias, proj_weight, proj_bias, fc1_weight, fc1_bias, fc2_weight, fc2_bias)
    first_out = run_block(feats, 0, 0, params)
    moved = jnp.zeros_like(first_out).at[:, serial_rank.astype(jnp.int32)].set(first_out)
    low_values = jnp.concatenate([moved.astype(jnp.bfloat16), jnp.zeros((C, 1), jnp.bfloat16)], axis=1)
    columns = jnp.where(neighbours < 0, TOKENS, neighbours).astype(jnp.int32)

    def offset_step(running, pieces):
        kernel, picked = pieces
        return (running + jnp.dot(kernel.T, low_values[:, picked], preferred_element_type=jnp.float32), None)
    start_value = jnp.zeros((C, TOKENS), jnp.float32) + conv_bias.astype(jnp.float32)[:, None]
    summed, _ = lax.scan(offset_step, start_value, (conv_weight, columns))
    conv_out = summed.astype(jnp.bfloat16)
    mixture = jnp.dot(cpe_weight.T, conv_out, preferred_element_type=jnp.float32) + cpe_bias.astype(jnp.float32)[:, None]
    encoded = moved + layer_norm(mixture, norm_gain[2], norm_bias[2])
    return run_block(encoded, 1, 3, params)
```

```python
import functools
import math

import jax
import jax.numpy as jnp
from jax import lax
from jax.experimental import pallas as pl
from jax.experimental.pallas import tpu as pltpu
from jax.sharding import PartitionSpec as P

C = 256
PATCH = 1024
HALO = 128
HDIM = 16
HEADS = 16
OFFS = 27
TOK = 4096
SLOTS = 64
CAP = 288
EPS = 1e-05
LOG2E = math.log2(math.e)
f32, bf16, i32 = jnp.float32, jnp.bfloat16, jnp.int32
VMEM = pl.BlockSpec(memory_space=pltpu.VMEM)
SMEM = pl.BlockSpec(memory_space=pltpu.SMEM)
ANY = pl.BlockSpec(memory_space=pl.ANY)
S = jax.ShapeDtypeStruct
COL_GAIN, COL_SHIFT, COL_PROJ, COL_FC2, COL_QKV, COL_FC1, COL_CONV, COL_CPE = 0, 5, 10, 12, 14, 20, 28, 29


def kernel_params(**more):
    return pltpu.CompilerParams(vmem_limit_bytes=56 * 2**20, **more)


def iota(shape, dim):
    return lax.broadcasted_iota(i32, shape, dim)


def one_hot(left, right):
    return jnp.where(left == right, 1.0, 0.0).astype(bf16)


def dot(left, right):
    return jnp.dot(left, right, preferred_element_type=f32)


def norm_columns(values, gain, shift):
    average = jnp.mean(values, axis=0, keepdims=True)
    centred = values - average
    variance = jnp.mean(centred * centred, axis=0, keepdims=True)
    return centred * lax.rsqrt(variance + EPS) * gain + shift


def send_map_kernel(rank_ref, src_ref, pos_ref, oh_ref, prefix_ref):
    member = lax.axis_index("mp")
    chunks = TOK // 128
    rank = rank_ref[...]
    by_lane = jnp.concatenate([rank, jnp.zeros((128 - chunks, 128), i32)], axis=0).T
    lower = jnp.where(iota((128, 128), 1) < iota((128, 128), 0), 1.0, 0.0).astype(bf16)
    lanes = iota((128, 128), 1)
    carry = jnp.zeros((1, 128), f32)
    for c in range(chunks):
        hot = jnp.where(by_lane[:, c : c + 1] // PATCH == lanes, 1.0, 0.0)
        oh_ref[c] = hot
        prefix_ref[c] = dot(lower, hot.astype(bf16)) + carry
        carry = carry + jnp.sum(hot, axis=0, keepdims=True)
    row, col = iota((128, 128), 0), iota((128, 128), 1)
    ahead = jnp.where((row // 4 == col // 4) & (row < col), 1.0, 0.0).astype(bf16)
    base = dot(jnp.broadcast_to(carry, (8, 128)).astype(bf16), ahead)[0:1]
    acc = jnp.zeros((160, 128), f32)
    slot_ids = iota((1, 128), 1) * 4 + member
    slot_ids = jnp.where(iota((1, 128), 1) < SLOTS, slot_ids, -1)
    lane_row = iota((1, 128), 1)
    for c in range(chunks):
        slot = jnp.sum(oh_ref[c] * (prefix_ref[c] + base), axis=1, keepdims=True).astype(i32)
        right = one_hot(slot, slot_ids)
        rank_row = rank[c : c + 1, :]
        owner = jnp.where(iota((32, 128), 0) == rank_row // TOK, 1.0, 0.0)
        spot = rank_row % TOK
        token = c * 128 + lane_row
        pieces = [token // 256, token % 256, spot // 256, spot % 256]
        left = jnp.concatenate([owner * piece.astype(f32) for piece in pieces] + [owner], axis=0)
        acc = acc + dot(left.astype(bf16), right)
    acc = acc[:, :SLOTS]
    src_ref[...] = (acc[0:32] * 256.0 + acc[32:64]).astype(i32)
    pos_ref[...] = jnp.where(
        acc[128:160] > 0.5, (acc[64:96] * 256.0 + acc[96:128]).astype(i32), TOK
    )


def send_map(rank):
    return pl.pallas_call(
        send_map_kernel,
        out_shape=[S((32, SLOTS), i32), S((32, SLOTS), i32)],
        in_specs=[VMEM],
        out_specs=[VMEM, VMEM],
        scratch_shapes=[pltpu.VMEM((32, 128, 128), f32), pltpu.VMEM((32, 128, 128), f32)],
        compiler_params=kernel_params(),
        name="send_map",
    )(rank)


def list_map_kernel(pos_ref, src_ref, place_ref):
    pos = pos_ref[...]
    wide = jnp.concatenate([pos, jnp.full((32, 128 - SLOTS), TOK, i32)], axis=1)
    wide = jnp.concatenate([wide, jnp.full((96, 128), TOK, i32)], axis=0)
    by_lane = wide.T[:SLOTS]
    lower = jnp.where(iota((SLOTS, SLOTS), 1) < iota((SLOTS, SLOTS), 0), 1.0, 0.0).astype(bf16)
    lanes = iota((SLOTS, 128), 1)
    carry = jnp.zeros((1, 128), f32)
    acc = jnp.zeros((40, 384), f32)
    unit = iota((1, SLOTS), 1)
    for i in range(32):
        hot = jnp.where(by_lane[:, i : i + 1] // PATCH == lanes, 1.0, 0.0)
        spot = jnp.sum(hot * (dot(lower, hot.astype(bf16)) + carry), axis=1, keepdims=True)
        carry = carry + jnp.sum(hot, axis=0, keepdims=True)
        right = one_hot(spot.astype(i32), iota((SLOTS, 384), 1))
        row = pos[i : i + 1, :]
        member = jnp.where(iota((8, SLOTS), 0) == row // PATCH, 1.0, 0.0)
        inside = row % PATCH
        pieces = [jnp.full((1, SLOTS), i, i32), unit, inside // 32, inside % 32]
        left = jnp.concatenate([member * p.astype(f32) for p in pieces] + [member], axis=0)
        acc = acc + dot(left.astype(bf16), right)
    acc = acc[:, :CAP]
    src_ref[...] = (acc[0:4] * float(SLOTS) + acc[8:12]).astype(i32)
    place_ref[...] = jnp.where(
        acc[32:36] > 0.5, (acc[16:20] * 32.0 + acc[24:28]).astype(i32), -1
    )


def list_map(pos):
    return pl.pallas_call(
        list_map_kernel,
        out_shape=[S((4, CAP), i32), S((4, CAP), i32)],
        in_specs=[VMEM],
        out_specs=[VMEM, VMEM],
        compiler_params=kernel_params(),
        name="list_map",
    )(pos)


def place_map_kernel(place_ref, src_ref):
    place = jnp.concatenate([place_ref[...], jnp.full((4, CAP), -1, i32)], axis=0)
    place = jnp.concatenate([place, jnp.full((8, 384 - CAP), -1, i32)], axis=1)
    acc = jnp.zeros((8, PATCH), f32)
    lane = iota((1, 384), 1)
    by_lane = place.T
    rows = iota((8, 384), 0)
    for q in range(4):
        right = one_hot(by_lane[:, q : q + 1], iota((384, PATCH), 1))
        entry = q * CAP + lane
        left = jnp.where(rows == 0, entry // 64, jnp.where(rows == 1, entry % 64, 0))
        acc = acc + dot(left.astype(f32).astype(bf16), right)
    src_ref[...] = (acc[0:1] * 64.0 + acc[1:2]).astype(i32)


def place_map(place):
    return pl.pallas_call(
        place_map_kernel,
        out_shape=S((1, PATCH), i32),
        in_specs=[VMEM],
        out_specs=VMEM,
        compiler_params=kernel_params(),
        name="place_map",
    )(place)


def pick_kernel(rows, width, index_ref, src_ref, out_ref):
    def step(i, carry):
        for u in range(16):
            r = i * 16 + u
            out_ref[r] = src_ref[index_ref[r // width, r % width]]
        return carry

    lax.fori_loop(0, rows // 16, step, 0)


def pick_rows(index, source, name):
    rows, width = index.shape[0] * index.shape[1], index.shape[1]
    return pl.pallas_call(
        functools.partial(pick_kernel, rows, width),
        out_shape=S((rows, 2, 128), f32),
        in_specs=[SMEM, VMEM],
        out_specs=VMEM,
        compiler_params=kernel_params(),
        name=name,
    )(index, source)


def land_kernel(index_ref, src_ref, moved_ref, low_ref, rows_ref):
    def step(i, carry):
        for u in range(16):
            r = i * 16 + u
            rows_ref[r] = src_ref[index_ref[0, r]]
        return carry

    lax.fori_loop(0, PATCH // 16, step, 0)
    for half in range(2):
        part = rows_ref[:, half, :].T
        moved_ref[half * 128 : half * 128 + 128, :] = part
        low_ref[half * 128 : half * 128 + 128, :] = part.astype(bf16)


def land_rows(index, source):
    return pl.pallas_call(
        land_kernel,
        out_shape=[S((C, PATCH), f32), S((C, PATCH), bf16)],
        in_specs=[SMEM, VMEM],
        out_specs=[VMEM, VMEM],
        scratch_shapes=[pltpu.VMEM((PATCH, 2, 128), f32)],
        compiler_params=kernel_params(),
        name="land",
    )(index, source)


def block_scratch():
    return [
        pltpu.VMEM((C, PATCH), bf16),
        pltpu.VMEM((3, C, PATCH), bf16),
        pltpu.VMEM((2, PATCH, 128), bf16),
        pltpu.VMEM((PATCH, PATCH), f32),
        pltpu.VMEM((PATCH, PATCH), f32),
        pltpu.VMEM((2, 8, PATCH), f32),
        pltpu.VMEM((C, PATCH), bf16),
    ]


def run_block(block, first_norm, x_ref, w_ref, cols_ref, scratch, emit):
    normed_ref, qkv_ref, keys_ref, s0_ref, s1_ref, top_ref, heads_ref = scratch

    def column(k):
        return cols_ref[:, k : k + 1]

    for c in range(4):
        span = slice(c * 256, c * 256 + 256)
        normed_ref[:, span] = norm_columns(
            x_ref[:, span], column(COL_GAIN + first_norm), column(COL_SHIFT + first_norm)
        ).astype(bf16)
    for r in range(4):
        made = dot(w_ref[r, 0:192, :], normed_ref[...])
        for j in range(3):
            bias = cols_ref[r * 64 : r * 64 + 64, COL_QKV + 3 * block + j : COL_QKV + 3 * block + j + 1]
            qkv_ref[j, r * 64 : r * 64 + 64, :] = (made[j * 64 : j * 64 + 64] + bias).astype(bf16)
    for g in range(2):
        keys_ref[g] = qkv_ref[1, g * 128 : g * 128 + 128, :].T

    head_of_row = iota((128, 1), 0) // HDIM
    buffers = (s0_ref, s1_ref)

    def scores(h, b):
        g = h // 8
        queries = qkv_ref[0, pl.ds(pl.multiple_of(g * 128, 128), 128), :]
        queries = jnp.where(head_of_row == h % 8, queries.astype(f32), 0.0).astype(bf16)
        s = dot(keys_ref[g], queries)
        buffers[b][...] = s
        top_ref[b, 0:1, :] = jnp.max(s, axis=0, keepdims=True)

    def finish(h, b):
        p = jnp.exp2((buffers[b][...] - top_ref[b, 0:1, :]) * (0.25 * LOG2E))
        inverse = 1.0 / jnp.sum(p, axis=0, keepdims=True)
        chances = (p * inverse).astype(bf16)
        rows = pl.ds(pl.multiple_of(h * HDIM, HDIM), HDIM)
        heads_ref[rows, :] = dot(qkv_ref[2, rows, :], chances).astype(bf16)

    scores(0, 0)

    def pair(j, carry):
        h = 2 * j
        scores(h + 1, 1)
        finish(h, 0)
        scores(jnp.minimum(h + 2, HEADS - 1), 0)
        finish(h + 1, 1)
        return carry

    lax.fori_loop(0, HEADS // 2, pair, 0)

    proj = [w_ref[r, 192:256, :].T for r in range(4)]
    for c in range(4):
        span = slice(c * 256, c * 256 + 256)
        mixed = dot(proj[0], heads_ref[0:64, span])
        for r in range(1, 4):
            mixed = mixed + dot(proj[r], heads_ref[r * 64 : r * 64 + 64, span])
        attended = x_ref[:, span] + (mixed + column(COL_PROJ + block))
        normed = norm_columns(
            attended, column(COL_GAIN + first_norm + 1), column(COL_SHIFT + first_norm + 1)
        ).astype(bf16)
        total = None
        for r in range(4):
            hidden = dot(w_ref[r, 256:512, :], normed) + column(COL_FC1 + 4 * block + r)
            hidden = 0.5 * hidden * (1.0 + lax.erf(hidden * math.sqrt(0.5)))
            part = dot(w_ref[r, 512:768, :], hidden.astype(bf16))
            total = part if total is None else total + part
        emit(c, attended + (total + column(COL_FC2 + block)))


def first_kernel(feats_ref, w_ref, cols_ref, out_ref, x_ref, sem, *scratch):
    start = pl.multiple_of(lax.axis_index("mp") * PATCH, PATCH)
    copy = pltpu.make_async_copy(feats_ref.at[:, pl.ds(start, PATCH)], x_ref, sem)
    copy.start()
    copy.wait()

    def emit(c, value):
        rows = value.T
        for half in range(2):
            out_ref[c * 256 : c * 256 + 256, half, :] = rows[:, half * 128 : half * 128 + 128]

    run_block(0, 0, x_ref, w_ref, cols_ref, scratch, emit)


def first_block(feats, weights, cols):
    return pl.pallas_call(
        first_kernel,
        out_shape=S((PATCH, 2, 128), f32),
        in_specs=[ANY, VMEM, VMEM],
        out_specs=VMEM,
        scratch_shapes=[pltpu.VMEM((C, PATCH), f32), pltpu.SemaphoreType.DMA] + block_scratch(),
        compiler_params=kernel_params(),
        name="first_block",
    )(feats, weights, cols)


def second_kernel(
    wide_ref, moved_ref, near_ref, conv_ref, cpe_ref, w_ref, cols_ref, out_ref,
    x_ref, index_ref, picked_ref, sem, *scratch
):
    member, group = lax.axis_index("mp"), lax.axis_index("order")
    start = pl.multiple_of(member * PATCH, PATCH)
    copy = pltpu.make_async_copy(near_ref.at[:, pl.ds(start, PATCH)], index_ref, sem)
    copy.start()
    copy.wait()
    first_token = group * TOK + member * PATCH

    def column(k):
        return cols_ref[:, k : k + 1]

    cpe = cpe_ref[...].T
    places = iota((512, 256), 0)
    for c in range(4):
        span = slice(c * 256, c * 256 + 256)
        window = wide_ref[:, c * 256 : c * 256 + 512]
        origin = first_token + c * 256 - HALO

        def pick(k, carry):
            near = index_ref[pl.ds(k, 1), span]
            near = jnp.where(near < 0, -1, near - origin)
            rows = pl.ds(pl.multiple_of(k * C, C), C)
            picked_ref[rows, :] = dot(window, one_hot(places, near)).astype(bf16)
            return carry

        lax.fori_loop(0, OFFS, pick, 0, unroll=3)
        conv = (dot(conv_ref[...], picked_ref[...]) + column(COL_CONV)).astype(bf16)
        mixture = dot(cpe, conv) + column(COL_CPE)
        x_ref[:, span] = moved_ref[:, span] + norm_columns(
            mixture, column(COL_GAIN + 2), column(COL_SHIFT + 2)
        )

    def emit(c, value):
        out_ref[:, c * 256 : c * 256 + 256] = value

    run_block(1, 3, x_ref, w_ref, cols_ref, scratch, emit)


def second_block(wide, moved, neighbours, conv, cpe, weights, cols):
    return pl.pallas_call(
        second_kernel,
        out_shape=S((C, PATCH), f32),
        in_specs=[VMEM, VMEM, ANY, VMEM, VMEM, VMEM, VMEM],
        out_specs=VMEM,
        scratch_shapes=[
            pltpu.VMEM((C, PATCH), f32),
            pltpu.VMEM((OFFS, PATCH), i32),
            pltpu.VMEM((OFFS * C, 256), bf16),
            pltpu.SemaphoreType.DMA,
        ]
        + block_scratch(),
        compiler_params=kernel_params(),
        name="second_block",
    )(wide, moved, neighbours, conv, cpe, weights, cols)


def shards(
    feats, serial_rank, neighbours, norm_gain, norm_bias, qkv_weight, qkv_bias, proj_weight, proj_bias,
    fc1_weight, fc1_bias, fc2_weight, fc2_bias, conv_weight, conv_bias, cpe_weight, cpe_bias,
):
    weights = []
    for b in range(2):
        own = jnp.concatenate(
            [
                qkv_weight[b].transpose(0, 2, 1).reshape(192, C),
                proj_weight[b],
                fc1_weight[b].T,
                fc2_weight[b].T,
            ],
            axis=0,
        )
        weights.append(lax.all_gather(own, "mp", axis=0, tiled=False))
    conv = conv_weight.transpose(2, 0, 1).reshape(64, OFFS * C)
    conv = lax.all_gather(conv, "mp", axis=0, tiled=True)
    small = jnp.concatenate([qkv_bias.reshape(6, 64), fc1_bias.reshape(8, 64), conv_bias[None]], axis=0)
    small = lax.all_gather(small, "mp", axis=0, tiled=False).astype(f32)
    qkv_rows = small[:, 0:6].transpose(1, 0, 2).reshape(6, C)
    fc1_rows = small[:, 6:14].reshape(4, 2, C).transpose(1, 0, 2).reshape(8, C)
    conv_row = small[:, 14].reshape(1, C)
    cols = jnp.concatenate(
        [
            norm_gain, norm_bias, proj_bias.astype(f32), fc2_bias.astype(f32), qkv_rows, fc1_rows, conv_row,
            cpe_bias.astype(f32)[None],
        ],
        axis=0,
    ).T

    send, spots = send_map(serial_rank.reshape(32, 128))
    spots = lax.all_to_all(spots, "order", split_axis=0, concat_axis=0, tiled=True)
    listed, places = list_map(spots)
    places = lax.all_to_all(places, "mp", split_axis=0, concat_axis=0, tiled=True)
    landing = place_map(places)

    rows = first_block(feats, weights[0], cols)
    rows = lax.all_gather(rows, "mp", axis=0, tiled=True)
    frames = pick_rows(send, rows, "pack")
    frames = lax.all_to_all(frames, "order", split_axis=0, concat_axis=0, tiled=True)
    lists = pick_rows(listed, frames, "repack")
    lists = lax.all_to_all(lists, "mp", split_axis=0, concat_axis=0, tiled=True)
    moved, low = land_rows(landing, lists)

    count = 128
    up = [(i, i + 1) for i in range(count - 1)]
    down = [(i + 1, i) for i in range(count - 1)]
    before = lax.ppermute(low[:, PATCH - HALO :], ("order", "mp"), up)
    after = lax.ppermute(low[:, :HALO], ("order", "mp"), down)
    wide = jnp.concatenate([before, low, after], axis=1)
    result = second_block(wide, moved, neighbours, conv, cpe_weight, weights[1], cols)
    return lax.all_to_all(result, "mp", split_axis=0, concat_axis=1, tiled=True)


def solution(mesh):
    in_specs = (
        P(None, "order"),
        P("order"),
        P(None, "order"),
        P(),
        P(),
        P(None, None, None, "mp"),
        P(None, None, "mp"),
        P(None, "mp", None),
        P(),
        P(None, None, "mp"),
        P(None, "mp"),
        P(None, "mp", None),
        P(),
        P(None, None, "mp"),
        P("mp"),
        P(),
        P(),
    )
    return jax.shard_map(shards, mesh=mesh, in_specs=in_specs, out_specs=P("mp", "order"), check_vma=False)
```

```python
import functools
import math

import jax
import jax.numpy as jnp
from jax import lax
from jax.experimental import pallas as pl
from jax.experimental.pallas import tpu as pltpu
from jax.sharding import PartitionSpec as P

C = 256
PATCH = 1024
HALO = 128
HDIM = 16
HEADS = 16
OFFS = 27
TOK = 4096
SLOTS = 64
CAP = 288
CAP_OUT = 352
ORDERS = 32
MESH = pl.DeviceIdType.MESH
EPS = 1e-05
LOG2E = math.log2(math.e)
f32, bf16, i32 = jnp.float32, jnp.bfloat16, jnp.int32
VMEM = pl.BlockSpec(memory_space=pltpu.VMEM)
SMEM = pl.BlockSpec(memory_space=pltpu.SMEM)
ANY = pl.BlockSpec(memory_space=pl.ANY)
S = jax.ShapeDtypeStruct
COL_GAIN, COL_SHIFT, COL_PROJ, COL_FC2, COL_QKV, COL_FC1, COL_CONV, COL_CPE = 0, 5, 10, 12, 14, 20, 28, 29


def kernel_params(**more):
    return pltpu.CompilerParams(vmem_limit_bytes=56 * 2**20, **more)


def iota(shape, dim):
    return lax.broadcasted_iota(i32, shape, dim)


def one_hot(left, right):
    return jnp.where(left == right, 1.0, 0.0).astype(bf16)


def dot_rows(left, right):
    return lax.dot_general(left, right, (((1,), (1,)), ((), ())), preferred_element_type=f32)


def dot(left, right):
    return jnp.dot(left, right, preferred_element_type=f32)


def norm_columns(values, gain, shift):
    average = jnp.mean(values, axis=0, keepdims=True)
    centred = values - average
    variance = jnp.mean(centred * centred, axis=0, keepdims=True)
    return centred * lax.rsqrt(variance + EPS) * gain + shift


def greet(order_peers, halo):
    barrier = pltpu.get_barrier_semaphore()
    group, member = lax.axis_index("order"), lax.axis_index("mp")
    for d in range(1, 4):
        pl.semaphore_signal(barrier, inc=1, device_id=(group, member ^ d), device_id_type=MESH)
    count = 3
    if order_peers:

        def step(d, carry):
            pl.semaphore_signal(barrier, inc=1, device_id=(group ^ d, member), device_id_type=MESH)
            return carry

        lax.fori_loop(1, ORDERS, step, 0)
        count += ORDERS - 1
    if halo:
        for shift in (1, 127):
            pl.semaphore_signal(barrier, inc=1, device_id=neighbour(shift), device_id_type=MESH)
        count += 2
    return barrier, count


def neighbour(shift):
    place = (lax.axis_index("order") * 4 + lax.axis_index("mp") + shift) % 128
    return (place // 4, place % 4)


def remote(src, dst, send, recv, device):
    return pltpu.make_async_remote_copy(
        src_ref=src, dst_ref=dst, send_sem=send, recv_sem=recv, device_id=device, device_id_type=MESH
    )


def routes_kernel(
    rank_ref, send_ref, listed_ref, landing_ref, leave_ref,
    made_ref, slot_ref, spot_ref, left_ref, right_ref, left2_ref, right2_ref,
    pos_out, pos_in, place_out, place_in, send_sem, recv_sem, send2_sem, recv2_sem,
):
    group, member = lax.axis_index("order"), lax.axis_index("mp")
    barrier, count = greet(True, False)
    rank = rank_ref[...]
    upper = jnp.where(iota((128, 128), 0) < iota((128, 128), 1), 1.0, 0.0).astype(bf16)
    both = jnp.concatenate([upper, jnp.ones((128, 128), bf16)], axis=1)
    lane = iota((1, 128), 1)

    def classes(c):
        return jnp.where(iota((128, 128), 0) == rank_ref[pl.ds(c, 1), :] // PATCH, 1.0, 0.0)

    def count_classes(c, total):
        made = dot(classes(c).astype(bf16), both)
        made_ref[c] = made
        return total + made[:, 128:]

    total = lax.fori_loop(0, 32, count_classes, jnp.zeros((128, 128), f32), unroll=8)
    row, col = iota((128, 128), 0), iota((128, 128), 1)
    ahead = jnp.where((row // 4 == col // 4) & (col < row), 1.0, 0.0).astype(bf16)

    def number(c, carry):
        made = made_ref[c]
        slot = jnp.sum(classes(c) * (made[:, :128] + carry), axis=0, keepdims=True)
        slot_ref[pl.ds(c, 1), :] = slot.astype(i32)
        return carry + made[:, 128:]

    lax.fori_loop(0, 32, number, dot(ahead, total.astype(bf16)), unroll=4)

    slots = slot_ref[...]
    hot = jnp.where(iota((32, 8, 128), 1) == (slots % 4)[:, None, :], 1.0, 0.0).reshape(256, 128)
    made = dot(hot.astype(bf16), both)
    row, col = iota((256, 256), 0), iota((256, 256), 1)
    earlier = (row % 8 == col % 8) & (row // 64 == col // 64) & (col < row)
    carry = dot(jnp.where(earlier, 1.0, 0.0).astype(bf16), made[:, 128:].astype(bf16))
    spot_ref[...] = jnp.sum((hot * (made[:, :128] + carry)).reshape(32, 8, 128), axis=1).astype(i32)

    def frames(c, carry):
        span = pl.ds(pl.multiple_of(c * 128, 128), 128)
        rank_row, spot_row = rank_ref[pl.ds(c, 1), :], spot_ref[pl.ds(c, 1), :]
        owner = jnp.where(iota((32, 128), 0) == rank_row // TOK, 1.0, 0.0)
        entry = (c // 8) * CAP_OUT + spot_row
        inside = rank_row % TOK
        pieces = [entry // 64, entry % 64, inside // 64, inside % 64]
        left = jnp.concatenate([owner * p.astype(f32) for p in pieces] + [owner], axis=0)
        left_ref[:, span] = left.astype(bf16)
        right_ref[:, span] = one_hot(iota((SLOTS, 128), 0) * 4 + member, slot_ref[pl.ds(c, 1), :])
        return carry

    lax.fori_loop(0, 32, frames, 0, unroll=2)
    acc = dot_rows(left_ref[...], right_ref[...])
    send_ref[...] = (acc[0:32] * 64.0 + acc[32:64]).astype(i32)
    inside = jnp.where(acc[128:160] > 0.5, (acc[64:96] * 64.0 + acc[96:128]).astype(i32), TOK)
    inside = jnp.concatenate([inside, jnp.full((32, 128 - SLOTS), TOK, i32)], axis=1)
    pos_out[...] = jnp.broadcast_to(inside[:, None, :], (32, 8, 128))
    pos_in[group] = pos_out[group]

    pl.semaphore_wait(barrier, count)

    def frame_copy(d):
        return remote(
            pos_out.at[group ^ d], pos_in.at[group], send_sem.at[d], recv_sem.at[d], (group ^ d, member)
        )

    def frame_start(d, carry):
        frame_copy(d).start()
        return carry

    def frame_wait(d, carry):
        frame_copy(d).wait()
        return carry

    lax.fori_loop(1, ORDERS, frame_start, 0)

    def leaving(c, carry):
        span = pl.ds(pl.multiple_of(c * 128, 128), 128)
        at = pl.ds(member * 8 + c, 1)
        hot = jnp.where(iota((8, 128), 0) == slot_ref[at, :] % 4, 1.0, 0.0)
        token = c * 128 + lane
        left = jnp.concatenate([hot * (token // 64).astype(f32), hot * (token % 64).astype(f32)], axis=0)
        left2_ref[:, span] = left.astype(bf16)
        right2_ref[:, span] = one_hot(iota((CAP_OUT, 128), 0), spot_ref[at, :])
        return carry

    lax.fori_loop(0, 8, leaving, 0)
    acc = dot_rows(left2_ref[...], right2_ref[...])
    leave_ref[...] = (acc[0:4] * 64.0 + acc[8:12]).astype(i32)

    lax.fori_loop(1, ORDERS, frame_wait, 0)

    pos = pos_in[:, 0, :]
    hot = jnp.where(iota((32, 8, 128), 1) == (pos // PATCH)[:, None, :], 1.0, 0.0).reshape(256, 128)
    made = dot(hot.astype(bf16), both)
    earlier = (row % 8 == col % 8) & (col < row)
    carry = dot(jnp.where(earlier, 1.0, 0.0).astype(bf16), made[:, 128:].astype(bf16))
    spot_ref[...] = jnp.sum((hot * (made[:, :128] + carry)).reshape(32, 8, 128), axis=1).astype(i32)
    slot_ref[...] = pos

    def lists(c, acc):
        inside = slot_ref[pl.ds(c, 1), :]
        hot = jnp.where(iota((8, 128), 0) == inside // PATCH, 1.0, 0.0)
        inside = inside % PATCH
        pieces = [jnp.broadcast_to(c, (1, 128)), lane, inside // 32, inside % 32]
        left = jnp.concatenate([hot * p.astype(f32) for p in pieces] + [hot], axis=0)
        right = one_hot(iota((384, 128), 0), spot_ref[pl.ds(c, 1), :])
        return acc + dot_rows(left.astype(bf16), right)

    acc = lax.fori_loop(0, 32, lists, jnp.zeros((40, 384), f32), unroll=4)
    listed_ref[...] = (acc[0:4] * float(SLOTS) + acc[8:12]).astype(i32)[:, :CAP]
    place = jnp.where(acc[32:36] > 0.5, (acc[16:20] * 32.0 + acc[24:28]).astype(i32), -1)
    place_out[...] = jnp.broadcast_to(place[:, None, :], (4, 8, 384))
    place_in[member] = place_out[member]
    copies = [
        remote(
            place_out.at[member ^ d], place_in.at[member], send2_sem.at[d], recv2_sem.at[d],
            (group, member ^ d),
        )
        for d in range(1, 4)
    ]
    for copy in copies:
        copy.start()
    for copy in copies:
        copy.wait()

    acc = jnp.zeros((8, PATCH), f32)
    entry = iota((1, 384), 1)
    kind = iota((8, 384), 0)
    for q in range(4):
        right = one_hot(iota((PATCH, 384), 0), place_in[q, 0:1, :])
        at = q * CAP + entry
        left = jnp.where(kind == 0, at // 64, jnp.where(kind == 1, at % 64, 0))
        acc = acc + dot_rows(left.astype(f32).astype(bf16), right)
    landing_ref[...] = (acc[0:1] * 64.0 + acc[1:2]).astype(i32)


def routes(rank):
    return pl.pallas_call(
        routes_kernel,
        out_shape=[S((32, SLOTS), i32), S((4, CAP), i32), S((1, PATCH), i32), S((4, CAP_OUT), i32)],
        in_specs=[VMEM],
        out_specs=[VMEM] * 4,
        scratch_shapes=[
            pltpu.VMEM((32, 128, 256), f32),
            pltpu.VMEM((32, 128), i32),
            pltpu.VMEM((32, 128), i32),
            pltpu.VMEM((160, TOK), bf16),
            pltpu.VMEM((SLOTS, TOK), bf16),
            pltpu.VMEM((16, PATCH), bf16),
            pltpu.VMEM((CAP_OUT, PATCH), bf16),
            pltpu.VMEM((32, 8, 128), i32),
            pltpu.VMEM((32, 8, 128), i32),
            pltpu.VMEM((4, 8, 384), i32),
            pltpu.VMEM((4, 8, 384), i32),
            pltpu.SemaphoreType.DMA((ORDERS,)),
            pltpu.SemaphoreType.DMA((ORDERS,)),
            pltpu.SemaphoreType.DMA((4,)),
            pltpu.SemaphoreType.DMA((4,)),
        ],
        compiler_params=kernel_params(collective_id=0, has_side_effects=True),
        name="routes",
    )(rank)


def move_rows(count, index, source, store):
    def step(i, carry):
        records = [source[index(i * 16 + u)] for u in range(16)]
        for u in range(16):
            store(i * 16 + u, records[u])
        return carry

    lax.fori_loop(0, count // 16, step, 0)


def relay_kernel(
    rows_ref, send_ref, listed_ref, landing_ref, moved_ref, wide_ref,
    out_ref, frames_ref, sorted_ref, lists_ref, land_ref,
    send_sem, recv_sem, send2_sem, recv2_sem, send3_sem, recv3_sem,
):
    group, member = lax.axis_index("order"), lax.axis_index("mp")
    barrier, count = greet(True, True)
    pl.semaphore_wait(barrier, count)

    def frame_copy(d):
        return remote(
            out_ref.at[d], frames_ref.at[pl.ds(pl.multiple_of(group * SLOTS, SLOTS), SLOTS)],
            send_sem.at[d], recv_sem.at[d], (group ^ d, member),
        )

    def pack(d, carry):
        target = group ^ d

        def store(r, record):
            out_ref[d, r] = record

        move_rows(SLOTS, lambda r: send_ref[target, r], rows_ref, store)
        frame_copy(d).start()
        return carry

    lax.fori_loop(1, ORDERS, pack, 0)

    def store_own(r, record):
        frames_ref[group * SLOTS + r] = record

    move_rows(SLOTS, lambda r: send_ref[group, r], rows_ref, store_own)

    def frame_wait(d, carry):
        frame_copy(d).wait()
        return carry

    lax.fori_loop(1, ORDERS, frame_wait, 0)

    copies = []
    for d in (2, 3, 1):
        target = member ^ d

        def store(r, record, d=d):
            sorted_ref[d, r] = record

        move_rows(CAP, lambda r: listed_ref[target, r], frames_ref, store)
        copy = remote(
            sorted_ref.at[d], lists_ref.at[pl.ds(member * CAP, CAP)], send2_sem.at[d], recv2_sem.at[d],
            (group, target),
        )
        copy.start()
        copies.append(copy)

    def store_mine(r, record):
        lists_ref[member * CAP + r] = record

    move_rows(CAP, lambda r: listed_ref[member, r], frames_ref, store_mine)
    for copy in copies:
        copy.wait()

    def land(start, rows):
        def store(r, record):
            land_ref[start + r] = record

        move_rows(rows, lambda r: landing_ref[0, start + r], lists_ref, store)
        for half in range(2):
            part = land_ref[start : start + rows, half, :].T
            at = slice(half * 128, half * 128 + 128)
            moved_ref[at, start : start + rows] = part
            wide_ref[at, HALO + start : HALO + start + rows] = part.astype(bf16)

    land(0, HALO)
    land(PATCH - HALO, HALO)
    halos = [
        remote(
            wide_ref.at[:, HALO : 2 * HALO], wide_ref.at[:, HALO + PATCH : 2 * HALO + PATCH],
            send3_sem.at[0], recv3_sem.at[0], neighbour(127),
        ),
        remote(
            wide_ref.at[:, PATCH : PATCH + HALO], wide_ref.at[:, 0:HALO],
            send3_sem.at[1], recv3_sem.at[1], neighbour(1),
        ),
    ]
    for copy in halos:
        copy.start()
    for c in range(3):
        land(HALO + c * 256, 256)
    for copy in halos:
        copy.wait()


def relay(rows, send, listed, landing):
    return pl.pallas_call(
        relay_kernel,
        out_shape=[S((C, PATCH), f32), S((C, PATCH + 2 * HALO), bf16)],
        in_specs=[VMEM, SMEM, SMEM, SMEM],
        out_specs=[VMEM, VMEM],
        scratch_shapes=[
            pltpu.VMEM((ORDERS, SLOTS, 2, 128), f32),
            pltpu.VMEM((ORDERS * SLOTS, 2, 128), f32),
            pltpu.VMEM((4, CAP, 2, 128), f32),
            pltpu.VMEM((4 * CAP, 2, 128), f32),
            pltpu.VMEM((PATCH, 2, 128), f32),
            pltpu.SemaphoreType.DMA((ORDERS,)),
            pltpu.SemaphoreType.DMA((ORDERS,)),
            pltpu.SemaphoreType.DMA((4,)),
            pltpu.SemaphoreType.DMA((4,)),
            pltpu.SemaphoreType.DMA((2,)),
            pltpu.SemaphoreType.DMA((2,)),
        ],
        compiler_params=kernel_params(collective_id=2, has_side_effects=True),
        name="relay",
    )(rows, send, listed, landing)


def block_scratch():
    return [
        pltpu.VMEM((C, PATCH), bf16),
        pltpu.VMEM((3, C, PATCH), bf16),
        pltpu.VMEM((2, PATCH, 128), bf16),
        pltpu.VMEM((PATCH, PATCH), f32),
        pltpu.VMEM((PATCH, PATCH), f32),
        pltpu.VMEM((2, 8, PATCH), f32),
        pltpu.VMEM((C, PATCH), bf16),
    ]


def run_block(block, first_norm, x_ref, w_ref, base, cols_ref, scratch, emit, arrive):
    normed_ref, qkv_ref, keys_ref, s0_ref, s1_ref, top_ref, heads_ref = scratch

    def column(k):
        return cols_ref[:, k : k + 1]

    for c in range(4):
        span = slice(c * 256, c * 256 + 256)
        normed_ref[:, span] = norm_columns(
            x_ref[:, span], column(COL_GAIN + first_norm), column(COL_SHIFT + first_norm)
        ).astype(bf16)
    for r in range(4):
        made = dot(w_ref[r, base : base + 192, :], normed_ref[...])
        for j in range(3):
            bias = cols_ref[r * 64 : r * 64 + 64, COL_QKV + 3 * block + j : COL_QKV + 3 * block + j + 1]
            qkv_ref[j, r * 64 : r * 64 + 64, :] = (made[j * 64 : j * 64 + 64] + bias).astype(bf16)
    for g in range(2):
        keys_ref[g] = qkv_ref[1, g * 128 : g * 128 + 128, :].T

    head_of_row = iota((128, 1), 0) // HDIM
    buffers = (s0_ref, s1_ref)

    def scores(h, b):
        g = h // 8
        queries = qkv_ref[0, pl.ds(pl.multiple_of(g * 128, 128), 128), :]
        queries = jnp.where(head_of_row == h % 8, queries.astype(f32), 0.0).astype(bf16)
        s = dot(keys_ref[g], queries)
        buffers[b][...] = s
        top_ref[b, 0:1, :] = jnp.max(s, axis=0, keepdims=True)

    def finish(h, b):
        p = jnp.exp2((buffers[b][...] - top_ref[b, 0:1, :]) * (0.25 * LOG2E))
        inverse = 1.0 / jnp.sum(p, axis=0, keepdims=True)
        chances = (p * inverse).astype(bf16)
        rows = pl.ds(pl.multiple_of(h * HDIM, HDIM), HDIM)
        heads_ref[rows, :] = dot(qkv_ref[2, rows, :], chances).astype(bf16)

    scores(0, 0)

    def pair(j, carry):
        h = 2 * j
        scores(h + 1, 1)
        finish(h, 0)
        scores(jnp.minimum(h + 2, HEADS - 1), 0)
        finish(h + 1, 1)
        return carry

    lax.fori_loop(0, HEADS // 2, pair, 0)

    arrive()
    proj = [w_ref[r, base + 192 : base + 256, :].T for r in range(4)]
    for c in range(4):
        span = slice(c * 256, c * 256 + 256)
        mixed = dot(proj[0], heads_ref[0:64, span])
        for r in range(1, 4):
            mixed = mixed + dot(proj[r], heads_ref[r * 64 : r * 64 + 64, span])
        attended = x_ref[:, span] + (mixed + column(COL_PROJ + block))
        normed = norm_columns(
            attended, column(COL_GAIN + first_norm + 1), column(COL_SHIFT + first_norm + 1)
        ).astype(bf16)
        total = None
        for r in range(4):
            hidden = dot(w_ref[r, base + 256 : base + 512, :], normed) + column(COL_FC1 + 4 * block + r)
            hidden = 0.5 * hidden * (1.0 + lax.erf(hidden * math.sqrt(0.5)))
            part = dot(w_ref[r, base + 512 : base + 768, :], hidden.astype(bf16))
            total = part if total is None else total + part
        emit(c, attended + (total + column(COL_FC2 + block)))


def first_kernel(
    feats_ref, qkv_w_ref, proj_w_ref, fc1_w_ref, fc2_w_ref, gain_ref, shift_ref, qkv_b_ref, proj_b_ref,
    fc1_b_ref, fc2_b_ref, conv_b_ref, cpe_b_ref, leave_ref, rows_ref, cols_ref,
    x_ref, w_ref, params_ref, records_ref, sorted_ref, sem, send_sem, recv_sem, send2_sem, recv2_sem, *scratch
):
    group, member = lax.axis_index("order"), lax.axis_index("mp")
    barrier, count = greet(False, False)
    start = pl.multiple_of(member * PATCH, PATCH)
    load = pltpu.make_async_copy(feats_ref.at[:, pl.ds(start, PATCH)], x_ref, sem)
    load.start()

    pad = jnp.zeros((16, C - 64), f32)
    narrow = jnp.concatenate(
        [qkv_b_ref[0].astype(f32), qkv_b_ref[1].astype(f32), conv_b_ref[...].astype(f32), jnp.zeros((9, 64), f32)],
        axis=0,
    )
    narrow = jnp.concatenate([narrow, pad], axis=1)
    wide = jnp.concatenate([jnp.zeros((8, C), f32), fc1_b_ref[...].astype(f32), jnp.zeros((6, C), f32)], axis=0)
    w_ref[member, 0:16, :] = (narrow + wide).astype(bf16)
    for j in range(3):
        w_ref[member, 16 + j * 64 : 80 + j * 64, :] = qkv_w_ref[0, j].T

    def weight_copy(part, d):
        rows = (pl.ds(0, 208), pl.ds(208, 576))[part]
        return remote(
            w_ref.at[member, rows], w_ref.at[member, rows], send_sem.at[part, d], recv_sem.at[part, d],
            (group, member ^ d),
        )

    pl.semaphore_wait(barrier, count)
    for d in (2, 3, 1):
        weight_copy(0, d).start()
    w_ref[member, 208:272, :] = proj_w_ref[0]
    w_ref[member, 272:528, :] = fc1_w_ref[0].T
    w_ref[member, 528:784, :] = fc2_w_ref[0].T
    for d in (2, 3, 1):
        weight_copy(1, d).start()
    load.wait()
    for d in (2, 3, 1):
        weight_copy(0, d).wait()

    params_ref[...] = jnp.zeros_like(params_ref)
    params_ref[COL_GAIN : COL_GAIN + 5, :] = gain_ref[...]
    params_ref[COL_SHIFT : COL_SHIFT + 5, :] = shift_ref[...]
    params_ref[COL_PROJ : COL_PROJ + 2, :] = proj_b_ref[...].astype(f32)
    params_ref[COL_FC2 : COL_FC2 + 2, :] = fc2_b_ref[...].astype(f32)
    bias = [w_ref[r, 0:16, :].astype(f32) for r in range(4)]
    narrow = jnp.concatenate([b[0:8, 0:64] for b in bias], axis=1)
    params_ref[COL_QKV : COL_QKV + 6, :] = narrow[0:6]
    params_ref[COL_CONV : COL_CONV + 1, :] = narrow[6:7]
    for r in range(4):
        for b in range(2):
            params_ref[COL_FC1 + 4 * b + r : COL_FC1 + 4 * b + r + 1, :] = bias[r][8 + b : 9 + b]
    params_ref[COL_CPE : COL_CPE + 1, :] = cpe_b_ref[...].astype(f32)
    cols_ref[...] = params_ref[...].T

    def emit(c, value):
        rows = value.T
        for half in range(2):
            records_ref[c * 256 : c * 256 + 256, half, :] = rows[:, half * 128 : half * 128 + 128]

    def arrive():
        for d in (2, 3, 1):
            weight_copy(1, d).wait()

    run_block(0, 0, x_ref, w_ref, 16, cols_ref, scratch, emit, arrive)

    copies = []
    for d in (2, 3, 1):
        target = member ^ d

        def store(r, record, d=d):
            sorted_ref[d, r] = record

        move_rows(CAP_OUT, lambda r: leave_ref[target, r], records_ref, store)
        copy = remote(
            sorted_ref.at[d], rows_ref.at[pl.ds(member * CAP_OUT, CAP_OUT)], send2_sem.at[d], recv2_sem.at[d],
            (group, target),
        )
        copy.start()
        copies.append(copy)

    def store_mine(r, record):
        rows_ref[member * CAP_OUT + r] = record

    move_rows(CAP_OUT, lambda r: leave_ref[member, r], records_ref, store_mine)
    for copy in copies:
        copy.wait()


def first_block(*operands):
    return pl.pallas_call(
        first_kernel,
        out_shape=[S((4 * CAP_OUT, 2, 128), f32), S((C, 128), f32)],
        in_specs=[ANY] + [VMEM] * 12 + [SMEM],
        out_specs=[VMEM, VMEM],
        scratch_shapes=[
            pltpu.VMEM((C, PATCH), f32),
            pltpu.VMEM((4, 784, C), bf16),
            pltpu.VMEM((128, C), f32),
            pltpu.VMEM((PATCH, 2, 128), f32),
            pltpu.VMEM((4, CAP_OUT, 2, 128), f32),
            pltpu.SemaphoreType.DMA,
            pltpu.SemaphoreType.DMA((2, 4)),
            pltpu.SemaphoreType.DMA((2, 4)),
            pltpu.SemaphoreType.DMA((4,)),
            pltpu.SemaphoreType.DMA((4,)),
        ]
        + block_scratch(),
        compiler_params=kernel_params(collective_id=1, has_side_effects=True),
        name="first_block",
    )(*operands)


def second_kernel(
    wide_ref, moved_ref, near_ref, conv_ref, cpe_ref, w_ref, cols_ref, out_ref,
    x_ref, index_ref, picked_ref, leave_ref, sem, send_sem, recv_sem, *scratch
):
    member, group = lax.axis_index("mp"), lax.axis_index("order")
    barrier, count = greet(False, False)
    start = pl.multiple_of(member * PATCH, PATCH)
    copy = pltpu.make_async_copy(near_ref.at[:, pl.ds(start, PATCH)], index_ref, sem)
    copy.start()
    copy.wait()
    first_token = group * TOK + member * PATCH

    def column(k):
        return cols_ref[:, k : k + 1]

    cpe = cpe_ref[...].T
    places = iota((512, 256), 0)
    for c in range(4):
        span = slice(c * 256, c * 256 + 256)
        window = wide_ref[:, c * 256 : c * 256 + 512]
        origin = first_token + c * 256 - HALO

        def pick(k, carry):
            near = index_ref[pl.ds(k, 1), span]
            near = jnp.where(near < 0, -1, near - origin)
            rows = pl.ds(pl.multiple_of(k * C, C), C)
            picked_ref[rows, :] = dot(window, one_hot(places, near)).astype(bf16)
            return carry

        lax.fori_loop(0, OFFS, pick, 0, unroll=3)
        conv = (dot(conv_ref[...], picked_ref[...]) + column(COL_CONV)).astype(bf16)
        mixture = dot(cpe, conv) + column(COL_CPE)
        x_ref[:, span] = moved_ref[:, span] + norm_columns(
            mixture, column(COL_GAIN + 2), column(COL_SHIFT + 2)
        )

    pl.semaphore_wait(barrier, count)
    copies = []

    def emit(c, value):
        span = slice(c * 256, c * 256 + 256)
        place = pl.ds(pl.multiple_of(member * PATCH + c * 256, 256), 256)
        leave_ref[:, span] = value
        for d in (2, 3, 1):
            target = member ^ d
            copy = remote(
                leave_ref.at[pl.ds(pl.multiple_of(target * 64, 64), 64), span], out_ref.at[:, place],
                send_sem.at[c, d], recv_sem.at[c, d], (group, target),
            )
            copy.start()
            copies.append(copy)
        out_ref[:, place] = leave_ref[pl.ds(pl.multiple_of(member * 64, 64), 64), span]

    run_block(1, 3, x_ref, w_ref, 0, cols_ref, scratch, emit, lambda: None)
    for copy in copies:
        copy.wait()


def second_block(wide, moved, neighbours, conv, cpe, weights, cols):
    return pl.pallas_call(
        second_kernel,
        out_shape=S((64, TOK), f32),
        in_specs=[VMEM, VMEM, ANY, VMEM, VMEM, VMEM, VMEM],
        out_specs=VMEM,
        scratch_shapes=[
            pltpu.VMEM((C, PATCH), f32),
            pltpu.VMEM((OFFS, PATCH), i32),
            pltpu.VMEM((OFFS * C, 256), bf16),
            pltpu.VMEM((C, PATCH), f32),
            pltpu.SemaphoreType.DMA,
            pltpu.SemaphoreType.DMA((4, 4)),
            pltpu.SemaphoreType.DMA((4, 4)),
        ]
        + block_scratch(),
        compiler_params=kernel_params(collective_id=3, has_side_effects=True),
        name="second_block",
    )(wide, moved, neighbours, conv, cpe, weights, cols)


def shards(
    feats, serial_rank, neighbours, norm_gain, norm_bias, qkv_weight, qkv_bias, proj_weight, proj_bias,
    fc1_weight, fc1_bias, fc2_weight, fc2_bias, conv_weight, conv_bias, cpe_weight, cpe_bias,
):
    conv = conv_weight.transpose(2, 0, 1).reshape(64, OFFS * C)
    conv = lax.all_gather(conv, "mp", axis=0, tiled=True)
    own = jnp.concatenate(
        [qkv_weight[1].transpose(0, 2, 1).reshape(192, C), proj_weight[1], fc1_weight[1].T, fc2_weight[1].T],
        axis=0,
    )
    weights = lax.all_gather(own, "mp", axis=0, tiled=False)
    send, listed, landing, leave = routes(serial_rank.reshape(32, 128))
    rows, cols = first_block(
        feats, qkv_weight, proj_weight, fc1_weight, fc2_weight, norm_gain, norm_bias, qkv_bias, proj_bias,
        fc1_bias, fc2_bias, conv_bias.reshape(1, 64), cpe_bias.reshape(1, C), leave,
    )
    moved, wide = relay(rows, send, listed, landing)
    return second_block(wide, moved, neighbours, conv, cpe_weight, weights, cols)


def solution(mesh):
    in_specs = (
        P(None, "order"),
        P("order"),
        P(None, "order"),
        P(),
        P(),
        P(None, None, None, "mp"),
        P(None, None, "mp"),
        P(None, "mp", None),
        P(),
        P(None, None, "mp"),
        P(None, "mp"),
        P(None, "mp", None),
        P(),
        P(None, None, "mp"),
        P("mp"),
        P(),
        P(),
    )
    return jax.shard_map(shards, mesh=mesh, in_specs=in_specs, out_specs=P("mp", "order"), check_vma=False)
```

```python
import functools
import math

import jax
import jax.numpy as jnp
from jax import lax
from jax.experimental import pallas as pl
from jax.experimental.pallas import tpu as pltpu
from jax.sharding import PartitionSpec as P

C = 256
PATCH = 1024
HALO = 128
HDIM = 16
HEADS = 16
OFFS = 27
TOK = 4096
SLOTS = 64
CAP = 288
CAP_OUT = 352
ORDERS = 32
MESH = pl.DeviceIdType.MESH
EPS = 1e-05
LOG2E = math.log2(math.e)
f32, bf16, i32 = jnp.float32, jnp.bfloat16, jnp.int32
VMEM = pl.BlockSpec(memory_space=pltpu.VMEM)
SMEM = pl.BlockSpec(memory_space=pltpu.SMEM)
ANY = pl.BlockSpec(memory_space=pl.ANY)
S = jax.ShapeDtypeStruct
COL_GAIN, COL_SHIFT, COL_PROJ, COL_FC2, COL_QKV, COL_FC1, COL_CONV, COL_CPE = 0, 5, 10, 12, 14, 20, 28, 29


def kernel_params(**more):
    return pltpu.CompilerParams(vmem_limit_bytes=56 * 2**20, **more)


def iota(shape, dim):
    return lax.broadcasted_iota(i32, shape, dim)


def one_hot(left, right):
    return jnp.where(left == right, 1.0, 0.0).astype(bf16)


def dot_rows(left, right):
    return lax.dot_general(left, right, (((1,), (1,)), ((), ())), preferred_element_type=f32)


def dot(left, right):
    return jnp.dot(left, right, preferred_element_type=f32)


def norm_columns(values, gain, shift):
    average = jnp.mean(values, axis=0, keepdims=True)
    centred = values - average
    variance = jnp.mean(centred * centred, axis=0, keepdims=True)
    return centred * lax.rsqrt(variance + EPS) * gain + shift


def greet(order_peers=False, halo=False, across=False):
    barrier = pltpu.get_barrier_semaphore()
    group, member = lax.axis_index("order"), lax.axis_index("mp")
    for d in range(1, 4):
        pl.semaphore_signal(barrier, inc=1, device_id=(group, member ^ d), device_id_type=MESH)
    count = 3
    if order_peers:

        def step(d, carry):
            pl.semaphore_signal(barrier, inc=1, device_id=(group ^ d, member), device_id_type=MESH)
            return carry

        lax.fori_loop(1, ORDERS, step, 0)
        count += ORDERS - 1
    if across:
        pl.semaphore_signal(barrier, inc=1, device_id=(group ^ 1, member ^ 2), device_id_type=MESH)
        count += 1
    if halo:
        for shift in (1, 127):
            pl.semaphore_signal(barrier, inc=1, device_id=neighbour(shift), device_id_type=MESH)
        count += 2
    return barrier, count


def neighbour(shift):
    place = (lax.axis_index("order") * 4 + lax.axis_index("mp") + shift) % 128
    return (place // 4, place % 4)


def remote(src, dst, send, recv, device):
    return pltpu.make_async_remote_copy(
        src_ref=src, dst_ref=dst, send_sem=send, recv_sem=recv, device_id=device, device_id_type=MESH
    )


def prefix_matrix():
    upper = jnp.where(iota((128, 128), 0) < iota((128, 128), 1), 1.0, 0.0).astype(bf16)
    return jnp.concatenate([upper, jnp.ones((128, 128), bf16)], axis=1)


def route_slots(rank_ref, send_ref, leave_ref, scratch):
    (made_ref, slot_ref, spot_ref, left_ref, right_ref, left2_ref, right2_ref, pos_out, pos_in) = scratch[:9]
    group, member = lax.axis_index("order"), lax.axis_index("mp")
    both = prefix_matrix()
    lane = iota((1, 128), 1)

    def classes(c):
        return jnp.where(iota((128, 128), 0) == rank_ref[pl.ds(c, 1), :] // PATCH, 1.0, 0.0)

    def count_classes(c, total):
        made = dot(classes(c).astype(bf16), both)
        made_ref[c] = made
        return total + made[:, 128:]

    total = lax.fori_loop(0, 32, count_classes, jnp.zeros((128, 128), f32), unroll=8)
    row, col = iota((128, 128), 0), iota((128, 128), 1)
    ahead = jnp.where((row // 4 == col // 4) & (col < row), 1.0, 0.0).astype(bf16)

    def number(c, carry):
        made = made_ref[c]
        slot = jnp.sum(classes(c) * (made[:, :128] + carry), axis=0, keepdims=True)
        slot_ref[pl.ds(c, 1), :] = slot.astype(i32)
        return carry + made[:, 128:]

    lax.fori_loop(0, 32, number, dot(ahead, total.astype(bf16)), unroll=4)

    slots = slot_ref[...]
    hot = jnp.where(iota((32, 8, 128), 1) == (slots % 4)[:, None, :], 1.0, 0.0).reshape(256, 128)
    made = dot(hot.astype(bf16), both)
    row, col = iota((256, 256), 0), iota((256, 256), 1)
    earlier = (row % 8 == col % 8) & (row // 64 == col // 64) & (col < row)
    carry = dot(jnp.where(earlier, 1.0, 0.0).astype(bf16), made[:, 128:].astype(bf16))
    spot_ref[...] = jnp.sum((hot * (made[:, :128] + carry)).reshape(32, 8, 128), axis=1).astype(i32)

    def frames(c, carry):
        span = pl.ds(pl.multiple_of(c * 128, 128), 128)
        rank_row, spot_row = rank_ref[pl.ds(c, 1), :], spot_ref[pl.ds(c, 1), :]
        owner = jnp.where(iota((32, 128), 0) == rank_row // TOK, 1.0, 0.0)
        entry = (c // 8) * CAP_OUT + spot_row
        inside = rank_row % TOK
        pieces = [entry // 64, entry % 64, inside // 64, inside % 64]
        left = jnp.concatenate([owner * p.astype(f32) for p in pieces] + [owner], axis=0)
        left_ref[:, span] = left.astype(bf16)
        right_ref[:, span] = one_hot(iota((SLOTS, 128), 0) * 4 + member, slot_ref[pl.ds(c, 1), :])
        return carry

    lax.fori_loop(0, 32, frames, 0, unroll=2)
    acc = dot_rows(left_ref[...], right_ref[...])
    send_ref[...] = (acc[0:32] * 64.0 + acc[32:64]).astype(i32)
    inside = jnp.where(acc[128:160] > 0.5, (acc[64:96] * 64.0 + acc[96:128]).astype(i32), TOK)
    inside = jnp.concatenate([inside, jnp.full((32, 128 - SLOTS), TOK, i32)], axis=1)
    pos_out[...] = jnp.broadcast_to(inside[:, None, :], (32, 8, 128))
    pos_in[group] = pos_out[group]

    def frame_start(d, carry):
        place_frame_copy(scratch, d).start()
        return carry

    lax.fori_loop(1, ORDERS, frame_start, 0)

    def leaving(c, carry):
        span = pl.ds(pl.multiple_of(c * 128, 128), 128)
        at = pl.ds(member * 8 + c, 1)
        hot = jnp.where(iota((8, 128), 0) == slot_ref[at, :] % 4, 1.0, 0.0)
        token = c * 128 + lane
        left = jnp.concatenate([hot * (token // 64).astype(f32), hot * (token % 64).astype(f32)], axis=0)
        left2_ref[:, span] = left.astype(bf16)
        right2_ref[:, span] = one_hot(iota((CAP_OUT, 128), 0), spot_ref[at, :])
        return carry

    lax.fori_loop(0, 8, leaving, 0)
    acc = dot_rows(left2_ref[...], right2_ref[...])
    leave_ref[...] = (acc[0:4] * 64.0 + acc[8:12]).astype(i32)


def route_lists(listed_ref, scratch):
    _, slot_ref, spot_ref, _, _, _, _, _, pos_in, place_out, place_in = scratch[:11]
    group, member = lax.axis_index("order"), lax.axis_index("mp")
    both = prefix_matrix()
    lane = iota((1, 128), 1)

    def frame_wait(d, carry):
        place_frame_copy(scratch, d).wait()
        return carry

    lax.fori_loop(1, ORDERS, frame_wait, 0)
    row, col = iota((256, 256), 0), iota((256, 256), 1)
    pos = pos_in[:, 0, :]
    hot = jnp.where(iota((32, 8, 128), 1) == (pos // PATCH)[:, None, :], 1.0, 0.0).reshape(256, 128)
    made = dot(hot.astype(bf16), both)
    earlier = (row % 8 == col % 8) & (col < row)
    carry = dot(jnp.where(earlier, 1.0, 0.0).astype(bf16), made[:, 128:].astype(bf16))
    spot_ref[...] = jnp.sum((hot * (made[:, :128] + carry)).reshape(32, 8, 128), axis=1).astype(i32)
    slot_ref[...] = pos

    def lists(c, acc):
        inside = slot_ref[pl.ds(c, 1), :]
        hot = jnp.where(iota((8, 128), 0) == inside // PATCH, 1.0, 0.0)
        inside = inside % PATCH
        pieces = [jnp.broadcast_to(c, (1, 128)), lane, inside // 32, inside % 32]
        left = jnp.concatenate([hot * p.astype(f32) for p in pieces] + [hot], axis=0)
        right = one_hot(iota((384, 128), 0), spot_ref[pl.ds(c, 1), :])
        return acc + dot_rows(left.astype(bf16), right)

    acc = lax.fori_loop(0, 32, lists, jnp.zeros((40, 384), f32), unroll=4)
    listed_ref[...] = (acc[0:4] * float(SLOTS) + acc[8:12]).astype(i32)[:, :CAP]
    place = jnp.where(acc[32:36] > 0.5, (acc[16:20] * 32.0 + acc[24:28]).astype(i32), -1)
    place_out[...] = jnp.broadcast_to(place[:, None, :], (4, 8, 384))
    place_in[member] = place_out[member]
    for d in range(1, 4):
        place_list_copy(scratch, d).start()


def route_landing(landing_ref, scratch):
    place_in = scratch[10]
    for d in range(1, 4):
        place_list_copy(scratch, d).wait()
    acc = jnp.zeros((8, PATCH), f32)
    entry = iota((1, 384), 1)
    kind = iota((8, 384), 0)
    for q in range(4):
        right = one_hot(iota((PATCH, 384), 0), place_in[q, 0:1, :])
        at = q * CAP + entry
        left = jnp.where(kind == 0, at // 64, jnp.where(kind == 1, at % 64, 0))
        acc = acc + dot_rows(left.astype(f32).astype(bf16), right)
    landing_ref[...] = (acc[0:1] * 64.0 + acc[1:2]).astype(i32)


def place_frame_copy(scratch, d):
    group, member = lax.axis_index("order"), lax.axis_index("mp")
    pos_out, pos_in, send_sem, recv_sem = scratch[7], scratch[8], scratch[11], scratch[12]
    return remote(
        pos_out.at[group ^ d], pos_in.at[group], send_sem.at[d], recv_sem.at[d], (group ^ d, member)
    )


def place_list_copy(scratch, d):
    group, member = lax.axis_index("order"), lax.axis_index("mp")
    place_out, place_in, send_sem, recv_sem = scratch[9], scratch[10], scratch[13], scratch[14]
    return remote(
        place_out.at[member ^ d], place_in.at[member], send_sem.at[d], recv_sem.at[d], (group, member ^ d)
    )


def route_scratch():
    return [
        pltpu.VMEM((32, 128, 256), f32),
        pltpu.VMEM((32, 128), i32),
        pltpu.VMEM((32, 128), i32),
        pltpu.VMEM((160, TOK), bf16),
        pltpu.VMEM((SLOTS, TOK), bf16),
        pltpu.VMEM((16, PATCH), bf16),
        pltpu.VMEM((CAP_OUT, PATCH), bf16),
        pltpu.VMEM((32, 8, 128), i32),
        pltpu.VMEM((32, 8, 128), i32),
        pltpu.VMEM((4, 8, 384), i32),
        pltpu.VMEM((4, 8, 384), i32),
        pltpu.SemaphoreType.DMA((ORDERS,)),
        pltpu.SemaphoreType.DMA((ORDERS,)),
        pltpu.SemaphoreType.DMA((4,)),
        pltpu.SemaphoreType.DMA((4,)),
    ]


def move_rows(count, index, source, store):
    def step(i, carry):
        records = [source[index(i * 16 + u)] for u in range(16)]
        for u in range(16):
            store(i * 16 + u, records[u])
        return carry

    lax.fori_loop(0, count // 16, step, 0)


def relay_kernel(
    records_ref, leave_ref, send_ref, listed_ref, landing_ref, moved_ref, wide_ref,
    leaving_ref, rows_ref, out_ref, frames_ref, sorted_ref, lists_ref, land_ref,
    send_sem, recv_sem, send2_sem, recv2_sem, send3_sem, recv3_sem, send4_sem, recv4_sem,
):
    group, member = lax.axis_index("order"), lax.axis_index("mp")
    barrier, count = greet(order_peers=True, halo=True)
    copies = []
    for d in (2, 3, 1):
        target = member ^ d

        def store(r, record, d=d):
            leaving_ref[d, r] = record

        move_rows(CAP_OUT, lambda r: leave_ref[target, r], records_ref, store)
        if d == 2:
            pl.semaphore_wait(barrier, count)
        copy = remote(
            leaving_ref.at[d], rows_ref.at[pl.ds(member * CAP_OUT, CAP_OUT)], send4_sem.at[d], recv4_sem.at[d],
            (group, target),
        )
        copy.start()
        copies.append(copy)

    def store_staying(r, record):
        rows_ref[member * CAP_OUT + r] = record

    move_rows(CAP_OUT, lambda r: leave_ref[member, r], records_ref, store_staying)
    for copy in copies:
        copy.wait()

    def frame_copy(d):
        return remote(
            out_ref.at[d], frames_ref.at[pl.ds(pl.multiple_of(group * SLOTS, SLOTS), SLOTS)],
            send_sem.at[d], recv_sem.at[d], (group ^ d, member),
        )

    def pack(t, carry):
        d = 1 + (t + 8 * member + 7 * group) % (ORDERS - 1)
        target = group ^ d

        def store(r, record):
            out_ref[d, r] = record

        move_rows(SLOTS, lambda r: send_ref[target, r], rows_ref, store)
        frame_copy(d).start()
        return carry

    lax.fori_loop(0, ORDERS - 1, pack, 0)

    def store_own(r, record):
        frames_ref[group * SLOTS + r] = record

    move_rows(SLOTS, lambda r: send_ref[group, r], rows_ref, store_own)

    def frame_wait(d, carry):
        frame_copy(d).wait()
        return carry

    lax.fori_loop(1, ORDERS, frame_wait, 0)

    copies = []
    for d in (2, 3, 1):
        target = member ^ d

        def store(r, record, d=d):
            sorted_ref[d, r] = record

        move_rows(CAP, lambda r: listed_ref[target, r], frames_ref, store)
        copy = remote(
            sorted_ref.at[d], lists_ref.at[pl.ds(member * CAP, CAP)], send2_sem.at[d], recv2_sem.at[d],
            (group, target),
        )
        copy.start()
        copies.append(copy)

    def store_mine(r, record):
        lists_ref[member * CAP + r] = record

    move_rows(CAP, lambda r: listed_ref[member, r], frames_ref, store_mine)
    for copy in copies:
        copy.wait()

    def land(start, rows):
        def store(r, record):
            land_ref[start + r] = record

        move_rows(rows, lambda r: landing_ref[0, start + r], lists_ref, store)
        for half in range(2):
            part = land_ref[start : start + rows, half, :]
            at = slice(half * 128, half * 128 + 128)
            moved_ref[at, start : start + rows] = part.T
            wide_ref[HALO + start : HALO + start + rows, at] = part.astype(bf16)

    land(0, HALO)
    land(PATCH - HALO, HALO)
    halos = [
        remote(
            wide_ref.at[HALO : 2 * HALO], wide_ref.at[HALO + PATCH : 2 * HALO + PATCH],
            send3_sem.at[0], recv3_sem.at[0], neighbour(127),
        ),
        remote(
            wide_ref.at[PATCH : PATCH + HALO], wide_ref.at[0:HALO],
            send3_sem.at[1], recv3_sem.at[1], neighbour(1),
        ),
    ]
    for copy in halos:
        copy.start()
    for c in range(3):
        land(HALO + c * 256, 256)
    for copy in halos:
        copy.wait()


def relay(records, leave, send, listed, landing):
    return pl.pallas_call(
        relay_kernel,
        out_shape=[S((C, PATCH), f32), S((PATCH + 2 * HALO, C), bf16)],
        in_specs=[VMEM, SMEM, SMEM, SMEM, SMEM],
        out_specs=[VMEM, VMEM],
        scratch_shapes=[
            pltpu.VMEM((4, CAP_OUT, 2, 128), f32),
            pltpu.VMEM((4 * CAP_OUT, 2, 128), f32),
            pltpu.VMEM((ORDERS, SLOTS, 2, 128), f32),
            pltpu.VMEM((ORDERS * SLOTS, 2, 128), f32),
            pltpu.VMEM((4, CAP, 2, 128), f32),
            pltpu.VMEM((4 * CAP, 2, 128), f32),
            pltpu.VMEM((PATCH, 2, 128), f32),
            pltpu.SemaphoreType.DMA((ORDERS,)),
            pltpu.SemaphoreType.DMA((ORDERS,)),
            pltpu.SemaphoreType.DMA((4,)),
            pltpu.SemaphoreType.DMA((4,)),
            pltpu.SemaphoreType.DMA((2,)),
            pltpu.SemaphoreType.DMA((2,)),
            pltpu.SemaphoreType.DMA((4,)),
            pltpu.SemaphoreType.DMA((4,)),
        ],
        compiler_params=kernel_params(collective_id=2, has_side_effects=True),
        name="relay",
    )(records, leave, send, listed, landing)


def block_scratch():
    return [
        pltpu.VMEM((C, PATCH), bf16),
        pltpu.VMEM((3, C, PATCH), bf16),
        pltpu.VMEM((2, PATCH, 128), bf16),
        pltpu.VMEM((PATCH, PATCH), f32),
        pltpu.VMEM((PATCH, PATCH), f32),
        pltpu.VMEM((2, 8, PATCH), f32),
        pltpu.VMEM((C, PATCH), bf16),
    ]


def run_block(block, first_norm, x_ref, w_ref, base, cols_ref, scratch, emit, between):
    normed_ref, qkv_ref, keys_ref, s0_ref, s1_ref, top_ref, heads_ref = scratch

    def column(k):
        return cols_ref[:, k : k + 1]

    for c in range(4):
        span = slice(c * 256, c * 256 + 256)
        normed_ref[:, span] = norm_columns(
            x_ref[:, span], column(COL_GAIN + first_norm), column(COL_SHIFT + first_norm)
        ).astype(bf16)
    for r in range(4):
        made = dot(w_ref[r, base : base + 192, :], normed_ref[...])
        for j in range(3):
            bias = cols_ref[r * 64 : r * 64 + 64, COL_QKV + 3 * block + j : COL_QKV + 3 * block + j + 1]
            qkv_ref[j, r * 64 : r * 64 + 64, :] = (made[j * 64 : j * 64 + 64] + bias).astype(bf16)
    for g in range(2):
        keys_ref[g] = qkv_ref[1, g * 128 : g * 128 + 128, :].T

    head_of_row = iota((128, 1), 0) // HDIM
    buffers = (s0_ref, s1_ref)

    def scores(h, b):
        g = h // 8
        queries = qkv_ref[0, pl.ds(pl.multiple_of(g * 128, 128), 128), :]
        queries = jnp.where(head_of_row == h % 8, queries.astype(f32), 0.0).astype(bf16)
        s = dot(keys_ref[g], queries)
        buffers[b][...] = s
        top_ref[b, 0:1, :] = jnp.max(s, axis=0, keepdims=True)

    def finish(h, b):
        p = jnp.exp2((buffers[b][...] - top_ref[b, 0:1, :]) * (0.25 * LOG2E))
        inverse = 1.0 / jnp.sum(p, axis=0, keepdims=True)
        chances = (p * inverse).astype(bf16)
        rows = pl.ds(pl.multiple_of(h * HDIM, HDIM), HDIM)
        heads_ref[rows, :] = dot(qkv_ref[2, rows, :], chances).astype(bf16)

    scores(0, 0)

    def pair(j, carry):
        h = 2 * j
        scores(h + 1, 1)
        finish(h, 0)
        scores(jnp.minimum(h + 2, HEADS - 1), 0)
        finish(h + 1, 1)
        return carry

    lax.fori_loop(0, HEADS // 2, pair, 0)

    between()
    proj = [w_ref[r, base + 192 : base + 256, :].T for r in range(4)]
    for c in range(4):
        span = slice(c * 256, c * 256 + 256)
        mixed = dot(proj[0], heads_ref[0:64, span])
        for r in range(1, 4):
            mixed = mixed + dot(proj[r], heads_ref[r * 64 : r * 64 + 64, span])
        attended = x_ref[:, span] + (mixed + column(COL_PROJ + block))
        normed = norm_columns(
            attended, column(COL_GAIN + first_norm + 1), column(COL_SHIFT + first_norm + 1)
        ).astype(bf16)
        total = None
        for r in range(4):
            hidden = dot(w_ref[r, base + 256 : base + 512, :], normed) + column(COL_FC1 + 4 * block + r)
            hidden = 0.5 * hidden * (1.0 + lax.erf(hidden * math.sqrt(0.5)))
            part = dot(w_ref[r, base + 512 : base + 768, :], hidden.astype(bf16))
            total = part if total is None else total + part
        emit(c, attended + (total + column(COL_FC2 + block)))


def first_kernel(
    feats_ref, qkv_w_ref, proj_w_ref, fc1_w_ref, fc2_w_ref, gain_ref, shift_ref, qkv_b_ref, proj_b_ref,
    fc1_b_ref, fc2_b_ref, conv_b_ref, cpe_b_ref, conv_w_ref, rank_ref,
    records_ref, cols_ref, send_ref, listed_ref, landing_ref, leave_ref, conv_ref, later_ref,
    x_ref, w_ref, params_ref, conv_own_ref, later_own_ref,
    sem, send_sem, recv_sem, local_sem, send3_sem, recv3_sem, *scratch
):
    group, member = lax.axis_index("order"), lax.axis_index("mp")
    routing, scratch = scratch[:15], scratch[15:]
    barrier, count = greet(order_peers=True, across=True)
    start = pl.multiple_of(member * PATCH, PATCH)
    load = pltpu.make_async_copy(feats_ref.at[:, pl.ds(start, PATCH)], x_ref, sem)
    load.start()

    pad = jnp.zeros((16, C - 64), f32)
    narrow = jnp.concatenate(
        [qkv_b_ref[0].astype(f32), qkv_b_ref[1].astype(f32), conv_b_ref[...].astype(f32), jnp.zeros((9, 64), f32)],
        axis=0,
    )
    narrow = jnp.concatenate([narrow, pad], axis=1)
    wide = jnp.concatenate([jnp.zeros((8, C), f32), fc1_b_ref[...].astype(f32), jnp.zeros((6, C), f32)], axis=0)
    w_ref[member, 0:16, :] = (narrow + wide).astype(bf16)
    for j in range(3):
        w_ref[member, 16 + j * 64 : 80 + j * 64, :] = qkv_w_ref[0, j].T

    def weight_copy(part, d):
        rows = (pl.ds(0, 208), pl.ds(208, 576))[part]
        return remote(
            w_ref.at[member, rows], w_ref.at[member, rows], send_sem.at[part, d], recv_sem.at[part, d],
            (group, member ^ d),
        )

    pl.semaphore_wait(barrier, count)
    for d in (2, 3, 1):
        weight_copy(0, d).start()
    w_ref[member, 208:272, :] = proj_w_ref[0]
    w_ref[member, 272:528, :] = fc1_w_ref[0].T
    w_ref[member, 528:784, :] = fc2_w_ref[0].T
    for d in (2, 3, 1):
        weight_copy(1, d).start()

    def turn(k, carry):
        span = pl.ds(pl.multiple_of(k * C, C), C)
        conv_own_ref[:, span] = conv_w_ref[k].T
        return carry

    lax.fori_loop(0, OFFS, turn, 0, unroll=3)
    for j in range(3):
        later_own_ref[j * 64 : j * 64 + 64, :] = qkv_w_ref[1, j].T
    later_own_ref[192:256, :] = proj_w_ref[1]
    later_own_ref[256:512, :] = fc1_w_ref[1].T
    later_own_ref[512:768, :] = fc2_w_ref[1].T
    later = [
        remote(conv_own_ref, conv_ref.at[1], send3_sem.at[0], recv3_sem.at[0], (group ^ 1, member ^ 2)),
        remote(later_own_ref, later_ref.at[1], send3_sem.at[1], recv3_sem.at[1], (group, member ^ 2)),
        pltpu.make_async_copy(conv_own_ref, conv_ref.at[0], local_sem.at[0]),
        pltpu.make_async_copy(later_own_ref, later_ref.at[0], local_sem.at[1]),
    ]
    for copy in later:
        copy.start()
    route_slots(rank_ref, send_ref, leave_ref, routing)
    load.wait()
    for d in (2, 3, 1):
        weight_copy(0, d).wait()

    params_ref[...] = jnp.zeros_like(params_ref)
    params_ref[COL_GAIN : COL_GAIN + 5, :] = gain_ref[...]
    params_ref[COL_SHIFT : COL_SHIFT + 5, :] = shift_ref[...]
    params_ref[COL_PROJ : COL_PROJ + 2, :] = proj_b_ref[...].astype(f32)
    params_ref[COL_FC2 : COL_FC2 + 2, :] = fc2_b_ref[...].astype(f32)
    bias = [w_ref[r, 0:16, :].astype(f32) for r in range(4)]
    narrow = jnp.concatenate([b[0:8, 0:64] for b in bias], axis=1)
    params_ref[COL_QKV : COL_QKV + 6, :] = narrow[0:6]
    params_ref[COL_CONV : COL_CONV + 1, :] = narrow[6:7]
    for r in range(4):
        for b in range(2):
            params_ref[COL_FC1 + 4 * b + r : COL_FC1 + 4 * b + r + 1, :] = bias[r][8 + b : 9 + b]
    params_ref[COL_CPE : COL_CPE + 1, :] = cpe_b_ref[...].astype(f32)
    cols_ref[...] = params_ref[...].T

    def emit(c, value):
        rows = value.T
        for half in range(2):
            records_ref[c * 256 : c * 256 + 256, half, :] = rows[:, half * 128 : half * 128 + 128]

    def between():
        route_lists(listed_ref, routing)
        for d in (2, 3, 1):
            weight_copy(1, d).wait()

    run_block(0, 0, x_ref, w_ref, 16, cols_ref, scratch, emit, between)
    route_landing(landing_ref, routing)
    for copy in later:
        copy.wait()


def first_block(*operands):
    return pl.pallas_call(
        first_kernel,
        out_shape=[
            S((PATCH, 2, 128), f32),
            S((C, 128), f32),
            S((ORDERS, SLOTS), i32),
            S((4, CAP), i32),
            S((1, PATCH), i32),
            S((4, CAP_OUT), i32),
            S((2, 64, OFFS * C), bf16),
            S((2, 768, C), bf16),
        ],
        in_specs=[ANY] + [VMEM] * 14,
        out_specs=[VMEM] * 6 + [ANY] * 2,
        scratch_shapes=[
            pltpu.VMEM((C, PATCH), f32),
            pltpu.VMEM((4, 784, C), bf16),
            pltpu.VMEM((128, C), f32),
            pltpu.VMEM((64, OFFS * C), bf16),
            pltpu.VMEM((768, C), bf16),
            pltpu.SemaphoreType.DMA,
            pltpu.SemaphoreType.DMA((2, 4)),
            pltpu.SemaphoreType.DMA((2, 4)),
            pltpu.SemaphoreType.DMA((2,)),
            pltpu.SemaphoreType.DMA((2,)),
            pltpu.SemaphoreType.DMA((2,)),
        ]
        + route_scratch()
        + block_scratch(),
        compiler_params=kernel_params(collective_id=1, has_side_effects=True),
        name="first_block",
    )(*operands)


def second_kernel(
    wide_ref, moved_ref, near_ref, conv_ref, cpe_ref, later_ref, cols_ref, out_ref,
    x_ref, index_ref, places_ref, hot_ref, picked_ref, conv_w_ref, w_ref, leave_ref,
    sem, local_sem, send2_sem, recv2_sem, send_sem, recv_sem, *scratch
):
    member, group = lax.axis_index("mp"), lax.axis_index("order")
    barrier, count = greet()
    start = pl.multiple_of(member * PATCH, PATCH)
    load = pltpu.make_async_copy(near_ref.at[:, pl.ds(start, PATCH)], index_ref, sem)
    load.start()
    first_token = group * TOK + member * PATCH

    def column(k):
        return cols_ref[:, k : k + 1]

    shares = []
    for i, owner in enumerate((member, member ^ 2)):
        rows = pl.ds(pl.multiple_of(owner * 64, 64), 64)
        shares += [
            pltpu.make_async_copy(conv_ref.at[i], conv_w_ref.at[rows], local_sem.at[i]),
            pltpu.make_async_copy(later_ref.at[i], w_ref.at[owner], local_sem.at[2 + i]),
        ]
    for copy in shares:
        copy.start()
    pl.semaphore_wait(barrier, count)
    for i, owner in enumerate((member, member ^ 2)):
        rows = pl.ds(pl.multiple_of(owner * 64, 64), 64)
        crossing = [
            remote(conv_ref.at[i], conv_w_ref.at[rows], send2_sem.at[i], recv2_sem.at[i], (group, member ^ 1)),
            remote(later_ref.at[i], w_ref.at[owner], send2_sem.at[2 + i], recv2_sem.at[2 + i], (group, member ^ 1)),
        ]
        for copy in crossing:
            copy.start()
        shares += crossing

    load.wait()
    near = index_ref[...]
    near = jnp.where(near < 0, -1, near - (first_token - HALO))
    places_ref[...] = jnp.concatenate([near, jnp.full((128 - OFFS, PATCH), -1, i32)], axis=0).T
    lanes = iota((256, 512), 1)
    for c in range(4):
        window = wide_ref[c * 256 : c * 256 + 512, :]
        places = places_ref[c * 256 : c * 256 + 256, :] - c * 256
        for b in range(OFFS // 3):
            for k in range(3):
                hot_ref[b % 2, k * 256 : k * 256 + 256, :] = one_hot(lanes, places[:, 3 * b + k : 3 * b + k + 1])
            picked = dot(hot_ref[b % 2], window).astype(bf16)
            for k in range(3):
                at = (3 * b + k) * C
                picked_ref[c * 256 : c * 256 + 256, at : at + C] = picked[k * 256 : k * 256 + 256]
    for copy in shares:
        copy.wait()
    summed = dot_rows(picked_ref[...], conv_w_ref[...]).T
    conv = (summed + column(COL_CONV)).astype(bf16)
    cpe = cpe_ref[...].T
    for c in range(4):
        span = slice(c * 256, c * 256 + 256)
        mixture = dot(cpe, conv[:, span]) + column(COL_CPE)
        x_ref[:, span] = moved_ref[:, span] + norm_columns(
            mixture, column(COL_GAIN + 2), column(COL_SHIFT + 2)
        )

    copies = []

    def emit(c, value):
        span = slice(c * 256, c * 256 + 256)
        place = pl.ds(pl.multiple_of(member * PATCH + c * 256, 256), 256)
        leave_ref[:, span] = value
        for d in (2, 3, 1):
            target = member ^ d
            copy = remote(
                leave_ref.at[pl.ds(pl.multiple_of(target * 64, 64), 64), span], out_ref.at[:, place],
                send_sem.at[c, d], recv_sem.at[c, d], (group, target),
            )
            copy.start()
            copies.append(copy)
        out_ref[:, place] = leave_ref[pl.ds(pl.multiple_of(member * 64, 64), 64), span]

    run_block(1, 3, x_ref, w_ref, 0, cols_ref, scratch, emit, lambda: None)
    for copy in copies:
        copy.wait()


def second_block(wide, moved, neighbours, conv, cpe, later, cols):
    return pl.pallas_call(
        second_kernel,
        out_shape=S((64, TOK), f32),
        in_specs=[VMEM, VMEM, ANY, ANY, VMEM, ANY, VMEM],
        out_specs=VMEM,
        scratch_shapes=[
            pltpu.VMEM((C, PATCH), f32),
            pltpu.VMEM((OFFS, PATCH), i32),
            pltpu.VMEM((PATCH, 128), i32),
            pltpu.VMEM((2, 3 * 256, 512), bf16),
            pltpu.VMEM((PATCH, OFFS * C), bf16),
            pltpu.VMEM((C, OFFS * C), bf16),
            pltpu.VMEM((4, 768, C), bf16),
            pltpu.VMEM((C, PATCH), f32),
            pltpu.SemaphoreType.DMA,
            pltpu.SemaphoreType.DMA((4,)),
            pltpu.SemaphoreType.DMA((4,)),
            pltpu.SemaphoreType.DMA((4,)),
            pltpu.SemaphoreType.DMA((4, 4)),
            pltpu.SemaphoreType.DMA((4, 4)),
        ]
        + block_scratch(),
        compiler_params=kernel_params(collective_id=3, has_side_effects=True),
        name="second_block",
    )(wide, moved, neighbours, conv, cpe, later, cols)


def shards(
    feats, serial_rank, neighbours, norm_gain, norm_bias, qkv_weight, qkv_bias, proj_weight, proj_bias,
    fc1_weight, fc1_bias, fc2_weight, fc2_bias, conv_weight, conv_bias, cpe_weight, cpe_bias,
):
    records, cols, send, listed, landing, leave, conv, later = first_block(
        feats, qkv_weight, proj_weight, fc1_weight, fc2_weight, norm_gain, norm_bias, qkv_bias, proj_bias,
        fc1_bias, fc2_bias, conv_bias.reshape(1, 64), cpe_bias.reshape(1, C), conv_weight,
        serial_rank.reshape(32, 128),
    )
    moved, wide = relay(records, leave, send, listed, landing)
    return second_block(wide, moved, neighbours, conv, cpe_weight, later, cols)


def solution(mesh):
    in_specs = (
        P(None, "order"),
        P("order"),
        P(None, "order"),
        P(),
        P(),
        P(None, None, None, "mp"),
        P(None, None, "mp"),
        P(None, "mp", None),
        P(),
        P(None, None, "mp"),
        P(None, "mp"),
        P(None, "mp", None),
        P(),
        P(None, None, "mp"),
        P("mp"),
        P(),
        P(),
    )
    return jax.shard_map(shards, mesh=mesh, in_specs=in_specs, out_specs=P("mp", "order"), check_vma=False)
```

```python
import functools
import math

import jax
import jax.numpy as jnp
from jax import lax
from jax.experimental import pallas as pl
from jax.experimental.pallas import tpu as pltpu
from jax.sharding import PartitionSpec as P

C = 256
PATCH = 1024
HALO = 128
HDIM = 16
HEADS = 16
OFFS = 27
TOK = 4096
SLOTS = 64
CAP = 288
CAP_OUT = 352
ORDERS = 32
MESH = pl.DeviceIdType.MESH
EPS = 1e-05
LOG2E = math.log2(math.e)
f32, bf16, i32 = jnp.float32, jnp.bfloat16, jnp.int32
VMEM = pl.BlockSpec(memory_space=pltpu.VMEM)
SMEM = pl.BlockSpec(memory_space=pltpu.SMEM)
ANY = pl.BlockSpec(memory_space=pl.ANY)
S = jax.ShapeDtypeStruct
COL_GAIN, COL_SHIFT, COL_PROJ, COL_FC2, COL_QKV, COL_FC1, COL_CONV, COL_CPE = 0, 5, 10, 12, 14, 20, 28, 29


def kernel_params(**more):
    return pltpu.CompilerParams(vmem_limit_bytes=61 * 2**20, **more)


def iota(shape, dim):
    return lax.broadcasted_iota(i32, shape, dim)


def one_hot(left, right):
    return jnp.where(left == right, 1.0, 0.0).astype(bf16)


def dot_rows(left, right):
    return lax.dot_general(left, right, (((1,), (1,)), ((), ())), preferred_element_type=f32)


def dot(left, right):
    return jnp.dot(left, right, preferred_element_type=f32)


def norm_columns(values, gain, shift):
    average = jnp.mean(values, axis=0, keepdims=True)
    centred = values - average
    variance = jnp.mean(centred * centred, axis=0, keepdims=True)
    return centred * lax.rsqrt(variance + EPS) * gain + shift


def greet(order_peers=False, halo=False, across=False):
    barrier = pltpu.get_barrier_semaphore()
    group, member = lax.axis_index("order"), lax.axis_index("mp")
    for d in range(1, 4):
        pl.semaphore_signal(barrier, inc=1, device_id=(group, member ^ d), device_id_type=MESH)
    count = 3
    if order_peers:

        def step(d, carry):
            pl.semaphore_signal(barrier, inc=1, device_id=(group ^ d, member), device_id_type=MESH)
            return carry

        lax.fori_loop(1, ORDERS, step, 0)
        count += ORDERS - 1
    if across:
        pl.semaphore_signal(barrier, inc=1, device_id=(group ^ 1, member ^ 2), device_id_type=MESH)
        count += 1
    if halo:
        for shift in (1, 127):
            pl.semaphore_signal(barrier, inc=1, device_id=neighbour(shift), device_id_type=MESH)
        count += 2
    return barrier, count


def neighbour(shift):
    place = (lax.axis_index("order") * 4 + lax.axis_index("mp") + shift) % 128
    return (place // 4, place % 4)


def remote(src, dst, send, recv, device):
    return pltpu.make_async_remote_copy(
        src_ref=src, dst_ref=dst, send_sem=send, recv_sem=recv, device_id=device, device_id_type=MESH
    )


def prefix_matrix():
    upper = jnp.where(iota((128, 128), 0) < iota((128, 128), 1), 1.0, 0.0).astype(bf16)
    return jnp.concatenate([upper, jnp.ones((128, 128), bf16)], axis=1)


def route_slots(rank_ref, send_ref, leave_ref, scratch):
    (made_ref, slot_ref, spot_ref, left_ref, right_ref, left2_ref, right2_ref, pos_out, pos_in) = scratch[:9]
    group, member = lax.axis_index("order"), lax.axis_index("mp")
    both = prefix_matrix()
    lane = iota((1, 128), 1)

    def classes(c):
        return jnp.where(iota((128, 128), 0) == rank_ref[pl.ds(c, 1), :] // PATCH, 1.0, 0.0)

    def count_classes(c, total):
        made = dot(classes(c).astype(bf16), both)
        made_ref[c] = made
        return total + made[:, 128:]

    total = lax.fori_loop(0, 32, count_classes, jnp.zeros((128, 128), f32), unroll=8)
    row, col = iota((128, 128), 0), iota((128, 128), 1)
    ahead = jnp.where((row // 4 == col // 4) & (col < row), 1.0, 0.0).astype(bf16)

    def number(c, carry):
        made = made_ref[c]
        slot = jnp.sum(classes(c) * (made[:, :128] + carry), axis=0, keepdims=True)
        slot_ref[pl.ds(c, 1), :] = slot.astype(i32)
        return carry + made[:, 128:]

    lax.fori_loop(0, 32, number, dot(ahead, total.astype(bf16)), unroll=4)

    slots = slot_ref[...]
    hot = jnp.where(iota((32, 8, 128), 1) == (slots % 4)[:, None, :], 1.0, 0.0).reshape(256, 128)
    made = dot(hot.astype(bf16), both)
    row, col = iota((256, 256), 0), iota((256, 256), 1)
    earlier = (row % 8 == col % 8) & (row // 64 == col // 64) & (col < row)
    carry = dot(jnp.where(earlier, 1.0, 0.0).astype(bf16), made[:, 128:].astype(bf16))
    spot_ref[...] = jnp.sum((hot * (made[:, :128] + carry)).reshape(32, 8, 128), axis=1).astype(i32)

    def frames(c, carry):
        span = pl.ds(pl.multiple_of(c * 128, 128), 128)
        rank_row, spot_row = rank_ref[pl.ds(c, 1), :], spot_ref[pl.ds(c, 1), :]
        owner = jnp.where(iota((32, 128), 0) == rank_row // TOK, 1.0, 0.0)
        entry = (c // 8) * CAP_OUT + spot_row
        inside = rank_row % TOK
        pieces = [entry // 64, entry % 64, inside // 64, inside % 64]
        left = jnp.concatenate([owner * p.astype(f32) for p in pieces] + [owner], axis=0)
        left_ref[:, span] = left.astype(bf16)
        right_ref[:, span] = one_hot(iota((SLOTS, 128), 0) * 4 + member, slot_ref[pl.ds(c, 1), :])
        return carry

    lax.fori_loop(0, 32, frames, 0, unroll=2)
    acc = dot_rows(left_ref[...], right_ref[...])
    send_ref[...] = (acc[0:32] * 64.0 + acc[32:64]).astype(i32)
    inside = jnp.where(acc[128:160] > 0.5, (acc[64:96] * 64.0 + acc[96:128]).astype(i32), TOK)
    inside = jnp.concatenate([inside, jnp.full((32, 128 - SLOTS), TOK, i32)], axis=1)
    pos_out[...] = jnp.broadcast_to(inside[:, None, :], (32, 8, 128))
    pos_in[group] = pos_out[group]

    def frame_start(d, carry):
        place_frame_copy(scratch, d).start()
        return carry

    lax.fori_loop(1, ORDERS, frame_start, 0)

    def leaving(c, carry):
        span = pl.ds(pl.multiple_of(c * 128, 128), 128)
        at = pl.ds(member * 8 + c, 1)
        hot = jnp.where(iota((8, 128), 0) == slot_ref[at, :] % 4, 1.0, 0.0)
        token = c * 128 + lane
        left = jnp.concatenate([hot * (token // 64).astype(f32), hot * (token % 64).astype(f32)], axis=0)
        left2_ref[:, span] = left.astype(bf16)
        right2_ref[:, span] = one_hot(iota((CAP_OUT, 128), 0), spot_ref[at, :])
        return carry

    lax.fori_loop(0, 8, leaving, 0)
    acc = dot_rows(left2_ref[...], right2_ref[...])
    leave_ref[...] = (acc[0:4] * 64.0 + acc[8:12]).astype(i32)


def route_lists(listed_ref, scratch):
    _, slot_ref, spot_ref, _, _, _, _, _, pos_in, place_out, place_in = scratch[:11]
    group, member = lax.axis_index("order"), lax.axis_index("mp")
    both = prefix_matrix()
    lane = iota((1, 128), 1)

    def frame_wait(d, carry):
        place_frame_copy(scratch, d).wait()
        return carry

    lax.fori_loop(1, ORDERS, frame_wait, 0)
    row, col = iota((256, 256), 0), iota((256, 256), 1)
    pos = pos_in[:, 0, :]
    hot = jnp.where(iota((32, 8, 128), 1) == (pos // PATCH)[:, None, :], 1.0, 0.0).reshape(256, 128)
    made = dot(hot.astype(bf16), both)
    earlier = (row % 8 == col % 8) & (col < row)
    carry = dot(jnp.where(earlier, 1.0, 0.0).astype(bf16), made[:, 128:].astype(bf16))
    spot_ref[...] = jnp.sum((hot * (made[:, :128] + carry)).reshape(32, 8, 128), axis=1).astype(i32)
    slot_ref[...] = pos

    def lists(c, acc):
        inside = slot_ref[pl.ds(c, 1), :]
        hot = jnp.where(iota((8, 128), 0) == inside // PATCH, 1.0, 0.0)
        inside = inside % PATCH
        pieces = [jnp.broadcast_to(c, (1, 128)), lane, inside // 32, inside % 32]
        left = jnp.concatenate([hot * p.astype(f32) for p in pieces] + [hot], axis=0)
        right = one_hot(iota((384, 128), 0), spot_ref[pl.ds(c, 1), :])
        return acc + dot_rows(left.astype(bf16), right)

    acc = lax.fori_loop(0, 32, lists, jnp.zeros((40, 384), f32), unroll=4)
    listed_ref[...] = (acc[0:4] * float(SLOTS) + acc[8:12]).astype(i32)[:, :CAP]
    place = jnp.where(acc[32:36] > 0.5, (acc[16:20] * 32.0 + acc[24:28]).astype(i32), -1)
    place_out[...] = jnp.broadcast_to(place[:, None, :], (4, 8, 384))
    place_in[member] = place_out[member]
    for d in range(1, 4):
        place_list_copy(scratch, d).start()


def route_landing(landing_ref, scratch):
    place_in = scratch[10]
    for d in range(1, 4):
        place_list_copy(scratch, d).wait()
    acc = jnp.zeros((8, PATCH), f32)
    entry = iota((1, 384), 1)
    kind = iota((8, 384), 0)
    for q in range(4):
        right = one_hot(iota((PATCH, 384), 0), place_in[q, 0:1, :])
        at = q * CAP + entry
        left = jnp.where(kind == 0, at // 64, jnp.where(kind == 1, at % 64, 0))
        acc = acc + dot_rows(left.astype(f32).astype(bf16), right)
    landing_ref[...] = (acc[0:1] * 64.0 + acc[1:2]).astype(i32)


def place_frame_copy(scratch, d):
    group, member = lax.axis_index("order"), lax.axis_index("mp")
    pos_out, pos_in, send_sem, recv_sem = scratch[7], scratch[8], scratch[11], scratch[12]
    return remote(
        pos_out.at[group ^ d], pos_in.at[group], send_sem.at[d], recv_sem.at[d], (group ^ d, member)
    )


def place_list_copy(scratch, d):
    group, member = lax.axis_index("order"), lax.axis_index("mp")
    place_out, place_in, send_sem, recv_sem = scratch[9], scratch[10], scratch[13], scratch[14]
    return remote(
        place_out.at[member ^ d], place_in.at[member], send_sem.at[d], recv_sem.at[d], (group, member ^ d)
    )


def route_scratch():
    return [
        pltpu.VMEM((32, 128, 256), f32),
        pltpu.VMEM((32, 128), i32),
        pltpu.VMEM((32, 128), i32),
        pltpu.VMEM((160, TOK), bf16),
        pltpu.VMEM((SLOTS, TOK), bf16),
        pltpu.VMEM((16, PATCH), bf16),
        pltpu.VMEM((CAP_OUT, PATCH), bf16),
        pltpu.VMEM((32, 8, 128), i32),
        pltpu.VMEM((32, 8, 128), i32),
        pltpu.VMEM((4, 8, 384), i32),
        pltpu.VMEM((4, 8, 384), i32),
        pltpu.SemaphoreType.DMA((ORDERS,)),
        pltpu.SemaphoreType.DMA((ORDERS,)),
        pltpu.SemaphoreType.DMA((4,)),
        pltpu.SemaphoreType.DMA((4,)),
    ]


def move_rows(count, index, source, store):
    def step(i, carry):
        records = [source[index(i * 16 + u)] for u in range(16)]
        for u in range(16):
            store(i * 16 + u, records[u])
        return carry

    lax.fori_loop(0, count // 16, step, 0)


def block_scratch():
    return [
        pltpu.VMEM((C, PATCH), bf16),
        pltpu.VMEM((3, C, PATCH), bf16),
        pltpu.VMEM((2, PATCH, 128), bf16),
        pltpu.VMEM((PATCH, PATCH), f32),
        pltpu.VMEM((PATCH, PATCH), f32),
        pltpu.VMEM((2, 8, PATCH), f32),
        pltpu.VMEM((C, PATCH), bf16),
    ]


def run_block(block, first_norm, x_ref, w_ref, base, cols_ref, scratch, emit, between, parts=((0, 1024),)):
    normed_ref, qkv_ref, keys_ref, s0_ref, s1_ref, top_ref, heads_ref = scratch

    def column(k):
        return cols_ref[:, k : k + 1]

    for c in range(4):
        span = slice(c * 256, c * 256 + 256)
        normed_ref[:, span] = norm_columns(
            x_ref[:, span], column(COL_GAIN + first_norm), column(COL_SHIFT + first_norm)
        ).astype(bf16)
    for r in range(4):
        made = dot(w_ref[r, base : base + 192, :], normed_ref[...])
        for j in range(3):
            bias = cols_ref[r * 64 : r * 64 + 64, COL_QKV + 3 * block + j : COL_QKV + 3 * block + j + 1]
            qkv_ref[j, r * 64 : r * 64 + 64, :] = (made[j * 64 : j * 64 + 64] + bias).astype(bf16)
    for g in range(2):
        keys_ref[g] = qkv_ref[1, g * 128 : g * 128 + 128, :].T

    head_of_row = iota((128, 1), 0) // HDIM
    buffers = (s0_ref, s1_ref)

    def attention(first, width):
        span = slice(first, first + width)

        def scores(h, b):
            g = h // 8
            queries = qkv_ref[0, pl.ds(pl.multiple_of(g * 128, 128), 128), span]
            queries = jnp.where(head_of_row == h % 8, queries.astype(f32), 0.0).astype(bf16)
            s = dot(keys_ref[g], queries)
            buffers[b][:, :width] = s
            top_ref[b, 0:1, :width] = jnp.max(s, axis=0, keepdims=True)

        def finish(h, b):
            p = jnp.exp2((buffers[b][:, :width] - top_ref[b, 0:1, :width]) * (0.25 * LOG2E))
            inverse = 1.0 / jnp.sum(p, axis=0, keepdims=True)
            chances = (p * inverse).astype(bf16)
            rows = pl.ds(pl.multiple_of(h * HDIM, HDIM), HDIM)
            heads_ref[rows, span] = dot(qkv_ref[2, rows, :], chances).astype(bf16)

        scores(0, 0)

        def pair(j, carry):
            h = 2 * j
            scores(h + 1, 1)
            finish(h, 0)
            scores(jnp.minimum(h + 2, HEADS - 1), 0)
            finish(h + 1, 1)
            return carry

        lax.fori_loop(0, HEADS // 2, pair, 0)

    for n, (first, width) in enumerate(parts):
        attention(first, width)
        if n == 0:
            between()
            proj = [w_ref[r, base + 192 : base + 256, :].T for r in range(4)]
        for c in range(first // 256, (first + width) // 256):
            span = slice(c * 256, c * 256 + 256)
            mixed = dot(proj[0], heads_ref[0:64, span])
            for r in range(1, 4):
                mixed = mixed + dot(proj[r], heads_ref[r * 64 : r * 64 + 64, span])
            attended = x_ref[:, span] + (mixed + column(COL_PROJ + block))
            normed = norm_columns(
                attended, column(COL_GAIN + first_norm + 1), column(COL_SHIFT + first_norm + 1)
            ).astype(bf16)
            total = None
            for r in range(4):
                hidden = dot(w_ref[r, base + 256 : base + 512, :], normed) + column(COL_FC1 + 4 * block + r)
                hidden = 0.5 * hidden * (1.0 + lax.erf(hidden * math.sqrt(0.5)))
                part = dot(w_ref[r, base + 512 : base + 768, :], hidden.astype(bf16))
                total = part if total is None else total + part
            emit(c, attended + (total + column(COL_FC2 + block)))


def first_kernel(
    feats_ref, qkv_w_ref, proj_w_ref, fc1_w_ref, fc2_w_ref, gain_ref, shift_ref, qkv_b_ref, proj_b_ref,
    fc1_b_ref, fc2_b_ref, conv_b_ref, cpe_b_ref, conv_w_ref, rank_ref,
    records_ref, cols_ref, send_ref, listed_ref, landing_ref, leave_ref, conv_ref, later_ref,
    x_ref, w_ref, params_ref, conv_own_ref, later_own_ref,
    sem, send_sem, recv_sem, local_sem, send3_sem, recv3_sem, *scratch
):
    group, member = lax.axis_index("order"), lax.axis_index("mp")
    routing, scratch = scratch[:15], scratch[15:]
    barrier, count = greet(order_peers=True, across=True)
    start = pl.multiple_of(member * PATCH, PATCH)
    load = pltpu.make_async_copy(feats_ref.at[:, pl.ds(start, PATCH)], x_ref, sem)
    load.start()

    pad = jnp.zeros((16, C - 64), f32)
    narrow = jnp.concatenate(
        [qkv_b_ref[j, b : b + 1].astype(f32) for b in range(2) for j in range(3)]
        + [conv_b_ref[...].astype(f32), jnp.zeros((9, 64), f32)],
        axis=0,
    )
    narrow = jnp.concatenate([narrow, pad], axis=1)
    wide = jnp.concatenate([jnp.zeros((8, C), f32), fc1_b_ref[...].astype(f32), jnp.zeros((6, C), f32)], axis=0)
    w_ref[member, 0:16, :] = (narrow + wide).astype(bf16)
    for j in range(3):
        w_ref[member, 16 + j * 64 : 80 + j * 64, :] = qkv_w_ref[0, j]

    def weight_copy(part, d):
        rows = (pl.ds(0, 208), pl.ds(208, 576))[part]
        return remote(
            w_ref.at[member, rows], w_ref.at[member, rows], send_sem.at[part, d], recv_sem.at[part, d],
            (group, member ^ d),
        )

    pl.semaphore_wait(barrier, count)
    for d in (2, 3, 1):
        weight_copy(0, d).start()
    route_slots(rank_ref, send_ref, leave_ref, routing)
    w_ref[member, 208:272, :] = proj_w_ref[0]
    w_ref[member, 272:528, :] = fc1_w_ref[0].T
    w_ref[member, 528:784, :] = fc2_w_ref[0].T
    for d in (2, 3, 1):
        weight_copy(1, d).start()

    def turn(k, carry):
        span = pl.ds(pl.multiple_of(k * C, C), C)
        conv_own_ref[:, span] = conv_w_ref[k]
        return carry

    lax.fori_loop(0, OFFS, turn, 0, unroll=3)
    for j in range(3):
        later_own_ref[j * 64 : j * 64 + 64, :] = qkv_w_ref[1, j]
    later_own_ref[192:256, :] = proj_w_ref[1]
    later_own_ref[256:512, :] = fc1_w_ref[1].T
    later_own_ref[512:768, :] = fc2_w_ref[1].T
    later = [
        remote(conv_own_ref, conv_ref.at[1], send3_sem.at[0], recv3_sem.at[0], (group ^ 1, member ^ 2)),
        remote(later_own_ref, later_ref.at[1], send3_sem.at[1], recv3_sem.at[1], (group, member ^ 2)),
        pltpu.make_async_copy(conv_own_ref, conv_ref.at[0], local_sem.at[0]),
        pltpu.make_async_copy(later_own_ref, later_ref.at[0], local_sem.at[1]),
    ]
    for copy in later:
        copy.start()
    load.wait()
    for d in (2, 3, 1):
        weight_copy(0, d).wait()

    params_ref[...] = jnp.zeros_like(params_ref)
    params_ref[COL_GAIN : COL_GAIN + 5, :] = gain_ref[...]
    params_ref[COL_SHIFT : COL_SHIFT + 5, :] = shift_ref[...]
    params_ref[COL_PROJ : COL_PROJ + 2, :] = proj_b_ref[...].astype(f32)
    params_ref[COL_FC2 : COL_FC2 + 2, :] = fc2_b_ref[...].astype(f32)
    bias = [w_ref[r, 0:16, :].astype(f32) for r in range(4)]
    narrow = jnp.concatenate([b[0:8, 0:64] for b in bias], axis=1)
    params_ref[COL_QKV : COL_QKV + 6, :] = narrow[0:6]
    params_ref[COL_CONV : COL_CONV + 1, :] = narrow[6:7]
    for r in range(4):
        for b in range(2):
            params_ref[COL_FC1 + 4 * b + r : COL_FC1 + 4 * b + r + 1, :] = bias[r][8 + b : 9 + b]
    halves = cpe_b_ref[...].astype(f32)
    params_ref[COL_CPE : COL_CPE + 1, :] = jnp.concatenate([halves[0:1], halves[1:2]], axis=1)
    cols_ref[...] = params_ref[...].T

    def emit(c, value):
        rows = value.T
        for half in range(2):
            records_ref[c * 256 : c * 256 + 256, half, :] = rows[:, half * 128 : half * 128 + 128]

    def between():
        route_lists(listed_ref, routing)
        for d in (2, 3, 1):
            weight_copy(1, d).wait()

    run_block(0, 0, x_ref, w_ref, 16, cols_ref, scratch, emit, between)
    route_landing(landing_ref, routing)
    for copy in later:
        copy.wait()


def first_block(*operands):
    return pl.pallas_call(
        first_kernel,
        out_shape=[
            S((PATCH, 2, 128), f32),
            S((C, 128), f32),
            S((ORDERS, SLOTS), i32),
            S((4, CAP), i32),
            S((1, PATCH), i32),
            S((4, CAP_OUT), i32),
            S((2, 64, OFFS * C), bf16),
            S((2, 768, C), bf16),
        ],
        in_specs=[ANY] + [VMEM] * 14,
        out_specs=[VMEM] * 6 + [ANY] * 2,
        scratch_shapes=[
            pltpu.VMEM((C, PATCH), f32),
            pltpu.VMEM((4, 784, C), bf16),
            pltpu.VMEM((128, C), f32),
            pltpu.VMEM((64, OFFS * C), bf16),
            pltpu.VMEM((768, C), bf16),
            pltpu.SemaphoreType.DMA,
            pltpu.SemaphoreType.DMA((2, 4)),
            pltpu.SemaphoreType.DMA((2, 4)),
            pltpu.SemaphoreType.DMA((2,)),
            pltpu.SemaphoreType.DMA((2,)),
            pltpu.SemaphoreType.DMA((2,)),
        ]
        + route_scratch()
        + block_scratch(),
        compiler_params=kernel_params(collective_id=1, has_side_effects=True),
        name="first_block",
    )(*operands)


def second_kernel(
    records_ref, leave_ref, send_ref, listed_ref, landing_ref, near_ref, conv_ref, cpe_ref, later_ref, cols_ref,
    out_ref,
    leaving_ref, rows_ref, packed_ref, frames_ref, sorted_ref, lists_ref, land_ref, wide_ref,
    x_ref, index_ref, places_ref, hot_ref, picked_ref, conv_w_ref, w_ref, leave_out_ref,
    sem, local_sem, send_sem, recv_sem, send2_sem, recv2_sem, send3_sem, recv3_sem, send4_sem, recv4_sem,
    send5_sem, recv5_sem, send6_sem, recv6_sem, *scratch
):
    group, member = lax.axis_index("order"), lax.axis_index("mp")
    barrier, count = greet(order_peers=True, halo=True)
    start = pl.multiple_of(member * PATCH, PATCH)
    load = pltpu.make_async_copy(near_ref.at[:, pl.ds(start, PATCH)], index_ref, sem)
    load.start()
    first_token = group * TOK + member * PATCH

    def column(k):
        return cols_ref[:, k : k + 1]

    shares = []
    for i, owner in enumerate((member, member ^ 2)):
        rows = pl.ds(pl.multiple_of(owner * 64, 64), 64)
        shares += [
            pltpu.make_async_copy(conv_ref.at[i], conv_w_ref.at[rows], local_sem.at[i]),
            pltpu.make_async_copy(later_ref.at[i], w_ref.at[owner], local_sem.at[2 + i]),
        ]
    for copy in shares:
        copy.start()
    copies = []
    for d in (2, 3, 1):
        target = member ^ d

        def store(r, record, d=d):
            leaving_ref[d, r] = record

        move_rows(CAP_OUT, lambda r: leave_ref[target, r], records_ref, store)
        if d == 2:
            pl.semaphore_wait(barrier, count)
        copy = remote(
            leaving_ref.at[d], rows_ref.at[pl.ds(member * CAP_OUT, CAP_OUT)], send4_sem.at[d], recv4_sem.at[d],
            (group, target),
        )
        copy.start()
        copies.append(copy)

    def store_staying(r, record):
        rows_ref[member * CAP_OUT + r] = record

    move_rows(CAP_OUT, lambda r: leave_ref[member, r], records_ref, store_staying)
    for copy in copies:
        copy.wait()

    def frame_copy(d):
        return remote(
            packed_ref.at[d], frames_ref.at[pl.ds(pl.multiple_of(group * SLOTS, SLOTS), SLOTS)],
            send_sem.at[d], recv_sem.at[d], (group ^ d, member),
        )

    def pack(t, carry):
        d = 1 + (t + 8 * member + 7 * group) % (ORDERS - 1)
        target = group ^ d

        def store(r, record):
            packed_ref[d, r] = record

        move_rows(SLOTS, lambda r: send_ref[target, r], rows_ref, store)
        frame_copy(d).start()
        return carry

    lax.fori_loop(0, ORDERS - 1, pack, 0)

    def store_own(r, record):
        frames_ref[group * SLOTS + r] = record

    move_rows(SLOTS, lambda r: send_ref[group, r], rows_ref, store_own)

    for i, owner in enumerate((member, member ^ 2)):
        rows = pl.ds(pl.multiple_of(owner * 64, 64), 64)
        crossing = [
            remote(conv_ref.at[i], conv_w_ref.at[rows], send5_sem.at[i], recv5_sem.at[i], (group, member ^ 1)),
            remote(later_ref.at[i], w_ref.at[owner], send5_sem.at[2 + i], recv5_sem.at[2 + i], (group, member ^ 1)),
        ]
        for copy in crossing:
            copy.start()
        shares += crossing
    load.wait()
    near = index_ref[...]
    near = jnp.where(near < 0, -1, near - (first_token - HALO))
    places_ref[...] = jnp.concatenate([near, jnp.full((128 - OFFS, PATCH), -1, i32)], axis=0).T

    def frame_wait(d, carry):
        frame_copy(d).wait()
        return carry

    lax.fori_loop(1, ORDERS, frame_wait, 0)

    copies = []
    for d in (2, 3, 1):
        target = member ^ d

        def store(r, record, d=d):
            sorted_ref[d, r] = record

        move_rows(CAP, lambda r: listed_ref[target, r], frames_ref, store)
        copy = remote(
            sorted_ref.at[d], lists_ref.at[pl.ds(member * CAP, CAP)], send2_sem.at[d], recv2_sem.at[d],
            (group, target),
        )
        copy.start()
        copies.append(copy)

    def store_mine(r, record):
        lists_ref[member * CAP + r] = record

    move_rows(CAP, lambda r: listed_ref[member, r], frames_ref, store_mine)
    for copy in copies:
        copy.wait()

    def land(start, rows):
        def store(r, record):
            land_ref[start + r] = record

        move_rows(rows, lambda r: landing_ref[0, start + r], lists_ref, store)
        for half in range(2):
            part = land_ref[start : start + rows, half, :]
            at = slice(half * 128, half * 128 + 128)
            x_ref[at, start : start + rows] = part.T
            wide_ref[HALO + start : HALO + start + rows, at] = part.astype(bf16)

    land(0, HALO)
    land(PATCH - HALO, HALO)
    halos = [
        remote(
            wide_ref.at[HALO : 2 * HALO], wide_ref.at[HALO + PATCH : 2 * HALO + PATCH],
            send3_sem.at[0], recv3_sem.at[0], neighbour(127),
        ),
        remote(
            wide_ref.at[PATCH : PATCH + HALO], wide_ref.at[0:HALO],
            send3_sem.at[1], recv3_sem.at[1], neighbour(1),
        ),
    ]
    for copy in halos:
        copy.start()
    for c in range(3):
        land(HALO + c * 256, 256)
    for copy in halos:
        copy.wait()

    lanes = iota((256, 512), 1)
    for c in range(4):
        window = wide_ref[c * 256 : c * 256 + 512, :]
        places = places_ref[c * 256 : c * 256 + 256, :] - c * 256
        for b in range(OFFS // 3):
            for k in range(3):
                hot_ref[b % 2, k * 256 : k * 256 + 256, :] = one_hot(lanes, places[:, 3 * b + k : 3 * b + k + 1])
            picked = dot(hot_ref[b % 2], window).astype(bf16)
            for k in range(3):
                at = (3 * b + k) * C
                picked_ref[c * 256 : c * 256 + 256, at : at + C] = picked[k * 256 : k * 256 + 256]
    for copy in shares:
        copy.wait()
    summed = dot_rows(picked_ref[...], conv_w_ref[...]).T
    conv = (summed + column(COL_CONV)).astype(bf16)
    cpe = cpe_ref[...].T
    for c in range(4):
        span = slice(c * 256, c * 256 + 256)
        mixture = dot(cpe, conv[:, span]) + column(COL_CPE)
        x_ref[:, span] = x_ref[:, span] + norm_columns(
            mixture, column(COL_GAIN + 2), column(COL_SHIFT + 2)
        )

    copies = []

    def emit(c, value):
        span = slice(c * 256, c * 256 + 256)
        place = pl.ds(pl.multiple_of(member * PATCH + c * 256, 256), 256)
        leave_out_ref[:, span] = value
        for d in (2, 3, 1):
            target = member ^ d
            copy = remote(
                leave_out_ref.at[pl.ds(pl.multiple_of(target * 64, 64), 64), span], out_ref.at[:, place],
                send6_sem.at[c, d], recv6_sem.at[c, d], (group, target),
            )
            copy.start()
            copies.append(copy)
        out_ref[:, place] = leave_out_ref[pl.ds(pl.multiple_of(member * 64, 64), 64), span]

    run_block(1, 3, x_ref, w_ref, 0, cols_ref, scratch, emit, lambda: None, ((0, 768), (768, 256)))
    for copy in copies:
        copy.wait()


def second_block(*operands):
    pairs = [pltpu.SemaphoreType.DMA((ORDERS,))] * 2 + [pltpu.SemaphoreType.DMA((4,))] * 2
    pairs += [pltpu.SemaphoreType.DMA((2,))] * 2 + [pltpu.SemaphoreType.DMA((4,))] * 4
    pairs += [pltpu.SemaphoreType.DMA((4, 4))] * 2
    return pl.pallas_call(
        second_kernel,
        out_shape=S((64, TOK), f32),
        in_specs=[VMEM, SMEM, SMEM, SMEM, SMEM, ANY, ANY, VMEM, ANY, VMEM],
        out_specs=VMEM,
        scratch_shapes=[
            pltpu.VMEM((4, CAP_OUT, 2, 128), f32),
            pltpu.VMEM((4 * CAP_OUT, 2, 128), f32),
            pltpu.VMEM((ORDERS, SLOTS, 2, 128), f32),
            pltpu.VMEM((ORDERS * SLOTS, 2, 128), f32),
            pltpu.VMEM((4, CAP, 2, 128), f32),
            pltpu.VMEM((4 * CAP, 2, 128), f32),
            pltpu.VMEM((PATCH, 2, 128), f32),
            pltpu.VMEM((PATCH + 2 * HALO, C), bf16),
            pltpu.VMEM((C, PATCH), f32),
            pltpu.VMEM((OFFS, PATCH), i32),
            pltpu.VMEM((PATCH, 128), i32),
            pltpu.VMEM((2, 3 * 256, 512), bf16),
            pltpu.VMEM((PATCH, OFFS * C), bf16),
            pltpu.VMEM((C, OFFS * C), bf16),
            pltpu.VMEM((4, 768, C), bf16),
            pltpu.VMEM((C, PATCH), f32),
            pltpu.SemaphoreType.DMA,
            pltpu.SemaphoreType.DMA((4,)),
        ]
        + pairs
        + block_scratch(),
        compiler_params=kernel_params(collective_id=2, has_side_effects=True),
        name="second_block",
    )(*operands)


def shards(
    feats, serial_rank, neighbours, norm_gain, norm_bias, qkv_weight, qkv_bias, proj_weight, proj_bias,
    fc1_weight, fc1_bias, fc2_weight, fc2_bias, conv_weight, conv_bias, cpe_weight, cpe_bias,
):
    records, cols, send, listed, landing, leave, conv, later = first_block(
        feats, qkv_weight.transpose(0, 1, 3, 2), proj_weight, fc1_weight, fc2_weight, norm_gain, norm_bias,
        qkv_bias.transpose(1, 0, 2), proj_bias, fc1_bias, fc2_bias, conv_bias.reshape(1, 64),
        cpe_bias.reshape(2, 128), conv_weight.transpose(0, 2, 1),
        serial_rank.reshape(32, 128),
    )
    return second_block(
        records, leave, send, listed, landing, neighbours, conv, cpe_weight, later, cols
    )


def solution(mesh):
    in_specs = (
        P(None, "order"),
        P("order"),
        P(None, "order"),
        P(),
        P(),
        P(None, None, None, "mp"),
        P(None, None, "mp"),
        P(None, "mp", None),
        P(),
        P(None, None, "mp"),
        P(None, "mp"),
        P(None, "mp", None),
        P(),
        P(None, None, "mp"),
        P("mp"),
        P(),
        P(),
    )
    return jax.shard_map(shards, mesh=mesh, in_specs=in_specs, out_specs=P("mp", "order"), check_vma=False)
```

```python
import functools
import math

import jax
import jax.numpy as jnp
from jax import lax
from jax.experimental import pallas as pl
from jax.experimental.pallas import tpu as pltpu
from jax.sharding import PartitionSpec as P

C = 256
PATCH = 1024
HALO = 128
HDIM = 16
HEADS = 16
OFFS = 27
TOK = 4096
SLOTS = 64
CAP = 288
CAP_OUT = 352
STRIDE = 384
ORDERS = 32
MESH = pl.DeviceIdType.MESH
EPS = 1e-05
LOG2E = math.log2(math.e)
f32, bf16, i32 = jnp.float32, jnp.bfloat16, jnp.int32
VMEM = pl.BlockSpec(memory_space=pltpu.VMEM)
SMEM = pl.BlockSpec(memory_space=pltpu.SMEM)
ANY = pl.BlockSpec(memory_space=pl.ANY)
S = jax.ShapeDtypeStruct
COL_GAIN, COL_SHIFT, COL_PROJ, COL_FC2, COL_QKV, COL_FC1, COL_CONV, COL_CPE = 0, 5, 10, 12, 14, 20, 28, 29


def kernel_params(**more):
    return pltpu.CompilerParams(vmem_limit_bytes=61 * 2**20, **more)


def iota(shape, dim):
    return lax.broadcasted_iota(i32, shape, dim)


def one_hot(left, right):
    return jnp.where(left == right, 1.0, 0.0).astype(bf16)


def dot_rows(left, right):
    return lax.dot_general(left, right, (((1,), (1,)), ((), ())), preferred_element_type=f32)


def dot(left, right):
    return jnp.dot(left, right, preferred_element_type=f32)


def norm_columns(values, gain, shift):
    average = jnp.mean(values, axis=0, keepdims=True)
    centred = values - average
    variance = jnp.mean(centred * centred, axis=0, keepdims=True)
    return centred * lax.rsqrt(variance + EPS) * gain + shift


def greet(order_peers=False, halo=False, across=False):
    barrier = pltpu.get_barrier_semaphore()
    group, member = lax.axis_index("order"), lax.axis_index("mp")
    for d in range(1, 4):
        pl.semaphore_signal(barrier, inc=1, device_id=(group, member ^ d), device_id_type=MESH)
    count = 3
    if order_peers:

        def step(d, carry):
            pl.semaphore_signal(barrier, inc=1, device_id=(group ^ d, member), device_id_type=MESH)
            return carry

        lax.fori_loop(1, ORDERS, step, 0)
        count += ORDERS - 1
    if across:
        pl.semaphore_signal(barrier, inc=1, device_id=(group ^ 1, member ^ 2), device_id_type=MESH)
        count += 1
    if halo:
        for shift in (1, 127):
            pl.semaphore_signal(barrier, inc=1, device_id=neighbour(shift), device_id_type=MESH)
        count += 2
    return barrier, count


def neighbour(shift):
    place = (lax.axis_index("order") * 4 + lax.axis_index("mp") + shift) % 128
    return (place // 4, place % 4)


def remote(src, dst, send, recv, device):
    return pltpu.make_async_remote_copy(
        src_ref=src, dst_ref=dst, send_sem=send, recv_sem=recv, device_id=device, device_id_type=MESH
    )


def in_rows(lists):
    rows = [lists[q : q + 1, k * 128 : k * 128 + 128] for q in range(4) for k in range(STRIDE // 128)]
    return jnp.concatenate(rows + [jnp.zeros((4, 128), i32)], axis=0)


def prefix_matrix():
    upper = jnp.where(iota((128, 128), 0) < iota((128, 128), 1), 1.0, 0.0).astype(bf16)
    return jnp.concatenate([upper, jnp.ones((128, 128), bf16)], axis=1)


def route_slots(rank_ref, send_ref, leave_ref, scratch):
    (made_ref, slot_ref, spot_ref, left_ref, right_ref, left2_ref, right2_ref, pos_out, pos_in) = scratch[:9]
    group, member = lax.axis_index("order"), lax.axis_index("mp")
    both = prefix_matrix()
    lane = iota((1, 128), 1)

    def classes(c):
        return jnp.where(iota((128, 128), 0) == rank_ref[pl.ds(c, 1), :] // PATCH, 1.0, 0.0)

    def count_classes(c, total):
        made = dot(classes(c).astype(bf16), both)
        made_ref[c] = made
        return total + made[:, 128:]

    total = lax.fori_loop(0, 32, count_classes, jnp.zeros((128, 128), f32), unroll=8)
    row, col = iota((128, 128), 0), iota((128, 128), 1)
    ahead = jnp.where((row // 4 == col // 4) & (col < row), 1.0, 0.0).astype(bf16)

    def number(c, carry):
        made = made_ref[c]
        slot = jnp.sum(classes(c) * (made[:, :128] + carry), axis=0, keepdims=True)
        slot_ref[pl.ds(c, 1), :] = slot.astype(i32)
        return carry + made[:, 128:]

    lax.fori_loop(0, 32, number, dot(ahead, total.astype(bf16)), unroll=4)

    slots = slot_ref[...]
    hot = jnp.where(iota((32, 8, 128), 1) == (slots % 4)[:, None, :], 1.0, 0.0).reshape(256, 128)
    made = dot(hot.astype(bf16), both)
    row, col = iota((256, 256), 0), iota((256, 256), 1)
    earlier = (row % 8 == col % 8) & (row // 64 == col // 64) & (col < row)
    carry = dot(jnp.where(earlier, 1.0, 0.0).astype(bf16), made[:, 128:].astype(bf16))
    spot_ref[...] = jnp.sum((hot * (made[:, :128] + carry)).reshape(32, 8, 128), axis=1).astype(i32)

    def frames(c, carry):
        span = pl.ds(pl.multiple_of(c * 128, 128), 128)
        rank_row, spot_row = rank_ref[pl.ds(c, 1), :], spot_ref[pl.ds(c, 1), :]
        owner = jnp.where(iota((32, 128), 0) == rank_row // TOK, 1.0, 0.0)
        entry = (c // 8) * CAP_OUT + spot_row
        inside = rank_row % TOK
        pieces = [entry // 64, entry % 64, inside // 64, inside % 64]
        left = jnp.concatenate([owner * p.astype(f32) for p in pieces] + [owner], axis=0)
        left_ref[:, span] = left.astype(bf16)
        right_ref[:, span] = one_hot(iota((SLOTS, 128), 0) * 4 + member, slot_ref[pl.ds(c, 1), :])
        return carry

    lax.fori_loop(0, 32, frames, 0, unroll=2)
    acc = dot_rows(left_ref[...], right_ref[...])
    send = (acc[0:32] * 64.0 + acc[32:64]).astype(i32)
    send_ref[...] = jnp.concatenate([send, jnp.zeros((32, 128 - SLOTS), i32)], axis=1)
    inside = jnp.where(acc[128:160] > 0.5, (acc[64:96] * 64.0 + acc[96:128]).astype(i32), TOK)
    unused = jnp.full((32, SLOTS), TOK, i32)
    inside = jnp.where(
        group % 2 == 0,
        jnp.concatenate([inside, unused], axis=1),
        jnp.concatenate([unused, inside], axis=1),
    )
    pos_out[...] = jnp.broadcast_to(inside[:, None, :], (32, 8, 128))
    pos_in[group] = pos_out[group]

    def frame_start(d, carry):
        place_frame_copy(scratch, d).start()
        return carry

    lax.fori_loop(1, ORDERS, frame_start, 0)

    def leaving(c, carry):
        span = pl.ds(pl.multiple_of(c * 128, 128), 128)
        at = pl.ds(member * 8 + c, 1)
        hot = jnp.where(iota((8, 128), 0) == slot_ref[at, :] % 4, 1.0, 0.0)
        token = c * 128 + lane
        left = jnp.concatenate([hot * (token // 64).astype(f32), hot * (token % 64).astype(f32)], axis=0)
        left2_ref[:, span] = left.astype(bf16)
        right2_ref[:, span] = one_hot(iota((CAP_OUT, 128), 0), spot_ref[at, :])
        return carry

    lax.fori_loop(0, 8, leaving, 0)
    acc = dot_rows(left2_ref[...], right2_ref[...])
    leave = (acc[0:4] * 64.0 + acc[8:12]).astype(i32)
    leave_ref[...] = in_rows(jnp.concatenate([leave, jnp.zeros((4, STRIDE - CAP_OUT), i32)], axis=1))


def route_lists(listed_ref, scratch):
    _, slot_ref, spot_ref, _, _, _, _, _, pos_in, place_out, place_in = scratch[:11]
    group, member = lax.axis_index("order"), lax.axis_index("mp")
    both = prefix_matrix()
    lane = iota((1, 128), 1)

    def frame_wait(d, carry):
        place_frame_copy(scratch, d).wait()
        return carry

    lax.fori_loop(1, ORDERS, frame_wait, 0)
    row, col = iota((128, 128), 0), iota((128, 128), 1)
    pos = jnp.min(pos_in[:, 0, :].reshape(16, 2, 128), axis=1)
    hot = jnp.where(iota((16, 8, 128), 1) == (pos // PATCH)[:, None, :], 1.0, 0.0).reshape(128, 128)
    made = dot(hot.astype(bf16), both)
    earlier = (row % 8 == col % 8) & (col < row)
    carry = dot(jnp.where(earlier, 1.0, 0.0).astype(bf16), made[:, 128:].astype(bf16))
    spot_ref[0:16, :] = jnp.sum((hot * (made[:, :128] + carry)).reshape(16, 8, 128), axis=1).astype(i32)
    slot_ref[0:16, :] = pos

    def lists(c, acc):
        inside = slot_ref[pl.ds(c, 1), :]
        hot = jnp.where(iota((8, 128), 0) == inside // PATCH, 1.0, 0.0)
        inside = inside % PATCH
        pieces = [2 * c + lane // SLOTS, lane % SLOTS, inside // 32, inside % 32]
        left = jnp.concatenate([hot * p.astype(f32) for p in pieces] + [hot], axis=0)
        right = one_hot(iota((384, 128), 0), spot_ref[pl.ds(c, 1), :])
        return acc + dot_rows(left.astype(bf16), right)

    acc = lax.fori_loop(0, 16, lists, jnp.zeros((40, 384), f32), unroll=8)
    listed_ref[...] = in_rows((acc[0:4] * float(SLOTS) + acc[8:12]).astype(i32))
    place = jnp.where(acc[32:36] > 0.5, (acc[16:20] * 32.0 + acc[24:28]).astype(i32), -1)
    place_out[...] = jnp.broadcast_to(place[:, None, :], (4, 8, 384))
    place_in[member] = place_out[member]
    for d in range(1, 4):
        place_list_copy(scratch, d).start()


def route_landing(landing_ref, scratch):
    place_in = scratch[10]
    for d in range(1, 4):
        place_list_copy(scratch, d).wait()
    acc = jnp.zeros((8, PATCH), f32)
    entry = iota((1, 384), 1)
    kind = iota((8, 384), 0)
    for q in range(4):
        right = one_hot(iota((PATCH, 384), 0), place_in[q, 0:1, :])
        at = q * CAP + entry
        left = jnp.where(kind == 0, at // 64, jnp.where(kind == 1, at % 64, 0))
        acc = acc + dot_rows(left.astype(f32).astype(bf16), right)
    landing = (acc[0:1] * 64.0 + acc[1:2]).astype(i32)
    landing_ref[...] = jnp.concatenate([landing[:, k * 128 : k * 128 + 128] for k in range(8)], axis=0)


def place_frame_copy(scratch, d):
    group, member = lax.axis_index("order"), lax.axis_index("mp")
    pos_out, pos_in, send_sem, recv_sem = scratch[7], scratch[8], scratch[11], scratch[12]
    return remote(
        pos_out.at[group ^ d], pos_in.at[group], send_sem.at[d], recv_sem.at[d], (group ^ d, member)
    )


def place_list_copy(scratch, d):
    group, member = lax.axis_index("order"), lax.axis_index("mp")
    place_out, place_in, send_sem, recv_sem = scratch[9], scratch[10], scratch[13], scratch[14]
    return remote(
        place_out.at[member ^ d], place_in.at[member], send_sem.at[d], recv_sem.at[d], (group, member ^ d)
    )


def route_scratch():
    return [
        pltpu.VMEM((32, 128, 256), f32),
        pltpu.VMEM((32, 128), i32),
        pltpu.VMEM((32, 128), i32),
        pltpu.VMEM((160, TOK), bf16),
        pltpu.VMEM((SLOTS, TOK), bf16),
        pltpu.VMEM((16, PATCH), bf16),
        pltpu.VMEM((CAP_OUT, PATCH), bf16),
        pltpu.VMEM((32, 8, 128), i32),
        pltpu.VMEM((32, 8, 128), i32),
        pltpu.VMEM((4, 8, 384), i32),
        pltpu.VMEM((4, 8, 384), i32),
        pltpu.SemaphoreType.DMA((ORDERS,)),
        pltpu.SemaphoreType.DMA((ORDERS,)),
        pltpu.SemaphoreType.DMA((4,)),
        pltpu.SemaphoreType.DMA((4,)),
    ]


def move_rows(count, index, source, store):
    def step(i, carry):
        records = [source[index(i * 32 + u)] for u in range(32)]
        for u in range(32):
            store(i * 32 + u, records[u])
        return carry

    lax.fori_loop(0, count // 32, step, 0)


def block_scratch():
    return [
        pltpu.VMEM((C, PATCH), bf16),
        pltpu.VMEM((3, C, PATCH), bf16),
        pltpu.VMEM((2, PATCH, 128), bf16),
        pltpu.VMEM((PATCH, PATCH), f32),
        pltpu.VMEM((PATCH, PATCH), f32),
        pltpu.VMEM((2, 8, PATCH), f32),
        pltpu.VMEM((C, PATCH), bf16),
    ]


def run_block(block, first_norm, x_ref, w_ref, base, cols_ref, scratch, emit, between, parts=((0, 1024),)):
    normed_ref, qkv_ref, keys_ref, s0_ref, s1_ref, top_ref, heads_ref = scratch

    def column(k):
        return cols_ref[:, k : k + 1]

    for c in range(4):
        span = slice(c * 256, c * 256 + 256)
        normed_ref[:, span] = norm_columns(
            x_ref[:, span], column(COL_GAIN + first_norm), column(COL_SHIFT + first_norm)
        ).astype(bf16)
    for r in range(4):
        made = dot(w_ref[r, base : base + 192, :], normed_ref[...])
        for j in range(3):
            bias = cols_ref[r * 64 : r * 64 + 64, COL_QKV + 3 * block + j : COL_QKV + 3 * block + j + 1]
            qkv_ref[j, r * 64 : r * 64 + 64, :] = (made[j * 64 : j * 64 + 64] + bias).astype(bf16)
    for g in range(2):
        keys_ref[g] = qkv_ref[1, g * 128 : g * 128 + 128, :].T

    head_of_row = iota((128, 1), 0) // HDIM
    buffers = (s0_ref, s1_ref)

    def attention(first, width):
        span = slice(first, first + width)

        def scores(h, b):
            g = h // 8
            queries = qkv_ref[0, pl.ds(pl.multiple_of(g * 128, 128), 128), span]
            queries = jnp.where(head_of_row == h % 8, queries.astype(f32), 0.0).astype(bf16)
            s = dot(keys_ref[g], queries)
            buffers[b][:, :width] = s
            top_ref[b, 0:1, :width] = jnp.max(s, axis=0, keepdims=True)

        def finish(h, b):
            p = jnp.exp2((buffers[b][:, :width] - top_ref[b, 0:1, :width]) * (0.25 * LOG2E))
            inverse = 1.0 / jnp.sum(p, axis=0, keepdims=True)
            chances = (p * inverse).astype(bf16)
            rows = pl.ds(pl.multiple_of(h * HDIM, HDIM), HDIM)
            heads_ref[rows, span] = dot(qkv_ref[2, rows, :], chances).astype(bf16)

        scores(0, 0)

        def pair(j, carry):
            h = 2 * j
            scores(h + 1, 1)
            finish(h, 0)
            scores(jnp.minimum(h + 2, HEADS - 1), 0)
            finish(h + 1, 1)
            return carry

        lax.fori_loop(0, HEADS // 2, pair, 0)

    for n, (first, width) in enumerate(parts):
        attention(first, width)
        if n == 0:
            between()
            proj = [w_ref[r, base + 192 : base + 256, :].T for r in range(4)]
        for c in range(first // 256, (first + width) // 256):
            span = slice(c * 256, c * 256 + 256)
            mixed = dot(proj[0], heads_ref[0:64, span])
            for r in range(1, 4):
                mixed = mixed + dot(proj[r], heads_ref[r * 64 : r * 64 + 64, span])
            attended = x_ref[:, span] + (mixed + column(COL_PROJ + block))
            normed = norm_columns(
                attended, column(COL_GAIN + first_norm + 1), column(COL_SHIFT + first_norm + 1)
            ).astype(bf16)
            total = None
            for r in range(4):
                hidden = dot(w_ref[r, base + 256 : base + 512, :], normed) + column(COL_FC1 + 4 * block + r)
                hidden = 0.5 * hidden * (1.0 + lax.erf(hidden * math.sqrt(0.5)))
                part = dot(w_ref[r, base + 512 : base + 768, :], hidden.astype(bf16))
                total = part if total is None else total + part
            emit(c, attended + (total + column(COL_FC2 + block)))


def first_kernel(
    feats_ref, qkv_w_ref, proj_w_ref, fc1_w_ref, fc2_w_ref, gain_ref, shift_ref, qkv_b_ref, proj_b_ref,
    fc1_b_ref, fc2_b_ref, conv_b_ref, cpe_b_ref, conv_w_ref, rank_ref,
    records_ref, cols_ref, send_ref, listed_ref, landing_ref, leave_ref, conv_ref, later_ref,
    x_ref, w_ref, params_ref, conv_own_ref, later_own_ref,
    sem, send_sem, recv_sem, local_sem, send3_sem, recv3_sem, *scratch
):
    group, member = lax.axis_index("order"), lax.axis_index("mp")
    routing, scratch = scratch[:15], scratch[15:]
    barrier, count = greet(order_peers=True, across=True)
    start = pl.multiple_of(member * PATCH, PATCH)
    load = pltpu.make_async_copy(feats_ref.at[:, pl.ds(start, PATCH)], x_ref, sem)
    load.start()

    pad = jnp.zeros((16, C - 64), f32)
    narrow = jnp.concatenate(
        [qkv_b_ref[j, b : b + 1].astype(f32) for b in range(2) for j in range(3)]
        + [conv_b_ref[...].astype(f32), jnp.zeros((9, 64), f32)],
        axis=0,
    )
    narrow = jnp.concatenate([narrow, pad], axis=1)
    wide = jnp.concatenate([jnp.zeros((8, C), f32), fc1_b_ref[...].astype(f32), jnp.zeros((6, C), f32)], axis=0)
    w_ref[member, 0:16, :] = (narrow + wide).astype(bf16)
    for j in range(3):
        w_ref[member, 16 + j * 64 : 80 + j * 64, :] = qkv_w_ref[0, j]

    def weight_copy(part, d):
        rows = (pl.ds(0, 208), pl.ds(208, 576))[part]
        return remote(
            w_ref.at[member, rows], w_ref.at[member, rows], send_sem.at[part, d], recv_sem.at[part, d],
            (group, member ^ d),
        )

    pl.semaphore_wait(barrier, count)
    for d in (2, 3, 1):
        weight_copy(0, d).start()
    route_slots(rank_ref, send_ref, leave_ref, routing)
    w_ref[member, 208:272, :] = proj_w_ref[0]
    w_ref[member, 272:528, :] = fc1_w_ref[0].T
    w_ref[member, 528:784, :] = fc2_w_ref[0].T
    for d in (2, 3, 1):
        weight_copy(1, d).start()

    def turn(k, carry):
        span = pl.ds(pl.multiple_of(k * C, C), C)
        conv_own_ref[:, span] = conv_w_ref[k]
        return carry

    lax.fori_loop(0, OFFS, turn, 0, unroll=3)
    for j in range(3):
        later_own_ref[j * 64 : j * 64 + 64, :] = qkv_w_ref[1, j]
    later_own_ref[192:256, :] = proj_w_ref[1]
    later_own_ref[256:512, :] = fc1_w_ref[1].T
    later_own_ref[512:768, :] = fc2_w_ref[1].T
    later = [
        remote(conv_own_ref, conv_ref.at[1], send3_sem.at[0], recv3_sem.at[0], (group ^ 1, member ^ 2)),
        remote(later_own_ref, later_ref.at[1], send3_sem.at[1], recv3_sem.at[1], (group, member ^ 2)),
        pltpu.make_async_copy(conv_own_ref, conv_ref.at[0], local_sem.at[0]),
        pltpu.make_async_copy(later_own_ref, later_ref.at[0], local_sem.at[1]),
    ]
    for copy in later:
        copy.start()
    load.wait()
    for d in (2, 3, 1):
        weight_copy(0, d).wait()

    params_ref[...] = jnp.zeros_like(params_ref)
    params_ref[COL_GAIN : COL_GAIN + 5, :] = gain_ref[...]
    params_ref[COL_SHIFT : COL_SHIFT + 5, :] = shift_ref[...]
    params_ref[COL_PROJ : COL_PROJ + 2, :] = proj_b_ref[...].astype(f32)
    params_ref[COL_FC2 : COL_FC2 + 2, :] = fc2_b_ref[...].astype(f32)
    bias = [w_ref[r, 0:16, :].astype(f32) for r in range(4)]
    narrow = jnp.concatenate([b[0:8, 0:64] for b in bias], axis=1)
    params_ref[COL_QKV : COL_QKV + 6, :] = narrow[0:6]
    params_ref[COL_CONV : COL_CONV + 1, :] = narrow[6:7]
    for r in range(4):
        for b in range(2):
            params_ref[COL_FC1 + 4 * b + r : COL_FC1 + 4 * b + r + 1, :] = bias[r][8 + b : 9 + b]
    halves = cpe_b_ref[...].astype(f32)
    params_ref[COL_CPE : COL_CPE + 1, :] = jnp.concatenate([halves[0:1], halves[1:2]], axis=1)
    cols_ref[...] = params_ref[...].T

    def emit(c, value):
        rows = value.T
        for half in range(2):
            records_ref[c * 256 : c * 256 + 256, half, :] = rows[:, half * 128 : half * 128 + 128]

    def between():
        route_lists(listed_ref, routing)
        for d in (2, 3, 1):
            weight_copy(1, d).wait()

    run_block(0, 0, x_ref, w_ref, 16, cols_ref, scratch, emit, between)
    route_landing(landing_ref, routing)
    for copy in later:
        copy.wait()


def first_block(*operands):
    return pl.pallas_call(
        first_kernel,
        out_shape=[
            S((PATCH, 2, 128), f32),
            S((C, 128), f32),
            S((ORDERS, 128), i32),
            S((16, 128), i32),
            S((8, 128), i32),
            S((16, 128), i32),
            S((2, 64, OFFS * C), bf16),
            S((2, 768, C), bf16),
        ],
        in_specs=[ANY] + [VMEM] * 14,
        out_specs=[VMEM] * 6 + [ANY] * 2,
        scratch_shapes=[
            pltpu.VMEM((C, PATCH), f32),
            pltpu.VMEM((4, 784, C), bf16),
            pltpu.VMEM((128, C), f32),
            pltpu.VMEM((64, OFFS * C), bf16),
            pltpu.VMEM((768, C), bf16),
            pltpu.SemaphoreType.DMA,
            pltpu.SemaphoreType.DMA((2, 4)),
            pltpu.SemaphoreType.DMA((2, 4)),
            pltpu.SemaphoreType.DMA((2,)),
            pltpu.SemaphoreType.DMA((2,)),
            pltpu.SemaphoreType.DMA((2,)),
        ]
        + route_scratch()
        + block_scratch(),
        compiler_params=kernel_params(collective_id=1, has_side_effects=True),
        name="first_block",
    )(*operands)


def second_kernel(
    records_ref, leave_ref, send_ref, listed_ref, landing_ref, near_ref, conv_ref, cpe_ref, later_ref, cols_ref,
    out_ref,
    leaving_ref, rows_ref, packed_ref, frames_ref, sorted_ref, lists_ref, land_ref, wide_ref,
    x_ref, index_ref, places_ref, hot_ref, picked_ref, conv_w_ref, w_ref,
    sem, local_sem, send_sem, recv_sem, send2_sem, recv2_sem, send3_sem, recv3_sem, send4_sem, recv4_sem,
    send5_sem, recv5_sem, send6_sem, recv6_sem, *scratch
):
    group, member = lax.axis_index("order"), lax.axis_index("mp")
    barrier, count = greet(order_peers=True, halo=True)
    start = pl.multiple_of(member * PATCH, PATCH)
    load = pltpu.make_async_copy(near_ref.at[:, pl.ds(start, PATCH)], index_ref, sem)
    load.start()
    first_token = group * TOK + member * PATCH

    def column(k):
        return cols_ref[:, k : k + 1]

    shares = []
    for i, owner in enumerate((member, member ^ 2)):
        rows = pl.ds(pl.multiple_of(owner * 64, 64), 64)
        shares += [
            pltpu.make_async_copy(conv_ref.at[i], conv_w_ref.at[rows], local_sem.at[i]),
            pltpu.make_async_copy(later_ref.at[i], w_ref.at[owner], local_sem.at[2 + i]),
        ]
    for copy in shares:
        copy.start()
    copies = []
    for d in (2, 3, 1):
        target = member ^ d

        def store(r, record, d=d):
            leaving_ref[d - 1, r] = record

        move_rows(CAP_OUT, lambda r: leave_ref[target * STRIDE + r], records_ref, store)
        if d == 2:
            pl.semaphore_wait(barrier, count)
        copy = remote(
            leaving_ref.at[d - 1], rows_ref.at[pl.ds(member * CAP_OUT, CAP_OUT)], send4_sem.at[d], recv4_sem.at[d],
            (group, target),
        )
        copy.start()
        copies.append(copy)

    def store_staying(r, record):
        rows_ref[member * CAP_OUT + r] = record

    move_rows(CAP_OUT, lambda r: leave_ref[member * STRIDE + r], records_ref, store_staying)
    for copy in copies:
        copy.wait()

    def frame_copy(d):
        return remote(
            packed_ref.at[d], frames_ref.at[pl.ds(pl.multiple_of(group * SLOTS, SLOTS), SLOTS)],
            send_sem.at[d], recv_sem.at[d], (group ^ d, member),
        )

    def pack(t, carry):
        d = 1 + (t + 8 * member + 7 * group) % (ORDERS - 1)
        target = group ^ d

        def store(r, record):
            packed_ref[d, r] = record

        move_rows(SLOTS, lambda r: send_ref[target * 128 + r], rows_ref, store)
        frame_copy(d).start()
        return carry

    lax.fori_loop(0, ORDERS - 1, pack, 0)

    def store_own(r, record):
        frames_ref[group * SLOTS + r] = record

    move_rows(SLOTS, lambda r: send_ref[group * 128 + r], rows_ref, store_own)

    for i, owner in enumerate((member, member ^ 2)):
        rows = pl.ds(pl.multiple_of(owner * 64, 64), 64)
        crossing = [
            remote(conv_ref.at[i], conv_w_ref.at[rows], send5_sem.at[i], recv5_sem.at[i], (group, member ^ 1)),
            remote(later_ref.at[i], w_ref.at[owner], send5_sem.at[2 + i], recv5_sem.at[2 + i], (group, member ^ 1)),
        ]
        for copy in crossing:
            copy.start()
        shares += crossing
    load.wait()
    near = index_ref[...]
    near = jnp.where(near < 0, -1, near - (first_token - HALO))
    places_ref[...] = jnp.concatenate([near, jnp.full((128 - OFFS, PATCH), -1, i32)], axis=0).T

    def frame_wait(d, carry):
        frame_copy(d).wait()
        return carry

    lax.fori_loop(1, ORDERS, frame_wait, 0)

    copies = []
    for d in (2, 3, 1):
        target = member ^ d

        def store(r, record, d=d):
            sorted_ref[d - 1, r] = record

        move_rows(CAP, lambda r: listed_ref[target * STRIDE + r], frames_ref, store)
        copy = remote(
            sorted_ref.at[d - 1], lists_ref.at[pl.ds(member * CAP, CAP)], send2_sem.at[d], recv2_sem.at[d],
            (group, target),
        )
        copy.start()
        copies.append(copy)

    def store_mine(r, record):
        lists_ref[member * CAP + r] = record

    move_rows(CAP, lambda r: listed_ref[member * STRIDE + r], frames_ref, store_mine)
    for copy in copies:
        copy.wait()

    def land(start, rows):
        def store(r, record):
            land_ref[start + r] = record

        move_rows(rows, lambda r: landing_ref[start + r], lists_ref, store)
        for half in range(2):
            part = land_ref[start : start + rows, half, :]
            at = slice(half * 128, half * 128 + 128)
            x_ref[at, start : start + rows] = part.T
            wide_ref[HALO + start : HALO + start + rows, at] = part.astype(bf16)

    land(0, HALO)
    land(PATCH - HALO, HALO)
    halos = [
        remote(
            wide_ref.at[HALO : 2 * HALO], wide_ref.at[HALO + PATCH : 2 * HALO + PATCH],
            send3_sem.at[0], recv3_sem.at[0], neighbour(127),
        ),
        remote(
            wide_ref.at[PATCH : PATCH + HALO], wide_ref.at[0:HALO],
            send3_sem.at[1], recv3_sem.at[1], neighbour(1),
        ),
    ]
    for copy in halos:
        copy.start()
    for c in range(3):
        land(HALO + c * 256, 256)
    for copy in halos:
        copy.wait()

    lanes = iota((256, 512), 1)
    for c in range(4):
        window = wide_ref[c * 256 : c * 256 + 512, :]
        places = places_ref[c * 256 : c * 256 + 256, :] - c * 256
        for b in range(OFFS // 3):
            for k in range(3):
                hot_ref[b % 2, k * 256 : k * 256 + 256, :] = one_hot(lanes, places[:, 3 * b + k : 3 * b + k + 1])
            picked = dot(hot_ref[b % 2], window).astype(bf16)
            for k in range(3):
                at = (3 * b + k) * C
                picked_ref[c * 256 : c * 256 + 256, at : at + C] = picked[k * 256 : k * 256 + 256]
    for copy in shares:
        copy.wait()
    summed = dot_rows(picked_ref[...], conv_w_ref[...]).T
    conv = (summed + column(COL_CONV)).astype(bf16)
    cpe = cpe_ref[...].T
    for c in range(4):
        span = slice(c * 256, c * 256 + 256)
        mixture = dot(cpe, conv[:, span]) + column(COL_CPE)
        x_ref[:, span] = x_ref[:, span] + norm_columns(
            mixture, column(COL_GAIN + 2), column(COL_SHIFT + 2)
        )

    copies = []

    def emit(c, value):
        span = slice(c * 256, c * 256 + 256)
        place = pl.ds(pl.multiple_of(member * PATCH + c * 256, 256), 256)
        x_ref[:, span] = value
        for d in (2, 3, 1):
            target = member ^ d
            copy = remote(
                x_ref.at[pl.ds(pl.multiple_of(target * 64, 64), 64), span], out_ref.at[:, place],
                send6_sem.at[c, d], recv6_sem.at[c, d], (group, target),
            )
            copy.start()
            copies.append(copy)
        out_ref[:, place] = x_ref[pl.ds(pl.multiple_of(member * 64, 64), 64), span]

    run_block(1, 3, x_ref, w_ref, 0, cols_ref, scratch, emit, lambda: None, ((0, 768), (768, 256)))
    for copy in copies:
        copy.wait()


def second_block(*operands):
    pairs = [pltpu.SemaphoreType.DMA((ORDERS,))] * 2 + [pltpu.SemaphoreType.DMA((4,))] * 2
    pairs += [pltpu.SemaphoreType.DMA((2,))] * 2 + [pltpu.SemaphoreType.DMA((4,))] * 4
    pairs += [pltpu.SemaphoreType.DMA((4, 4))] * 2
    return pl.pallas_call(
        second_kernel,
        out_shape=S((64, TOK), f32),
        in_specs=[VMEM, SMEM, SMEM, SMEM, SMEM, ANY, ANY, VMEM, ANY, VMEM],
        out_specs=VMEM,
        scratch_shapes=[
            pltpu.VMEM((3, CAP_OUT, 2, 128), f32),
            pltpu.VMEM((4 * CAP_OUT, 2, 128), f32),
            pltpu.VMEM((ORDERS, SLOTS, 2, 128), f32),
            pltpu.VMEM((ORDERS * SLOTS, 2, 128), f32),
            pltpu.VMEM((3, CAP, 2, 128), f32),
            pltpu.VMEM((4 * CAP, 2, 128), f32),
            pltpu.VMEM((PATCH, 2, 128), f32),
            pltpu.VMEM((PATCH + 2 * HALO, C), bf16),
            pltpu.VMEM((C, PATCH), f32),
            pltpu.VMEM((OFFS, PATCH), i32),
            pltpu.VMEM((PATCH, 128), i32),
            pltpu.VMEM((2, 3 * 256, 512), bf16),
            pltpu.VMEM((PATCH, OFFS * C), bf16),
            pltpu.VMEM((C, OFFS * C), bf16),
            pltpu.VMEM((4, 768, C), bf16),
            pltpu.SemaphoreType.DMA,
            pltpu.SemaphoreType.DMA((4,)),
        ]
        + pairs
        + block_scratch(),
        compiler_params=kernel_params(collective_id=2, has_side_effects=True),
        name="second_block",
    )(*operands)


def shards(
    feats, serial_rank, neighbours, norm_gain, norm_bias, qkv_weight, qkv_bias, proj_weight, proj_bias,
    fc1_weight, fc1_bias, fc2_weight, fc2_bias, conv_weight, conv_bias, cpe_weight, cpe_bias,
):
    records, cols, send, listed, landing, leave, conv, later = first_block(
        feats, qkv_weight.transpose(0, 1, 3, 2), proj_weight, fc1_weight, fc2_weight, norm_gain, norm_bias,
        qkv_bias.transpose(1, 0, 2), proj_bias, fc1_bias, fc2_bias, conv_bias.reshape(1, 64),
        cpe_bias.reshape(2, 128), conv_weight.transpose(0, 2, 1),
        serial_rank.reshape(32, 128),
    )
    return second_block(
        records, leave.reshape(-1), send.reshape(-1), listed.reshape(-1), landing.reshape(-1), neighbours, conv,
        cpe_weight, later, cols,
    )


def solution(mesh):
    in_specs = (
        P(None, "order"),
        P("order"),
        P(None, "order"),
        P(),
        P(),
        P(None, None, None, "mp"),
        P(None, None, "mp"),
        P(None, "mp", None),
        P(),
        P(None, None, "mp"),
        P(None, "mp"),
        P(None, "mp", None),
        P(),
        P(None, None, "mp"),
        P("mp"),
        P(),
        P(),
    )
    return jax.shard_map(shards, mesh=mesh, in_specs=in_specs, out_specs=P("mp", "order"), check_vma=False)
```

```python
import functools
import math

import jax
import jax.numpy as jnp
from jax import lax
from jax.experimental import pallas as pl
from jax.experimental.pallas import tpu as pltpu
from jax.sharding import PartitionSpec as P

C = 256
PATCH = 1024
HALO = 128
HDIM = 16
HEADS = 16
OFFS = 27
TOK = 4096
SLOTS = 64
CAP = 288
CAP_OUT = 352
STRIDE = 384
ORDERS = 32
MESH = pl.DeviceIdType.MESH
EPS = 1e-05
LOG2E = math.log2(math.e)
f32, bf16, i32 = jnp.float32, jnp.bfloat16, jnp.int32
VMEM = pl.BlockSpec(memory_space=pltpu.VMEM)
SMEM = pl.BlockSpec(memory_space=pltpu.SMEM)
ANY = pl.BlockSpec(memory_space=pl.ANY)
S = jax.ShapeDtypeStruct
COL_GAIN, COL_SHIFT, COL_PROJ, COL_FC2, COL_QKV, COL_FC1, COL_CONV, COL_CPE = 0, 5, 10, 12, 14, 20, 28, 29


def kernel_params(**more):
    return pltpu.CompilerParams(vmem_limit_bytes=61 * 2**20, **more)


def iota(shape, dim):
    return lax.broadcasted_iota(i32, shape, dim)


def one_hot(left, right):
    return jnp.where(left == right, 1.0, 0.0).astype(bf16)


def dot_rows(left, right):
    return lax.dot_general(left, right, (((1,), (1,)), ((), ())), preferred_element_type=f32)


def dot(left, right):
    return jnp.dot(left, right, preferred_element_type=f32)


def norm_columns(values, gain, shift):
    average = jnp.mean(values, axis=0, keepdims=True)
    centred = values - average
    variance = jnp.mean(centred * centred, axis=0, keepdims=True)
    return centred * lax.rsqrt(variance + EPS) * gain + shift


def greet(order_peers=False, halo=False, across=False):
    barrier = pltpu.get_barrier_semaphore()
    group, member = lax.axis_index("order"), lax.axis_index("mp")
    for d in range(1, 4):
        pl.semaphore_signal(barrier, inc=1, device_id=(group, member ^ d), device_id_type=MESH)
    count = 3
    if order_peers:

        def step(d, carry):
            pl.semaphore_signal(barrier, inc=1, device_id=(group ^ d, member), device_id_type=MESH)
            return carry

        lax.fori_loop(1, ORDERS, step, 0)
        count += ORDERS - 1
    if across:
        pl.semaphore_signal(barrier, inc=1, device_id=(group ^ 1, member ^ 2), device_id_type=MESH)
        count += 1
    if halo:
        for shift in (1, 127):
            pl.semaphore_signal(barrier, inc=1, device_id=neighbour(shift), device_id_type=MESH)
        count += 2
    return barrier, count


def neighbour(shift):
    place = (lax.axis_index("order") * 4 + lax.axis_index("mp") + shift) % 128
    return (place // 4, place % 4)


def remote(src, dst, send, recv, device):
    return pltpu.make_async_remote_copy(
        src_ref=src, dst_ref=dst, send_sem=send, recv_sem=recv, device_id=device, device_id_type=MESH
    )


def in_rows(lists):
    rows = [lists[q : q + 1, k * 128 : k * 128 + 128] for q in range(4) for k in range(STRIDE // 128)]
    return jnp.concatenate(rows + [jnp.zeros((4, 128), i32)], axis=0)


def prefix_matrix():
    upper = jnp.where(iota((128, 128), 0) < iota((128, 128), 1), 1.0, 0.0).astype(bf16)
    return jnp.concatenate([upper, jnp.ones((128, 128), bf16)], axis=1)


def route_slots(rank_ref, send_ref, leave_ref, scratch):
    (made_ref, slot_ref, spot_ref, left_ref, right_ref, left2_ref, right2_ref, pos_out, pos_in) = scratch[:9]
    group, member = lax.axis_index("order"), lax.axis_index("mp")
    both = prefix_matrix()
    lane = iota((1, 128), 1)

    def classes(c):
        return jnp.where(iota((128, 128), 0) == rank_ref[pl.ds(c, 1), :] // PATCH, 1.0, 0.0)

    def count_classes(c, total):
        made = dot(classes(c).astype(bf16), both)
        made_ref[c] = made
        return total + made[:, 128:]

    total = lax.fori_loop(0, 32, count_classes, jnp.zeros((128, 128), f32), unroll=8)
    row, col = iota((128, 128), 0), iota((128, 128), 1)
    ahead = jnp.where((row // 4 == col // 4) & (col < row), 1.0, 0.0).astype(bf16)

    def number(c, carry):
        made = made_ref[c]
        slot = jnp.sum(classes(c) * (made[:, :128] + carry), axis=0, keepdims=True)
        slot_ref[pl.ds(c, 1), :] = slot.astype(i32)
        return carry + made[:, 128:]

    lax.fori_loop(0, 32, number, dot(ahead, total.astype(bf16)), unroll=4)

    slots = slot_ref[...]
    hot = jnp.where(iota((32, 8, 128), 1) == (slots % 4)[:, None, :], 1.0, 0.0).reshape(256, 128)
    made = dot(hot.astype(bf16), both)
    row, col = iota((256, 256), 0), iota((256, 256), 1)
    earlier = (row % 8 == col % 8) & (row // 64 == col // 64) & (col < row)
    carry = dot(jnp.where(earlier, 1.0, 0.0).astype(bf16), made[:, 128:].astype(bf16))
    spot_ref[...] = jnp.sum((hot * (made[:, :128] + carry)).reshape(32, 8, 128), axis=1).astype(i32)

    def frames(c, carry):
        span = pl.ds(pl.multiple_of(c * 128, 128), 128)
        rank_row, spot_row = rank_ref[pl.ds(c, 1), :], spot_ref[pl.ds(c, 1), :]
        owner = jnp.where(iota((32, 128), 0) == rank_row // TOK, 1.0, 0.0)
        entry = (c // 8) * CAP_OUT + spot_row
        inside = rank_row % TOK
        pieces = [entry // 64, entry % 64, inside // 64, inside % 64]
        left = jnp.concatenate([owner * p.astype(f32) for p in pieces] + [owner], axis=0)
        left_ref[:, span] = left.astype(bf16)
        right_ref[:, span] = one_hot(iota((SLOTS, 128), 0) * 4 + member, slot_ref[pl.ds(c, 1), :])
        return carry

    lax.fori_loop(0, 32, frames, 0, unroll=2)
    acc = dot_rows(left_ref[...], right_ref[...])
    send = (acc[0:32] * 64.0 + acc[32:64]).astype(i32)
    send_ref[...] = jnp.concatenate([send, jnp.zeros((32, 128 - SLOTS), i32)], axis=1)
    inside = jnp.where(acc[128:160] > 0.5, (acc[64:96] * 64.0 + acc[96:128]).astype(i32), TOK)
    unused = jnp.full((32, SLOTS), TOK, i32)
    inside = jnp.where(
        group % 2 == 0,
        jnp.concatenate([inside, unused], axis=1),
        jnp.concatenate([unused, inside], axis=1),
    )
    pos_out[...] = jnp.broadcast_to(inside[:, None, :], (32, 8, 128))
    pos_in[group] = pos_out[group]

    def frame_start(d, carry):
        place_frame_copy(scratch, d).start()
        return carry

    lax.fori_loop(1, ORDERS, frame_start, 0)

    def leaving(c, carry):
        span = pl.ds(pl.multiple_of(c * 128, 128), 128)
        at = pl.ds(member * 8 + c, 1)
        hot = jnp.where(iota((8, 128), 0) == slot_ref[at, :] % 4, 1.0, 0.0)
        token = c * 128 + lane
        left = jnp.concatenate([hot * (token // 64).astype(f32), hot * (token % 64).astype(f32)], axis=0)
        left2_ref[:, span] = left.astype(bf16)
        right2_ref[:, span] = one_hot(iota((CAP_OUT, 128), 0), spot_ref[at, :])
        return carry

    lax.fori_loop(0, 8, leaving, 0)
    acc = dot_rows(left2_ref[...], right2_ref[...])
    leave = (acc[0:4] * 64.0 + acc[8:12]).astype(i32)
    leave_ref[...] = in_rows(jnp.concatenate([leave, jnp.zeros((4, STRIDE - CAP_OUT), i32)], axis=1))


def route_lists(listed_ref, scratch):
    _, slot_ref, spot_ref, _, _, _, _, _, pos_in, place_out, place_in = scratch[:11]
    group, member = lax.axis_index("order"), lax.axis_index("mp")
    both = prefix_matrix()
    lane = iota((1, 128), 1)

    def frame_wait(d, carry):
        place_frame_copy(scratch, d).wait()
        return carry

    lax.fori_loop(1, ORDERS, frame_wait, 0)
    row, col = iota((128, 128), 0), iota((128, 128), 1)
    pos = jnp.min(pos_in[:, 0, :].reshape(16, 2, 128), axis=1)
    hot = jnp.where(iota((16, 8, 128), 1) == (pos // PATCH)[:, None, :], 1.0, 0.0).reshape(128, 128)
    made = dot(hot.astype(bf16), both)
    earlier = (row % 8 == col % 8) & (col < row)
    carry = dot(jnp.where(earlier, 1.0, 0.0).astype(bf16), made[:, 128:].astype(bf16))
    spot_ref[0:16, :] = jnp.sum((hot * (made[:, :128] + carry)).reshape(16, 8, 128), axis=1).astype(i32)
    slot_ref[0:16, :] = pos

    def lists(c, acc):
        inside = slot_ref[pl.ds(c, 1), :]
        hot = jnp.where(iota((8, 128), 0) == inside // PATCH, 1.0, 0.0)
        inside = inside % PATCH
        pieces = [2 * c + lane // SLOTS, lane % SLOTS, inside // 32, inside % 32]
        left = jnp.concatenate([hot * p.astype(f32) for p in pieces] + [hot], axis=0)
        right = one_hot(iota((384, 128), 0), spot_ref[pl.ds(c, 1), :])
        return acc + dot_rows(left.astype(bf16), right)

    acc = lax.fori_loop(0, 16, lists, jnp.zeros((40, 384), f32), unroll=8)
    listed_ref[...] = in_rows((acc[0:4] * float(SLOTS) + acc[8:12]).astype(i32))
    place = jnp.where(acc[32:36] > 0.5, (acc[16:20] * 32.0 + acc[24:28]).astype(i32), -1)
    place_out[...] = jnp.broadcast_to(place[:, None, :], (4, 8, 384))
    place_in[member] = place_out[member]
    for d in range(1, 4):
        place_list_copy(scratch, d).start()


def route_landing(landing_ref, scratch):
    place_in = scratch[10]
    for d in range(1, 4):
        place_list_copy(scratch, d).wait()
    acc = jnp.zeros((8, PATCH), f32)
    entry = iota((1, 384), 1)
    kind = iota((8, 384), 0)
    for q in range(4):
        right = one_hot(iota((PATCH, 384), 0), place_in[q, 0:1, :])
        at = q * CAP + entry
        left = jnp.where(kind == 0, at // 64, jnp.where(kind == 1, at % 64, 0))
        acc = acc + dot_rows(left.astype(f32).astype(bf16), right)
    landing = (acc[0:1] * 64.0 + acc[1:2]).astype(i32)
    landing_ref[...] = jnp.concatenate([landing[:, k * 128 : k * 128 + 128] for k in range(8)], axis=0)


def place_frame_copy(scratch, d):
    group, member = lax.axis_index("order"), lax.axis_index("mp")
    pos_out, pos_in, send_sem, recv_sem = scratch[7], scratch[8], scratch[11], scratch[12]
    return remote(
        pos_out.at[group ^ d], pos_in.at[group], send_sem.at[d], recv_sem.at[d], (group ^ d, member)
    )


def place_list_copy(scratch, d):
    group, member = lax.axis_index("order"), lax.axis_index("mp")
    place_out, place_in, send_sem, recv_sem = scratch[9], scratch[10], scratch[13], scratch[14]
    return remote(
        place_out.at[member ^ d], place_in.at[member], send_sem.at[d], recv_sem.at[d], (group, member ^ d)
    )


def route_scratch():
    return [
        pltpu.VMEM((32, 128, 256), f32),
        pltpu.VMEM((32, 128), i32),
        pltpu.VMEM((32, 128), i32),
        pltpu.VMEM((160, TOK), bf16),
        pltpu.VMEM((SLOTS, TOK), bf16),
        pltpu.VMEM((16, PATCH), bf16),
        pltpu.VMEM((CAP_OUT, PATCH), bf16),
        pltpu.VMEM((32, 8, 128), i32),
        pltpu.VMEM((32, 8, 128), i32),
        pltpu.VMEM((4, 8, 384), i32),
        pltpu.VMEM((4, 8, 384), i32),
        pltpu.SemaphoreType.DMA((ORDERS,)),
        pltpu.SemaphoreType.DMA((ORDERS,)),
        pltpu.SemaphoreType.DMA((4,)),
        pltpu.SemaphoreType.DMA((4,)),
    ]


def move_rows(count, index, source, store):
    def step(i, carry):
        records = [source[index(i * 32 + u)] for u in range(32)]
        for u in range(32):
            store(i * 32 + u, records[u])
        return carry

    lax.fori_loop(0, count // 32, step, 0)


def block_scratch():
    return [
        pltpu.VMEM((C, PATCH), bf16),
        pltpu.VMEM((3, C, PATCH), bf16),
        pltpu.VMEM((2, PATCH, 128), bf16),
        pltpu.VMEM((PATCH, PATCH), f32),
        pltpu.VMEM((PATCH, PATCH), f32),
        pltpu.VMEM((2, 8, PATCH), f32),
        pltpu.VMEM((C, PATCH), bf16),
    ]


def run_block(block, first_norm, x_ref, w_ref, base, cols_ref, scratch, emit, between, parts=((0, 1024),)):
    normed_ref, qkv_ref, keys_ref, s0_ref, s1_ref, top_ref, heads_ref = scratch

    def column(k):
        return cols_ref[:, k : k + 1]

    for c in range(4):
        span = slice(c * 256, c * 256 + 256)
        normed_ref[:, span] = norm_columns(
            x_ref[:, span], column(COL_GAIN + first_norm), column(COL_SHIFT + first_norm)
        ).astype(bf16)
    for r in range(4):
        made = dot(w_ref[r, base : base + 192, :], normed_ref[...])
        for j in range(3):
            bias = cols_ref[r * 64 : r * 64 + 64, COL_QKV + 3 * block + j : COL_QKV + 3 * block + j + 1]
            qkv_ref[j, r * 64 : r * 64 + 64, :] = (made[j * 64 : j * 64 + 64] + bias).astype(bf16)
    for g in range(2):
        keys_ref[g] = qkv_ref[1, g * 128 : g * 128 + 128, :].T

    head_of_row = iota((128, 1), 0) // HDIM
    buffers = (s0_ref, s1_ref)

    def attention(first, width):
        span = slice(first, first + width)

        def scores(h, b):
            g = h // 8
            queries = qkv_ref[0, pl.ds(pl.multiple_of(g * 128, 128), 128), span]
            queries = jnp.where(head_of_row == h % 8, queries.astype(f32), 0.0).astype(bf16)
            s = dot(keys_ref[g], queries)
            buffers[b][:, :width] = s
            top_ref[b, 0:1, :width] = jnp.max(s, axis=0, keepdims=True)

        def finish(h, b):
            p = jnp.exp2((buffers[b][:, :width] - top_ref[b, 0:1, :width]) * (0.25 * LOG2E))
            inverse = 1.0 / jnp.sum(p, axis=0, keepdims=True)
            chances = (p * inverse).astype(bf16)
            rows = pl.ds(pl.multiple_of(h * HDIM, HDIM), HDIM)
            heads_ref[rows, span] = dot(qkv_ref[2, rows, :], chances).astype(bf16)

        scores(0, 0)

        def pair(j, carry):
            h = 2 * j
            scores(h + 1, 1)
            finish(h, 0)
            scores(jnp.minimum(h + 2, HEADS - 1), 0)
            finish(h + 1, 1)
            return carry

        lax.fori_loop(0, HEADS // 2, pair, 0)

    for n, (first, width) in enumerate(parts):
        attention(first, width)
        if n == 0:
            between()
            proj = [w_ref[r, base + 192 : base + 256, :].T for r in range(4)]
        for c in range(first // 256, (first + width) // 256):
            span = slice(c * 256, c * 256 + 256)
            mixed = dot(proj[0], heads_ref[0:64, span])
            for r in range(1, 4):
                mixed = mixed + dot(proj[r], heads_ref[r * 64 : r * 64 + 64, span])
            attended = x_ref[:, span] + (mixed + column(COL_PROJ + block))
            normed = norm_columns(
                attended, column(COL_GAIN + first_norm + 1), column(COL_SHIFT + first_norm + 1)
            ).astype(bf16)
            total = None
            for r in range(4):
                hidden = dot(w_ref[r, base + 256 : base + 512, :], normed) + column(COL_FC1 + 4 * block + r)
                hidden = 0.5 * hidden * (1.0 + lax.erf(hidden * math.sqrt(0.5)))
                part = dot(w_ref[r, base + 512 : base + 768, :], hidden.astype(bf16))
                total = part if total is None else total + part
            emit(c, attended + (total + column(COL_FC2 + block)))


def first_kernel(
    feats_ref, qkv_w_ref, proj_w_ref, fc1_w_ref, fc2_w_ref, gain_ref, shift_ref, qkv_b_ref, proj_b_ref,
    fc1_b_ref, fc2_b_ref, conv_b_ref, cpe_b_ref, conv_w_ref, rank_ref,
    records_ref, cols_ref, send_ref, listed_ref, landing_ref, leave_ref, conv_ref, later_ref,
    x_ref, w_ref, params_ref, conv_own_ref, later_own_ref,
    sem, send_sem, recv_sem, local_sem, send3_sem, recv3_sem, *scratch
):
    group, member = lax.axis_index("order"), lax.axis_index("mp")
    routing, scratch = scratch[:15], scratch[15:]
    barrier, count = greet(order_peers=True, across=True)
    start = pl.multiple_of(member * PATCH, PATCH)
    load = pltpu.make_async_copy(feats_ref.at[:, pl.ds(start, PATCH)], x_ref, sem)
    load.start()

    pad = jnp.zeros((16, C - 64), f32)
    narrow = jnp.concatenate(
        [qkv_b_ref[j, b : b + 1].astype(f32) for b in range(2) for j in range(3)]
        + [conv_b_ref[...].astype(f32), jnp.zeros((9, 64), f32)],
        axis=0,
    )
    narrow = jnp.concatenate([narrow, pad], axis=1)
    wide = jnp.concatenate([jnp.zeros((8, C), f32), fc1_b_ref[...].astype(f32), jnp.zeros((6, C), f32)], axis=0)
    w_ref[member, 0:16, :] = (narrow + wide).astype(bf16)
    for j in range(3):
        w_ref[member, 16 + j * 64 : 80 + j * 64, :] = qkv_w_ref[0, j]

    def weight_copy(part, d):
        rows = (pl.ds(0, 208), pl.ds(208, 576))[part]
        return remote(
            w_ref.at[member, rows], w_ref.at[member, rows], send_sem.at[part, d], recv_sem.at[part, d],
            (group, member ^ d),
        )

    pl.semaphore_wait(barrier, count)
    for d in (2, 3, 1):
        weight_copy(0, d).start()
    route_slots(rank_ref, send_ref, leave_ref, routing)
    w_ref[member, 208:272, :] = proj_w_ref[0]
    w_ref[member, 272:528, :] = fc1_w_ref[0].T
    w_ref[member, 528:784, :] = fc2_w_ref[0].T
    for d in (2, 3, 1):
        weight_copy(1, d).start()

    def turn(k, carry):
        span = pl.ds(pl.multiple_of(k * C, C), C)
        conv_own_ref[:, span] = conv_w_ref[k]
        return carry

    lax.fori_loop(0, OFFS, turn, 0, unroll=3)
    for j in range(3):
        later_own_ref[j * 64 : j * 64 + 64, :] = qkv_w_ref[1, j]
    later_own_ref[192:256, :] = proj_w_ref[1]
    later_own_ref[256:512, :] = fc1_w_ref[1].T
    later_own_ref[512:768, :] = fc2_w_ref[1].T
    later = [
        remote(conv_own_ref, conv_ref.at[1], send3_sem.at[0], recv3_sem.at[0], (group ^ 1, member ^ 2)),
        remote(later_own_ref, later_ref.at[1], send3_sem.at[1], recv3_sem.at[1], (group, member ^ 2)),
        pltpu.make_async_copy(conv_own_ref, conv_ref.at[0], local_sem.at[0]),
        pltpu.make_async_copy(later_own_ref, later_ref.at[0], local_sem.at[1]),
    ]
    for copy in later:
        copy.start()
    load.wait()
    for d in (2, 3, 1):
        weight_copy(0, d).wait()

    params_ref[...] = jnp.zeros_like(params_ref)
    params_ref[COL_GAIN : COL_GAIN + 5, :] = gain_ref[...]
    params_ref[COL_SHIFT : COL_SHIFT + 5, :] = shift_ref[...]
    params_ref[COL_PROJ : COL_PROJ + 2, :] = proj_b_ref[...].astype(f32)
    params_ref[COL_FC2 : COL_FC2 + 2, :] = fc2_b_ref[...].astype(f32)
    bias = [w_ref[r, 0:16, :].astype(f32) for r in range(4)]
    narrow = jnp.concatenate([b[0:8, 0:64] for b in bias], axis=1)
    params_ref[COL_QKV : COL_QKV + 6, :] = narrow[0:6]
    params_ref[COL_CONV : COL_CONV + 1, :] = narrow[6:7]
    for r in range(4):
        for b in range(2):
            params_ref[COL_FC1 + 4 * b + r : COL_FC1 + 4 * b + r + 1, :] = bias[r][8 + b : 9 + b]
    halves = cpe_b_ref[...].astype(f32)
    params_ref[COL_CPE : COL_CPE + 1, :] = jnp.concatenate([halves[0:1], halves[1:2]], axis=1)
    cols_ref[...] = params_ref[...].T

    def emit(c, value):
        rows = value.T
        for half in range(2):
            records_ref[c * 256 : c * 256 + 256, half, :] = rows[:, half * 128 : half * 128 + 128]

    def between():
        route_lists(listed_ref, routing)
        for d in (2, 3, 1):
            weight_copy(1, d).wait()

    run_block(0, 0, x_ref, w_ref, 16, cols_ref, scratch, emit, between)
    route_landing(landing_ref, routing)
    for copy in later:
        copy.wait()


def first_block(*operands):
    return pl.pallas_call(
        first_kernel,
        out_shape=[
            S((PATCH, 2, 128), f32),
            S((C, 128), f32),
            S((ORDERS, 128), i32),
            S((16, 128), i32),
            S((8, 128), i32),
            S((16, 128), i32),
            S((2, 64, OFFS * C), bf16),
            S((2, 768, C), bf16),
        ],
        in_specs=[ANY] + [VMEM] * 14,
        out_specs=[VMEM] * 6 + [ANY] * 2,
        scratch_shapes=[
            pltpu.VMEM((C, PATCH), f32),
            pltpu.VMEM((4, 784, C), bf16),
            pltpu.VMEM((128, C), f32),
            pltpu.VMEM((64, OFFS * C), bf16),
            pltpu.VMEM((768, C), bf16),
            pltpu.SemaphoreType.DMA,
            pltpu.SemaphoreType.DMA((2, 4)),
            pltpu.SemaphoreType.DMA((2, 4)),
            pltpu.SemaphoreType.DMA((2,)),
            pltpu.SemaphoreType.DMA((2,)),
            pltpu.SemaphoreType.DMA((2,)),
        ]
        + route_scratch()
        + block_scratch(),
        compiler_params=kernel_params(collective_id=1, has_side_effects=True),
        name="first_block",
    )(*operands)


def second_kernel(
    records_ref, leave_ref, send_ref, listed_ref, landing_ref, near_ref, conv_ref, cpe_ref, later_ref, cols_ref,
    out_ref,
    leaving_ref, rows_ref, packed_ref, frames_ref, sorted_ref, lists_ref, land_ref, wide_ref,
    x_ref, index_ref, places_ref, hot_ref, picked_ref, conv_w_ref, w_ref,
    sem, local_sem, send_sem, recv_sem, send2_sem, recv2_sem, send3_sem, recv3_sem, send4_sem, recv4_sem,
    send5_sem, recv5_sem, send6_sem, recv6_sem, *scratch
):
    group, member = lax.axis_index("order"), lax.axis_index("mp")
    barrier, count = greet(order_peers=True, halo=True)
    start = pl.multiple_of(member * PATCH, PATCH)
    load = pltpu.make_async_copy(near_ref.at[:, pl.ds(start, PATCH)], index_ref, sem)
    load.start()
    first_token = group * TOK + member * PATCH

    def column(k):
        return cols_ref[:, k : k + 1]

    shares = []
    for i, owner in enumerate((member, member ^ 2)):
        rows = pl.ds(pl.multiple_of(owner * 64, 64), 64)
        shares += [
            pltpu.make_async_copy(conv_ref.at[i], conv_w_ref.at[rows], local_sem.at[i]),
            pltpu.make_async_copy(later_ref.at[i], w_ref.at[owner], local_sem.at[2 + i]),
        ]
    for copy in shares:
        copy.start()
    copies = []
    for d in (2, 3, 1):
        target = member ^ d

        def store(r, record, d=d):
            leaving_ref[d - 1, r] = record

        for n, (start, rows) in enumerate(((0, 160), (160, 192)) if d == 2 else ((0, CAP_OUT),)):
            move_rows(
                rows, lambda r: leave_ref[target * STRIDE + start + r], records_ref,
                lambda r, record: store(start + r, record),
            )
            if d == 2 and n == 0:
                pl.semaphore_wait(barrier, count)
            copy = remote(
                leaving_ref.at[d - 1, pl.ds(start, rows)], rows_ref.at[pl.ds(member * CAP_OUT + start, rows)],
                send4_sem.at[d - 2 * n], recv4_sem.at[d - 2 * n], (group, target),
            )
            copy.start()
            copies.append(copy)

    def store_staying(r, record):
        rows_ref[member * CAP_OUT + r] = record

    move_rows(CAP_OUT, lambda r: leave_ref[member * STRIDE + r], records_ref, store_staying)
    for copy in copies:
        copy.wait()

    def frame_copy(d):
        return remote(
            packed_ref.at[d], frames_ref.at[pl.ds(pl.multiple_of(group * SLOTS, SLOTS), SLOTS)],
            send_sem.at[d], recv_sem.at[d], (group ^ d, member),
        )

    def pack(t, carry):
        d = 1 + (t + 8 * member + 7 * group) % (ORDERS - 1)
        target = group ^ d

        def store(r, record):
            packed_ref[d, r] = record

        move_rows(SLOTS, lambda r: send_ref[target * 128 + r], rows_ref, store)
        frame_copy(d).start()
        return carry

    lax.fori_loop(0, ORDERS - 1, pack, 0)

    def store_own(r, record):
        frames_ref[group * SLOTS + r] = record

    move_rows(SLOTS, lambda r: send_ref[group * 128 + r], rows_ref, store_own)

    for i, owner in enumerate((member, member ^ 2)):
        rows = pl.ds(pl.multiple_of(owner * 64, 64), 64)
        crossing = [
            remote(conv_ref.at[i], conv_w_ref.at[rows], send5_sem.at[i], recv5_sem.at[i], (group, member ^ 1)),
            remote(later_ref.at[i], w_ref.at[owner], send5_sem.at[2 + i], recv5_sem.at[2 + i], (group, member ^ 1)),
        ]
        for copy in crossing:
            copy.start()
        shares += crossing
    load.wait()
    near = index_ref[...]
    near = jnp.where(near < 0, -1, near - (first_token - HALO))
    places_ref[...] = jnp.concatenate([near, jnp.full((128 - OFFS, PATCH), -1, i32)], axis=0).T

    def frame_wait(d, carry):
        frame_copy(d).wait()
        return carry

    lax.fori_loop(1, ORDERS, frame_wait, 0)

    copies = []
    for d in (2, 3, 1):
        target = member ^ d

        def store(r, record, d=d):
            sorted_ref[d - 1, r] = record

        for n, (start, rows) in enumerate(((0, 128), (128, 160)) if d == 2 else ((0, CAP),)):
            move_rows(
                rows, lambda r: listed_ref[target * STRIDE + start + r], frames_ref,
                lambda r, record: store(start + r, record),
            )
            copy = remote(
                sorted_ref.at[d - 1, pl.ds(start, rows)], lists_ref.at[pl.ds(member * CAP + start, rows)],
                send2_sem.at[d - 2 * n], recv2_sem.at[d - 2 * n], (group, target),
            )
            copy.start()
            copies.append(copy)

    def store_mine(r, record):
        lists_ref[member * CAP + r] = record

    move_rows(CAP, lambda r: listed_ref[member * STRIDE + r], frames_ref, store_mine)
    for copy in copies:
        copy.wait()

    def land(start, rows):
        def store(r, record):
            land_ref[start + r] = record

        move_rows(rows, lambda r: landing_ref[start + r], lists_ref, store)
        for half in range(2):
            part = land_ref[start : start + rows, half, :]
            at = slice(half * 128, half * 128 + 128)
            x_ref[at, start : start + rows] = part.T
            wide_ref[HALO + start : HALO + start + rows, at] = part.astype(bf16)

    land(0, HALO)
    land(PATCH - HALO, HALO)
    halos = [
        remote(
            wide_ref.at[HALO : 2 * HALO], wide_ref.at[HALO + PATCH : 2 * HALO + PATCH],
            send3_sem.at[0], recv3_sem.at[0], neighbour(127),
        ),
        remote(
            wide_ref.at[PATCH : PATCH + HALO], wide_ref.at[0:HALO],
            send3_sem.at[1], recv3_sem.at[1], neighbour(1),
        ),
    ]
    for copy in halos:
        copy.start()
    for c in range(3):
        land(HALO + c * 256, 256)

    lanes = iota((256, 512), 1)
    for c in (1, 2, 0, 3):
        if c == 0:
            for copy in halos:
                copy.wait()
        window = wide_ref[c * 256 : c * 256 + 512, :]
        places = places_ref[c * 256 : c * 256 + 256, :] - c * 256
        for b in range(OFFS // 3):
            for k in range(3):
                hot_ref[b % 2, k * 256 : k * 256 + 256, :] = one_hot(lanes, places[:, 3 * b + k : 3 * b + k + 1])
            picked = dot(hot_ref[b % 2], window).astype(bf16)
            for k in range(3):
                at = (3 * b + k) * C
                picked_ref[c * 256 : c * 256 + 256, at : at + C] = picked[k * 256 : k * 256 + 256]
    for copy in shares:
        copy.wait()
    summed = dot_rows(picked_ref[...], conv_w_ref[...]).T
    conv = (summed + column(COL_CONV)).astype(bf16)
    cpe = cpe_ref[...].T
    for c in range(4):
        span = slice(c * 256, c * 256 + 256)
        mixture = dot(cpe, conv[:, span]) + column(COL_CPE)
        x_ref[:, span] = x_ref[:, span] + norm_columns(
            mixture, column(COL_GAIN + 2), column(COL_SHIFT + 2)
        )

    copies = []

    def emit(c, value):
        span = slice(c * 256, c * 256 + 256)
        place = pl.ds(pl.multiple_of(member * PATCH + c * 256, 256), 256)
        x_ref[:, span] = value
        for d in (2, 3, 1):
            target = member ^ d
            copy = remote(
                x_ref.at[pl.ds(pl.multiple_of(target * 64, 64), 64), span], out_ref.at[:, place],
                send6_sem.at[c, d], recv6_sem.at[c, d], (group, target),
            )
            copy.start()
            copies.append(copy)
        out_ref[:, place] = x_ref[pl.ds(pl.multiple_of(member * 64, 64), 64), span]

    run_block(1, 3, x_ref, w_ref, 0, cols_ref, scratch, emit, lambda: None, ((0, 768), (768, 256)))
    for copy in copies:
        copy.wait()


def second_block(*operands):
    pairs = [pltpu.SemaphoreType.DMA((ORDERS,))] * 2 + [pltpu.SemaphoreType.DMA((4,))] * 2
    pairs += [pltpu.SemaphoreType.DMA((2,))] * 2 + [pltpu.SemaphoreType.DMA((4,))] * 4
    pairs += [pltpu.SemaphoreType.DMA((4, 4))] * 2
    return pl.pallas_call(
        second_kernel,
        out_shape=S((64, TOK), f32),
        in_specs=[VMEM, SMEM, SMEM, SMEM, SMEM, ANY, ANY, VMEM, ANY, VMEM],
        out_specs=VMEM,
        scratch_shapes=[
            pltpu.VMEM((3, CAP_OUT, 2, 128), f32),
            pltpu.VMEM((4 * CAP_OUT, 2, 128), f32),
            pltpu.VMEM((ORDERS, SLOTS, 2, 128), f32),
            pltpu.VMEM((ORDERS * SLOTS, 2, 128), f32),
            pltpu.VMEM((3, CAP, 2, 128), f32),
            pltpu.VMEM((4 * CAP, 2, 128), f32),
            pltpu.VMEM((PATCH, 2, 128), f32),
            pltpu.VMEM((PATCH + 2 * HALO, C), bf16),
            pltpu.VMEM((C, PATCH), f32),
            pltpu.VMEM((OFFS, PATCH), i32),
            pltpu.VMEM((PATCH, 128), i32),
            pltpu.VMEM((2, 3 * 256, 512), bf16),
            pltpu.VMEM((PATCH, OFFS * C), bf16),
            pltpu.VMEM((C, OFFS * C), bf16),
            pltpu.VMEM((4, 768, C), bf16),
            pltpu.SemaphoreType.DMA,
            pltpu.SemaphoreType.DMA((4,)),
        ]
        + pairs
        + block_scratch(),
        compiler_params=kernel_params(collective_id=2, has_side_effects=True),
        name="second_block",
    )(*operands)


def shards(
    feats, serial_rank, neighbours, norm_gain, norm_bias, qkv_weight, qkv_bias, proj_weight, proj_bias,
    fc1_weight, fc1_bias, fc2_weight, fc2_bias, conv_weight, conv_bias, cpe_weight, cpe_bias,
):
    records, cols, send, listed, landing, leave, conv, later = first_block(
        feats, qkv_weight.transpose(0, 1, 3, 2), proj_weight, fc1_weight, fc2_weight, norm_gain, norm_bias,
        qkv_bias.transpose(1, 0, 2), proj_bias, fc1_bias, fc2_bias, conv_bias.reshape(1, 64),
        cpe_bias.reshape(2, 128), conv_weight.transpose(0, 2, 1),
        serial_rank.reshape(32, 128),
    )
    return second_block(
        records, leave.reshape(-1), send.reshape(-1), listed.reshape(-1), landing.reshape(-1), neighbours, conv,
        cpe_weight, later, cols,
    )


def solution(mesh):
    in_specs = (
        P(None, "order"),
        P("order"),
        P(None, "order"),
        P(),
        P(),
        P(None, None, None, "mp"),
        P(None, None, "mp"),
        P(None, "mp", None),
        P(),
        P(None, None, "mp"),
        P(None, "mp"),
        P(None, "mp", None),
        P(),
        P(None, None, "mp"),
        P("mp"),
        P(),
        P(),
    )
    return jax.shard_map(shards, mesh=mesh, in_specs=in_specs, out_specs=P("mp", "order"), check_vma=False)
```
